256 devices in a mesh: row: 16 (over z, y_hi), col: 8 (over x, core), dp: 2 (over y_lo).
Axes of the slice: x: 4, y: 4 (y_hi: 2, y_lo: 2; y = y_hi * 2 + y_lo), z: 8, core: 2. Of those that a mesh axis runs over, the one named last changes fastest.
Arguments:
- tokens: bfloat16 [512, 8192], P(('col', 'dp'), 'row'), may hold values from -6 to 6
- cotangent: bfloat16 [512, 8192], P(('col', 'dp'), 'row'), may hold values from -6 to 6
- gate_blocks: bfloat16 [16, 8, 32, 128, 128], P('row', 'col'), may hold values from -0.125 to 0.125
- up_blocks: bfloat16 [16, 8, 32, 128, 128], P('row', 'col'), may hold values from -0.125 to 0.125
- down_blocks: bfloat16 [8, 16, 32, 128, 128], P('col', 'row'), may hold values from -0.09375 to 0.09375
- gate_slots: int32 [16, 8, 32], P('row', 'col'), may hold values from -1 to 63, as said below
- up_slots: int32 [16, 8, 32], P('row', 'col'), may hold values from -1 to 63, as said below
- down_slots: int32 [8, 16, 32], P('col', 'row'), may hold values from -1 to 63, as said below
Outputs:
- layer_out: bfloat16 [512, 8192], P(('col', 'dp'), 'row')
- token_grad: bfloat16 [512, 8192], P(('col', 'dp'), 'row')
- gate_grad: float32 [16, 8, 32, 128, 128], P('row', 'col', None, 'dp')
- up_grad: float32 [16, 8, 32, 128, 128], P('row', 'col', None, 'dp')
- down_grad: float32 [8, 16, 32, 128, 128], P('col', 'row', None, 'dp')
The draws below stay inside these ranges and needn't reach their ends.
Inputs may be any that keep to these rules, and one draw needn't show every extreme that they name: `gate_slots`: every entry is -1 or a position within one device's tile of 4 x 16 blocks (block row times 16 plus block column); on each device the positions are distinct and come before the -1 entries; some device has all 32 slots filled. `up_slots`: as for gate_slots, drawn independently. `down_slots`: every entry is -1 or a position within one device's tile of 16 x 4 blocks (block row times 4 plus block column); on each device the positions are distinct and come before the -1 entries; some device has all 32 slots filled.
All inputs are finite; a program needn't handle non-finite values.
Results may differ from the reference program's by a relative error of at most 0.035.
Values may be sent and summed in bfloat16 or wider, within the bound.
A program may use at most 64 MiB of HBM per device.

```python
import jax
import jax.numpy as jnp
from jax import lax

D = 8192
FF = 16384
BLK = 128
TOKENS = 512
DRB = 4
FCB = 16
CAP = 32
N_ROW = 16
N_COL = 8


def slot_lists(key, outer_first, outer_second):
    places = DRB * FCB
    tile_count = outer_first * outer_second
    key_counts, key_fullest, key_order = jax.random.split(key, 3)
    counts = jax.random.randint(key_counts, (tile_count,), places // 8, 3 * places // 8 + 1)
    fullest = jax.random.randint(key_fullest, (), 0, tile_count)
    counts = jnp.where(jnp.arange(tile_count) == fullest, CAP, counts)
    orders = jax.vmap(lambda subkey: jax.random.permutation(subkey, places))(jax.random.split(key_order, tile_count))
    chosen = orders[:, :CAP].astype(jnp.int32)
    keep_mask = jnp.arange(CAP)[None, :] < counts[:, None]
    return jnp.where(keep_mask, chosen, -1).astype(jnp.int32).reshape(outer_first, outer_second, CAP)


def draw_gate_slots(key, part):
    key = jax.random.fold_in(key, 5)
    return slot_lists(key, N_ROW, N_COL)


def draw_up_slots(key, part):
    key = jax.random.fold_in(key, 6)
    return slot_lists(key, N_ROW, N_COL)


def draw_down_slots(key, part):
    key = jax.random.fold_in(key, 7)
    return slot_lists(key, N_COL, N_ROW)


def with_spikes(result, stream_key, source, target, blocks, factor):
    def block_of(dim):
        return (jnp.arange(result.shape[dim]) // (result.shape[dim] // blocks)).reshape((-1,) + (1,) * (result.ndim - 1 - dim))

    first = jax.random.permutation(stream_key, blocks)[block_of(target)]
    far = (block_of(target) + blocks // 2) % blocks
    return jnp.where((block_of(source) == first) | (block_of(source) == far), factor * result, result)


def steps_of(stream_key, dims, cuts, low, top_value):
    gain = 1.0
    for axis_at, shards_of in cuts:
        heights = jax.random.uniform(jax.random.fold_in(jax.random.fold_in(stream_key, 6), axis_at), (shards_of,), jnp.float32, low / len(cuts), top_value / len(cuts))
        gain = gain * jnp.repeat(jnp.exp(heights), dims[axis_at] // shards_of).reshape((-1,) + (1,) * (len(dims) - 1 - axis_at))
    return gain


def normal_values(key, extent, scale, bound, cuts=(), held_as=jnp.bfloat16):
    gain = steps_of(key, extent, cuts, -0.22, 0.18) if cuts else 1.0
    entries = jax.random.normal(key, extent, jnp.float32) * scale * gain
    return jnp.minimum(jnp.maximum(entries, -bound), bound).astype(held_as)


def noise_with(stream_key, dims, scale, reach, cuts, heavy, kind=jnp.bfloat16):
    values = scale * jax.random.normal(stream_key, dims, jnp.float32)
    if cuts:
        values = values * steps_of(stream_key, dims, cuts, -0.22, 0.18)
    return jnp.clip(with_spikes(values, jax.random.fold_in(stream_key, 3), *heavy), -reach, reach).astype(kind)


def setup_inputs(seed: int = 0) -> dict:
    key_list = jax.random.split(jax.random.key(seed), 9)
    return {
        "tokens": noise_with(key_list[0], (TOKENS, D), 1.0, 6.0, ((0, 16), (1, 16)), (1, 0, 16, 2.0)),
        "cotangent": normal_values(key_list[1], (TOKENS, D), 1.0, 6.0, ((0, 16), (1, 16))),
        "gate_blocks": normal_values(key_list[2], (N_ROW, N_COL, CAP, BLK, BLK), (D // 4) ** -0.5, 0.125, ((0, 16), (1, 8))),
        "up_blocks": normal_values(key_list[3], (N_ROW, N_COL, CAP, BLK, BLK), (D // 4) ** -0.5, 0.125, ((0, 16), (1, 8))),
        "down_blocks": normal_values(key_list[4], (N_COL, N_ROW, CAP, BLK, BLK), (FF // 4) ** -0.5, 0.09375, ((0, 8), (1, 16))),
        "gate_slots": draw_gate_slots(jax.random.fold_in(key_list[8], 71), 0),
        "up_slots": draw_up_slots(jax.random.fold_in(key_list[8], 71), 0),
        "down_slots": draw_down_slots(jax.random.fold_in(key_list[8], 71), 0),
    }


def block_indices(slot_list, count_first, count_second):
    live_mask = slot_list >= 0
    position = jnp.where(live_mask, slot_list, 0).astype(jnp.int32)
    outer_first = slot_list.shape[0]
    outer_second = slot_list.shape[1]
    first_index = jnp.arange(outer_first, dtype=jnp.int32)[:, None, None] * count_first + position // count_second
    second_index = jnp.arange(outer_second, dtype=jnp.int32)[None, :, None] * count_second + position % count_second
    return live_mask, first_index, second_index


def dense_from(blocks, slot_list, count_first, count_second):
    live_mask, first_index, second_index = block_indices(slot_list, count_first, count_second)
    total_first = slot_list.shape[0] * count_first
    total_second = slot_list.shape[1] * count_second
    flat_index = (first_index * total_second + second_index).reshape(-1)
    values = jnp.where(live_mask[..., None, None], blocks, jnp.zeros_like(blocks)).reshape(-1, BLK, BLK)
    grid = jnp.zeros((total_first * total_second, BLK, BLK), blocks.dtype).at[flat_index].add(values)
    grid = grid.reshape(total_first, total_second, BLK, BLK).transpose(0, 2, 1, 3)
    return grid.reshape(total_first * BLK, total_second * BLK)


def take_blocks(dense, slot_list, count_first, count_second):
    live_mask, first_index, second_index = block_indices(slot_list, count_first, count_second)
    total_first = slot_list.shape[0] * count_first
    total_second = slot_list.shape[1] * count_second
    tiled = dense.reshape(total_first, BLK, total_second, BLK).transpose(0, 2, 1, 3)
    picked = tiled[first_index, second_index]
    return jnp.where(live_mask[..., None, None], picked, jnp.zeros_like(picked))


def parts_sum(lefts, rights, parts):
    token_count = lefts[0].shape[0]
    width = lefts[0].shape[1] // parts
    left_parts = tuple(left.reshape(token_count, parts, width).transpose(1, 0, 2) for left in lefts)
    right_parts = tuple(right.reshape(parts, width, right.shape[1]) for right in rights)

    def add_part(running, portion):
        term = jnp.zeros((token_count, rights[0].shape[1]), jnp.float32)
        for index in range(len(lefts)):
            term = term + jnp.dot(portion[0][index], portion[1][index], preferred_element_type=jnp.float32)
        rounded = lax.optimization_barrier(term.astype(jnp.bfloat16))
        return running + rounded.astype(jnp.float32), None

    start_value = jnp.zeros((token_count, rights[0].shape[1]), jnp.float32)
    return lax.scan(add_part, start_value, (left_parts, right_parts))[0]


def reference(tokens, cotangent, gate_blocks, up_blocks, down_blocks, gate_slots, up_slots, down_slots):
    gate_matrix = dense_from(gate_blocks, gate_slots, DRB, FCB)
    up_matrix = dense_from(up_blocks, up_slots, DRB, FCB)
    down_matrix = dense_from(down_blocks, down_slots, FCB, DRB)
    gate_sum = parts_sum((tokens,), (gate_matrix,), N_ROW)
    up_sum = parts_sum((tokens,), (up_matrix,), N_ROW)
    hidden = (jax.nn.silu(gate_sum) * up_sum).astype(jnp.bfloat16)
    layer_out = parts_sum((hidden,), (down_matrix,), N_COL).astype(jnp.bfloat16)
    grad_hidden = parts_sum((cotangent,), (down_matrix.T,), N_ROW)
    sigma = jax.nn.sigmoid(gate_sum)
    grad_gate = (grad_hidden * up_sum * sigma * (1.0 + gate_sum * (1.0 - sigma))).astype(jnp.bfloat16)
    grad_up = (grad_hidden * gate_sum * sigma).astype(jnp.bfloat16)
    token_grad = parts_sum((grad_gate, grad_up), (gate_matrix.T, up_matrix.T), N_COL).astype(jnp.bfloat16)
    gate_dense = jnp.dot(tokens.T, grad_gate, preferred_element_type=jnp.float32)
    gate_grad = take_blocks(gate_dense, gate_slots, DRB, FCB)
    up_dense = jnp.dot(tokens.T, grad_up, preferred_element_type=jnp.float32)
    up_grad = take_blocks(up_dense, up_slots, DRB, FCB)
    down_dense = jnp.dot(hidden.T, cotangent, preferred_element_type=jnp.float32)
    down_grad = take_blocks(down_dense, down_slots, FCB, DRB)
    return (layer_out, token_grad, gate_grad, up_grad, down_grad)
```

```python
import functools

import jax
import jax.numpy as jnp
from jax import lax
from jax.experimental import pallas as pl
from jax.experimental.pallas import tpu as pltpu
from jax.sharding import PartitionSpec as P

FF = 16384
BLK = 128
UNITS = 2
MESH = pl.DeviceIdType.MESH
F32 = jnp.float32
BF16 = jnp.bfloat16


def dot(a, b):
    return lax.dot_general(a, b, (((1,), (0,)), ((), ())), preferred_element_type=F32)


def dot_t(a, b):
    return lax.dot_general(a, b, (((1,), (1,)), ((), ())), preferred_element_type=F32)


def al(value, step):
    return pl.multiple_of(value, step)


def kernel(
    dims,
    slots_ref,
    inv_ref,
    tok_in,
    cot_in,
    gate_in,
    up_in,
    down_in,
    layer_out,
    tgrad_out,
    gate_out,
    up_out,
    down_out,
    blocks,
    tcg,
    wg,
    wu,
    wd,
    part,
    rs_send,
    rs_recv,
    y_send,
    y_recv,
    y_own,
    act,
    tok_t,
    hid_t,
    dense,
    dp_send,
    dp_recv,
    dp_own,
    col_part,
    ca_send,
    ca_recv,
    cb_send,
    cb_recv,
    col_stage,
    loc_sem,
    out_sem,
    p1_s,
    p1_r,
    rs_s,
    rs_r,
    ys_s,
    ys_r,
    ya_s,
    ya_r,
    ag_s,
    ag_r,
    dp_s,
    dp_r,
    ca_s,
    ca_r,
    cb_s,
    cb_r,
):
    n_row, n_col, n_tok, width, hid, cap = dims
    nz, nx = n_row // 2, n_col // 2
    steps = nz // 2
    group = n_tok * n_col
    zrows = group // nz
    own_rows = zrows // 2
    cw = hid // UNITS
    half = cw // 2
    drb, fcb = width // BLK, hid // BLK

    row, col, dp = lax.axis_index("row"), lax.axis_index("col"), lax.axis_index("dp")
    z, yh = lax.div(row, 2), lax.rem(row, 2)
    x, core = lax.div(col, 2), lax.rem(col, 2)
    z_right = (lax.rem(z + 1, nz) * 2 + yh, col, dp)
    z_left = (lax.rem(z + nz - 1, nz) * 2 + yh, col, dp)
    z_dev = (z_right, z_left)
    y_dev = (z * 2 + 1 - yh, col, dp)
    sib = (row, x * 2 + 1 - core, dp)
    dp_dev = (row, col, 1 - dp)

    def x_dev(k):
        return (row, lax.rem(x + k, nx) * 2 + core, dp)

    sends = []

    def send(src, dst, s_sem, r_sem, dev):
        copy = pltpu.make_async_remote_copy(
            src_ref=src, dst_ref=dst, send_sem=s_sem, recv_sem=r_sem, device_id=dev, device_id_type=MESH
        )
        copy.start()
        sends.append(copy)

    def arrived(dst, s_sem, r_sem, dev):
        pltpu.make_async_remote_copy(
            src_ref=dst, dst_ref=dst, send_sem=s_sem, recv_sem=r_sem, device_id=dev, device_id_type=MESH
        ).wait_recv()

    def tok_rows(c):
        return tcg.at[:, pl.ds(al(c * n_tok, n_tok), n_tok), :]

    mine = pl.ds(al(col * n_tok, n_tok), n_tok)
    own_loads = [
        pltpu.make_async_copy(tok_in, tcg.at[0, mine, :], loc_sem.at[0]),
        pltpu.make_async_copy(cot_in, tcg.at[1, mine, :], loc_sem.at[1]),
    ]
    block_loads = [
        pltpu.make_async_copy(ref, blocks.at[i, pl.ds(0, cap)], loc_sem.at[2 + i])
        for i, ref in enumerate((gate_in, up_in, down_in))
    ]
    for c in own_loads + block_loads:
        c.start()

    barrier = pltpu.get_barrier_semaphore()
    peers = [z_right, z_left, y_dev, sib, dp_dev] + [x_dev(k) for k in range(1, nx)]
    for dev in peers:
        pl.semaphore_signal(barrier, inc=1, device_id=dev, device_id_type=MESH)
    pl.semaphore_wait(barrier, len(peers))

    for c in own_loads:
        c.wait()
    send(tok_rows(col), tok_rows(col), p1_s.at[0], p1_r.at[0], sib)
    for k in range(1, nx):
        send(tok_rows(col), tok_rows(col), p1_s.at[k], p1_r.at[k], x_dev(k))

    for c in block_loads:
        c.wait()
    for i in range(3):
        blocks[i, cap] = jnp.zeros((BLK, BLK), BF16)
    dense[drb * fcb] = jnp.zeros((BLK, BLK), F32)

    def place(p, carry):
        r0, c0 = al((p // fcb) * BLK, BLK), al((p % fcb) * BLK, BLK)
        wg[pl.ds(r0, BLK), pl.ds(c0, BLK)] = blocks[0, inv_ref[0, p]]
        wu[pl.ds(r0, BLK), pl.ds(c0, BLK)] = blocks[1, inv_ref[1, p]]
        r1, c1 = al((p // drb) * BLK, BLK), al((p % drb) * BLK, BLK)
        wd[pl.ds(r1, BLK), pl.ds(c1, BLK)] = blocks[2, inv_ref[2, p]]
        return carry

    lax.fori_loop(0, drb * fcb, place, 0)

    for k in range(1, nx):
        src = lax.rem(x + nx - k, nx) * 2 + core
        arrived(tok_rows(src), p1_s.at[k], p1_r.at[k], sib)
        send(tok_rows(src), tok_rows(src), p1_s.at[nx + k - 1], p1_r.at[nx + k - 1], sib)
    arrived(tok_rows(x * 2 + 1 - core), p1_s.at[0], p1_r.at[0], sib)
    for k in range(1, nx):
        src = lax.rem(x + nx - k, nx) * 2 + 1 - core
        arrived(tok_rows(src), p1_s.at[nx + k - 1], p1_r.at[nx + k - 1], sib)

    def z_rows(t):
        return al(lax.rem(t + 2 * nz, nz) * zrows, zrows)

    def rs_cols(d, k):
        if k == 0:
            return pl.ds(d * half, half)
        return pl.ds(0, cw)

    def rs_start(u, d, k):
        target = z + (steps - k) * (1 - 2 * d)
        r0 = z_rows(target)
        for t in range(3):
            for h in range(2):
                if k == 0 and h != d:
                    continue
                value = part[t, pl.ds(r0, zrows), pl.ds(u * cw + h * half, half)]
                if k > 1 or (k == 1 and h == d):
                    value = value + rs_recv[u, d, k - 1, t, :, pl.ds(h * half, half)].astype(F32)
                rs_send[u, d, k, t, :, pl.ds(h * half, half)] = value.astype(BF16)
        c = rs_cols(d, k)
        send(
            rs_send.at[u, d, k, :, :, c],
            rs_recv.at[u, d, k, :, :, c],
            rs_s.at[u, d, k],
            rs_r.at[u, d, k],
            z_dev[d],
        )

    def rs_wait(u, d, k):
        arrived(rs_recv.at[u, d, k, :, :, rs_cols(d, k)], rs_s.at[u, d, k], rs_r.at[u, d, k], z_dev[d])

    tile = min(256, cw)
    for u in range(UNITS):

        def product(j, carry):
            c0 = al(u * cw + j * tile, tile)
            part[0, :, pl.ds(c0, tile)] = dot(tcg[0], wg[:, pl.ds(c0, tile)])
            part[1, :, pl.ds(c0, tile)] = dot(tcg[0], wu[:, pl.ds(c0, tile)])
            part[2, :, pl.ds(c0, tile)] = dot_t(tcg[1], wd[pl.ds(c0, tile), :])
            return carry

        lax.fori_loop(0, cw // tile, product, 0)
        for d in range(2):
            rs_start(u, d, 0)

    tok_t[...] = tcg[0].astype(F32).T.astype(BF16)

    for k in range(1, steps):
        for u in range(UNITS):
            for d in range(2):
                rs_wait(u, d, k - 1)
                rs_start(u, d, k)

    mine_r = al(z * zrows + yh * own_rows, own_rows)
    theirs_r = al(z * zrows + (1 - yh) * own_rows, own_rows)
    mine_o, theirs_o = al(yh * own_rows, own_rows), al((1 - yh) * own_rows, own_rows)
    zchunk = pl.ds(z_rows(z), zrows)

    for u in range(UNITS):
        for d in range(2):
            rs_wait(u, d, steps - 1)
        for t in range(3):

            def total(r0, o0):
                value = part[t, pl.ds(r0, own_rows), pl.ds(u * cw, cw)]
                for d in range(2):
                    value = value + rs_recv[u, d, steps - 1, t, pl.ds(o0, own_rows), :].astype(F32)
                return value

            y_send[u, t] = total(theirs_r, theirs_o).astype(BF16)
            y_own[u, t] = total(mine_r, mine_o)
        send(y_send.at[u], y_recv.at[u], ys_s.at[u], ys_r.at[u], y_dev)

    def act_rows(r0, u):
        return act.at[:, pl.ds(r0, own_rows), pl.ds(u * cw, cw)]

    for u in range(UNITS):
        arrived(y_recv.at[u], ys_s.at[u], ys_r.at[u], y_dev)
        for q in range(2):
            cs = pl.ds(q * half, half)
            gate = y_own[u, 0, :, cs] + y_recv[u, 0, :, cs].astype(F32)
            up = y_own[u, 1, :, cs] + y_recv[u, 1, :, cs].astype(F32)
            grad = y_own[u, 2, :, cs] + y_recv[u, 2, :, cs].astype(F32)
            sg = 1.0 / (1.0 + jnp.exp(-gate))
            co = pl.ds(u * cw + q * half, half)
            act[0, pl.ds(mine_r, own_rows), co] = (gate * sg * up).astype(BF16)
            act[1, pl.ds(mine_r, own_rows), co] = (
                grad * up * sg * (1.0 + gate * (1.0 - sg))
            ).astype(BF16)
            act[2, pl.ds(mine_r, own_rows), co] = (grad * gate * sg).astype(BF16)
        send(act_rows(mine_r, u), act_rows(mine_r, u), ya_s.at[u], ya_r.at[u], y_dev)

    def ag_slice(t, u, d, k, chunk):
        if k == steps - 1:
            c = pl.ds(u * cw + d * half, half)
        else:
            c = pl.ds(u * cw, cw)
        return act.at[t, pl.ds(z_rows(chunk), zrows), c]

    def ag_start(t, u, d, k):
        ref = ag_slice(t, u, d, k, z - k * (1 - 2 * d))
        send(ref, ref, ag_s.at[t, u, d, k], ag_r.at[t, u, d, k], z_dev[d])

    def ag_wait(t, u, d, k):
        ref = ag_slice(t, u, d, k, z - (k + 1) * (1 - 2 * d))
        arrived(ref, ag_s.at[t, u, d, k], ag_r.at[t, u, d, k], z_dev[d])

    def ag_step(t, k):
        for u in range(UNITS):
            if k == 0 and t == 0:
                arrived(act_rows(theirs_r, u), ya_s.at[u], ya_r.at[u], y_dev)
            for d in range(2):
                if k > 0:
                    ag_wait(t, u, d, k - 1)
                if k < steps:
                    ag_start(t, u, d, k)

    hb = BLK // 2

    def emit_blocks(i):
        def body(s, carry):
            value = dense[slots_ref[i, s]]
            low, high = value[:hb], value[hb:]
            dp_own[i, s] = jnp.where(dp == 0, low, high)
            dp_send[i, s] = jnp.where(dp == 0, high, low).astype(BF16)
            return carry

        lax.fori_loop(0, cap, body, 0)
        send(dp_send.at[i], dp_recv.at[i], dp_s.at[i], dp_r.at[i], dp_dev)

    out_copies = []

    def finish_blocks(i, out):
        arrived(dp_recv.at[i], dp_s.at[i], dp_r.at[i], dp_dev)

        def body(s, carry):
            dp_own[i, s] = dp_own[i, s] + dp_recv[i, s].astype(F32)
            return carry

        lax.fori_loop(0, cap, body, 0)
        copy = pltpu.make_async_copy(dp_own.at[i], out, out_sem.at[i])
        copy.start()
        out_copies.append(copy)

    def col_rows(c):
        return pl.ds(al(c * n_tok, n_tok), n_tok)

    def col_first(j):
        for xx in range(nx):
            ca_send[j, xx] = col_part[j, col_rows(xx * 2 + 1 - core), :].astype(BF16)
        send(ca_send.at[j], ca_recv.at[j], ca_s.at[j], ca_r.at[j], sib)

    def pair_sum(j, xx):
        return col_part[j, col_rows(xx * 2 + core), :] + ca_recv[j, xx].astype(F32)

    def col_second(j):
        arrived(ca_recv.at[j], ca_s.at[j], ca_r.at[j], sib)
        for k in range(1, nx):
            cb_send[j, k - 1] = pair_sum(j, lax.rem(x + k, nx)).astype(BF16)
            send(cb_send.at[j, k - 1], cb_recv.at[j, k - 1], cb_s.at[j, k - 1], cb_r.at[j, k - 1], x_dev(k))

    def col_last(j, out):
        value = pair_sum(j, x)
        for k in range(1, nx):
            arrived(cb_recv.at[j, k - 1], cb_s.at[j, k - 1], cb_r.at[j, k - 1], sib)
            value = value + cb_recv[j, k - 1].astype(F32)
        col_stage[j] = value.astype(BF16)
        copy = pltpu.make_async_copy(col_stage.at[j], out, out_sem.at[3 + j])
        copy.start()
        out_copies.append(copy)

    def transpose_hidden():
        def body(j, carry):
            c0 = al(j * BLK, BLK)
            hid_t[pl.ds(c0, BLK), :] = act[0, :, pl.ds(c0, BLK)].astype(F32).T.astype(BF16)
            return carry

        lax.fori_loop(0, fcb, body, 0)

    def down_dense():
        def body(j, carry):
            value = dot(hid_t[pl.ds(al(j * 2 * BLK, BLK), 2 * BLK), :], tcg[1])
            for a in range(2):
                for b in range(drb):
                    dense[(2 * j + a) * drb + b] = value[a * BLK : (a + 1) * BLK, b * BLK : (b + 1) * BLK]
            return carry

        lax.fori_loop(0, fcb // 2, body, 0)

    def wide_dense(t):
        def body(j, carry):
            value = dot(tok_t[...], act[t, :, pl.ds(al(j * 2 * BLK, BLK), 2 * BLK)])
            for a in range(drb):
                for b in range(2):
                    dense[a * fcb + 2 * j + b] = value[a * BLK : (a + 1) * BLK, b * BLK : (b + 1) * BLK]
            return carry

        lax.fori_loop(0, fcb // 2, body, 0)

    def layer_product():
        step = min(256, width)

        def body(j, carry):
            c0 = al(j * step, step)
            col_part[0, :, pl.ds(c0, step)] = dot(act[0], wd[:, pl.ds(c0, step)])
            return carry

        lax.fori_loop(0, width // step, body, 0)

    def grad_product(t, w):
        step = min(256, width)

        def body(j, carry):
            c0 = al(j * step, step)
            value = dot_t(act[t], w[pl.ds(c0, step), :])
            if t == 2:
                value = value + col_part[1, :, pl.ds(c0, step)]
            col_part[1, :, pl.ds(c0, step)] = value
            return carry

        lax.fori_loop(0, width // step, body, 0)

    stages = [[] for _ in range(steps + 5)]
    for t in range(3):
        for k in range(steps):
            stages[2 * t + k].append((t, k))
    for s in range(steps + 4):
        for t, k in stages[s]:
            ag_step(t, k)
        if s == steps:
            ag_step(0, steps)
            transpose_hidden()
            down_dense()
            emit_blocks(2)
            layer_product()
            col_first(0)
        if s == steps + 1:
            col_second(0)
        if s == steps + 2:
            ag_step(1, steps)
            wide_dense(1)
            emit_blocks(0)
            grad_product(1, wg)
        if s == steps + 3:
            col_last(0, layer_out)
    ag_step(2, steps)
    grad_product(2, wu)
    col_first(1)
    wide_dense(2)
    emit_blocks(1)
    col_second(1)
    finish_blocks(2, down_out)
    finish_blocks(0, gate_out)
    col_last(1, tgrad_out)
    finish_blocks(1, up_out)
    for c in out_copies:
        c.wait()
    for c in sends:
        c.wait_send()


def per_device(tokens, cotangent, gate_blocks, up_blocks, down_blocks, gate_slots, up_slots, down_slots):
    n_row, n_col = lax.axis_size("row"), lax.axis_size("col")
    n_tok, width = tokens.shape
    cap = gate_blocks.shape[2]
    hid = FF // n_col
    nz, nx = n_row // 2, n_col // 2
    steps = nz // 2
    group = n_tok * n_col
    zrows = group // nz
    own_rows = zrows // 2
    cw = hid // UNITS
    drb, fcb = width // BLK, hid // BLK
    hb = BLK // 2
    slots = jnp.concatenate([gate_slots[0], up_slots[0], down_slots[0]], axis=0)
    place = jnp.arange(drb * fcb, dtype=jnp.int32)
    order = jnp.arange(cap, dtype=jnp.int32)
    inv = jnp.min(
        jnp.where(slots[:, None, :] == place[None, :, None], order[None, None, :], cap), axis=2
    )
    slots = jnp.where(slots < 0, drb * fcb, slots)
    dims = (n_row, n_col, n_tok, width, hid, cap)
    smem = pl.BlockSpec(memory_space=pltpu.SMEM)
    anym = pl.BlockSpec(memory_space=pl.ANY)
    vm = pltpu.VMEM
    dma = pltpu.SemaphoreType.DMA
    scratch = [
        vm((3, cap + 1, BLK, BLK), BF16),
        vm((2, group, width), BF16),
        vm((width, hid), BF16),
        vm((width, hid), BF16),
        vm((hid, width), BF16),
        vm((3, group, hid), F32),
        vm((UNITS, 2, steps, 3, zrows, cw), BF16),
        vm((UNITS, 2, steps, 3, zrows, cw), BF16),
        vm((UNITS, 3, own_rows, cw), BF16),
        vm((UNITS, 3, own_rows, cw), BF16),
        vm((UNITS, 3, own_rows, cw), F32),
        vm((3, group, hid), BF16),
        vm((width, group), BF16),
        vm((hid, group), BF16),
        vm((drb * fcb + 1, BLK, BLK), F32),
        vm((3, cap, hb, BLK), BF16),
        vm((3, cap, hb, BLK), BF16),
        vm((3, cap, hb, BLK), F32),
        vm((2, group, width), F32),
        vm((2, nx, n_tok, width), BF16),
        vm((2, nx, n_tok, width), BF16),
        vm((2, nx - 1, n_tok, width), BF16),
        vm((2, nx - 1, n_tok, width), BF16),
        vm((2, n_tok, width), BF16),
        dma((5,)),
        dma((5,)),
        dma((2 * nx - 1,)),
        dma((2 * nx - 1,)),
        dma((UNITS, 2, steps)),
        dma((UNITS, 2, steps)),
        dma((UNITS,)),
        dma((UNITS,)),
        dma((UNITS,)),
        dma((UNITS,)),
        dma((3, UNITS, 2, steps)),
        dma((3, UNITS, 2, steps)),
        dma((3,)),
        dma((3,)),
        dma((2,)),
        dma((2,)),
        dma((2, nx - 1)),
        dma((2, nx - 1)),
    ]
    flops = 9 * 2 * group * width * hid
    layer, tgrad, gate_grad, up_grad, down_grad = pl.pallas_call(
        functools.partial(kernel, dims),
        out_shape=(
            jax.ShapeDtypeStruct((n_tok, width), BF16),
            jax.ShapeDtypeStruct((n_tok, width), BF16),
            jax.ShapeDtypeStruct((cap, hb, BLK), F32),
            jax.ShapeDtypeStruct((cap, hb, BLK), F32),
            jax.ShapeDtypeStruct((cap, hb, BLK), F32),
        ),
        in_specs=[smem, smem, anym, anym, anym, anym, anym],
        out_specs=(anym, anym, anym, anym, anym),
        scratch_shapes=scratch,
        compiler_params=pltpu.CompilerParams(
            collective_id=0, has_side_effects=True, vmem_limit_bytes=56 * 1024 * 1024
        ),
        cost_estimate=pl.CostEstimate(flops=flops, bytes_accessed=8 * 1024 * 1024, transcendentals=0),
        name="ffn",
    )(slots, inv, tokens, cotangent, gate_blocks[0, 0], up_blocks[0, 0], down_blocks[0, 0])
    return (layer, tgrad, gate_grad[None, None], up_grad[None, None], down_grad[None, None])


def solution(mesh):
    in_specs = (
        P(("col", "dp"), "row"),
        P(("col", "dp"), "row"),
        P("row", "col", None, None, None),
        P("row", "col", None, None, None),
        P("col", "row", None, None, None),
        P("row", "col", None),
        P("row", "col", None),
        P("col", "row", None),
    )
    out_specs = (
        P(("col", "dp"), "row"),
        P(("col", "dp"), "row"),
        P("row", "col", None, "dp", None),
        P("row", "col", None, "dp", None),
        P("col", "row", None, "dp", None),
    )
    return jax.shard_map(
        per_device, mesh=mesh, in_specs=in_specs, out_specs=out_specs, check_vma=False
    )
```

```python
import functools

import jax
import jax.numpy as jnp
from jax import lax
from jax.experimental import pallas as pl
from jax.experimental.pallas import tpu as pltpu
from jax.sharding import PartitionSpec as P

FF = 16384
BLK = 128
HB = BLK // 2
UNITS = 2
GRID = 4
MESH = pl.DeviceIdType.MESH
F32 = jnp.float32
BF16 = jnp.bfloat16


def dot(a, b):
    return lax.dot_general(a, b, (((1,), (0,)), ((), ())), preferred_element_type=F32)


def dot_t(a, b):
    return lax.dot_general(a, b, (((1,), (1,)), ((), ())), preferred_element_type=F32)


def al(value, step):
    return pl.multiple_of(value, step)


def swap(value):
    return pltpu.roll(value, HB, 1)


def lane_half(rows):
    return (lax.broadcasted_iota(jnp.int32, (rows, BLK), 1) >= HB).astype(jnp.int32)


def kernel(
    dims,
    slots_ref,
    inv_ref,
    tok_in,
    cot_in,
    gate_in,
    up_in,
    down_in,
    layer_out,
    tgrad_out,
    own_out,
    recv_out,
    down_out,
    blocks,
    tcg,
    wg,
    wu,
    wd,
    part,
    rs_send,
    rs_recv,
    y_send,
    y_recv,
    y_own,
    act,
    tok_t,
    hid_t,
    dense,
    dp_send,
    dp_own,
    down_own,
    col_part,
    ca_send,
    ca_recv,
    cb_send,
    cb_recv,
    cc_sum,
    cc_send,
    cc_recv,
    col_stage,
    loc_sem,
    out_sem,
    p1_s,
    p1_r,
    rs_s,
    rs_r,
    ys_s,
    ys_r,
    ya_s,
    ya_r,
    ag_s,
    ag_r,
    dp_s,
    dp_r,
    ca_s,
    ca_r,
    cb_s,
    cb_r,
    cc_s,
    cc_r,
):
    n_row, n_col, n_tok, width, hid, cap = dims
    nz, nx = n_row // 2, n_col // 2
    steps = nz // 2
    group = 2 * n_tok * n_col
    zrows = group // nz
    own_rows = zrows // 2
    cw = hid // UNITS
    half = cw // 2
    drb, fcb = width // BLK, hid // HB
    pair = 2 * n_tok

    row, col, dp = lax.axis_index("row"), lax.axis_index("col"), lax.axis_index("dp")
    z, yh = lax.div(row, 2), lax.rem(row, 2)
    x, core = lax.div(col, 2), lax.rem(col, 2)
    z_right = (lax.rem(z + 1, nz) * 2 + yh, col, dp)
    z_left = (lax.rem(z + nz - 1, nz) * 2 + yh, col, dp)
    z_dev = (z_right, z_left)
    y_dev = (z * 2 + 1 - yh, col, dp)
    sib = (row, x * 2 + 1 - core, dp)
    dp_dev = (row, col, 1 - dp)

    def x_dev(k):
        return (row, lax.rem(x + k, nx) * 2 + core, dp)

    sends = []

    def send(src, dst, s_sem, r_sem, dev):
        copy = pltpu.make_async_remote_copy(
            src_ref=src, dst_ref=dst, send_sem=s_sem, recv_sem=r_sem, device_id=dev, device_id_type=MESH
        )
        copy.start()
        sends.append(copy)

    def arrived(dst, s_sem, r_sem, dev):
        pltpu.make_async_remote_copy(
            src_ref=dst, dst_ref=dst, send_sem=s_sem, recv_sem=r_sem, device_id=dev, device_id_type=MESH
        ).wait_recv()

    mine = pl.ds(al((col * 2 + dp) * n_tok, n_tok), n_tok)
    own_loads = [
        pltpu.make_async_copy(ref, tcg.at[j, mine, :], loc_sem.at[j])
        for j, ref in enumerate((tok_in, cot_in))
    ]
    block_loads = [
        pltpu.make_async_copy(ref, blocks.at[i, pl.ds(0, cap)], loc_sem.at[2 + i])
        for i, ref in enumerate((gate_in, up_in, down_in))
    ]
    for c in own_loads + block_loads:
        c.start()

    barrier = pltpu.get_barrier_semaphore()
    peers = [z_right, z_left, y_dev, sib, dp_dev] + [x_dev(k) for k in range(1, nx)]
    for dev in peers:
        pl.semaphore_signal(barrier, inc=1, device_id=dev, device_id_type=MESH)
    pl.semaphore_wait(barrier, len(peers))

    def piece(j, xk, c, d):
        index = (lax.rem(x + nx - xk, nx) * 2 + c) * 2 + d
        return tcg.at[j, pl.ds(al(index * n_tok, n_tok), n_tok), :]

    def give(j, ref, s, dev):
        send(ref, ref, p1_s.at[j, s], p1_r.at[j, s], dev)

    def take(j, ref, s, dev):
        arrived(ref, p1_s.at[j, s], p1_r.at[j, s], dev)

    def gather_start(j):
        own_loads[j].wait()
        own = piece(j, 0, core, dp)
        for k in range(1, nx):
            give(j, own, k, x_dev(k))
        give(j, own, nx, dp_dev)
        give(j, own, 0, sib)

    def gather_x(j):
        for k in range(1, nx):
            ref = piece(j, k, core, dp)
            take(j, ref, k, sib)
            give(j, ref, nx + k, dp_dev)
            give(j, ref, 2 * nx + k - 1, sib)

    def gather_dp(j):
        for k in range(nx):
            ref = piece(j, k, core, 1 - dp)
            take(j, ref, nx + k, dp_dev)
            give(j, ref, 3 * nx - 1 + k, sib)

    def gather_sib(j):
        take(j, piece(j, 0, 1 - core, dp), 0, sib)
        for k in range(1, nx):
            take(j, piece(j, k, 1 - core, dp), 2 * nx + k - 1, sib)
        for k in range(nx):
            take(j, piece(j, k, 1 - core, 1 - dp), 3 * nx - 1 + k, sib)

    gather_start(0)
    gather_start(1)

    for c in block_loads:
        c.wait()
    for i in range(3):
        blocks[i, cap] = jnp.zeros((BLK, BLK), BF16)
    dense[drb * fcb] = jnp.zeros((BLK, BLK), F32)

    def place_wide(p, carry):
        r, c = p // (fcb // 2), p % (fcb // 2)
        keep = lane_half(BLK) == dp
        for i, w in enumerate((wg, wu)):
            even = blocks[i, inv_ref[i, 2 * p]].astype(F32)
            odd = blocks[i, inv_ref[i, 2 * p + 1]].astype(F32)
            stay = jnp.where(dp == 0, even, odd)
            move = swap(jnp.where(dp == 0, odd, even))
            w[pl.ds(al(r * BLK, BLK), BLK), pl.ds(al(c * BLK, BLK), BLK)] = jnp.where(
                keep, stay, move
            ).astype(BF16)
        return carry

    def place_down(p, carry):
        value = blocks[2, inv_ref[2, p]]
        r, c = p // drb, p % drb
        wd[pl.ds(al(r * HB, HB), HB), pl.ds(al(c * BLK, BLK), BLK)] = jnp.where(
            dp == 0, value[:HB], value[HB:]
        )
        return carry

    lax.fori_loop(0, drb * fcb // 2, place_wide, 0)
    gather_x(0)
    lax.fori_loop(0, drb * fcb, place_down, 0)
    gather_dp(0)
    gather_x(1)
    gather_sib(0)

    def z_rows(t):
        return al(lax.rem(t + 2 * nz, nz) * zrows, zrows)

    def rs_ref(buf, t, u, d, k):
        if k == 0:
            return buf.at[t, u, d, k, :, pl.ds(d * half, half)]
        return buf.at[t, u, d, k]

    def rs_start(t, u, d, k):
        target = z + (steps - k) * (1 - 2 * d)
        r0 = z_rows(target)
        for h in range(2):
            if k == 0 and h != d:
                continue
            hc = pl.ds(h * half, half)
            value = part[t, pl.ds(r0, zrows), pl.ds(u * cw + h * half, half)]
            if k > 1 or (k == 1 and h == d):
                value = value + rs_recv[t, u, d, k - 1, :, hc].astype(F32)
            rs_send[t, u, d, k, :, hc] = value.astype(BF16)
        send(
            rs_ref(rs_send, t, u, d, k),
            rs_ref(rs_recv, t, u, d, k),
            rs_s.at[t, u, d, k],
            rs_r.at[t, u, d, k],
            z_dev[d],
        )

    def rs_wait(t, u, d, k):
        arrived(rs_ref(rs_recv, t, u, d, k), rs_s.at[t, u, d, k], rs_r.at[t, u, d, k], z_dev[d])

    def rs_step(u, k):
        for t in range(3):
            for d in range(2):
                rs_wait(t, u, d, k - 1)
                rs_start(t, u, d, k)

    tile = min(256, cw)

    def product(t, u):
        def body(j, carry):
            cs = pl.ds(al(u * cw + j * tile, tile), tile)
            if t == 2:
                part[t, :, cs] = dot_t(tcg[1], wd[cs, :])
            else:
                part[t, :, cs] = dot(tcg[0], (wg, wu)[t][:, cs])
            return carry

        lax.fori_loop(0, cw // tile, body, 0)

    for t in range(2):
        product(t, 0)
        for d in range(2):
            rs_start(t, 0, d, 0)
    gather_dp(1)
    for t in range(2):
        product(t, 1)
    gather_sib(1)
    product(2, 0)
    for d in range(2):
        rs_start(2, 0, d, 0)

    mine_r = al(z * zrows + yh * own_rows, own_rows)
    theirs_r = al(z * zrows + (1 - yh) * own_rows, own_rows)
    mine_o, theirs_o = al(yh * own_rows, own_rows), al((1 - yh) * own_rows, own_rows)

    def rs_finish(u):
        for t in range(3):
            for d in range(2):
                rs_wait(t, u, d, steps - 1)

            def total(r0, o0):
                value = part[t, pl.ds(r0, own_rows), pl.ds(u * cw, cw)]
                for d in range(2):
                    value = value + rs_recv[t, u, d, steps - 1, pl.ds(o0, own_rows), :].astype(F32)
                return value

            y_send[u, t] = total(theirs_r, theirs_o).astype(BF16)
            y_own[u, t] = total(mine_r, mine_o)
        send(y_send.at[u], y_recv.at[u], ys_s.at[u], ys_r.at[u], y_dev)

    def act_rows(r0, u):
        return act.at[:, pl.ds(r0, own_rows), pl.ds(u * cw, cw)]

    def activate(u):
        arrived(y_recv.at[u], ys_s.at[u], ys_r.at[u], y_dev)
        for q in range(2):
            cs = pl.ds(q * half, half)
            gate = y_own[u, 0, :, cs] + y_recv[u, 0, :, cs].astype(F32)
            up = y_own[u, 1, :, cs] + y_recv[u, 1, :, cs].astype(F32)
            grad = y_own[u, 2, :, cs] + y_recv[u, 2, :, cs].astype(F32)
            sg = 1.0 / (1.0 + jnp.exp(-gate))
            co = pl.ds(u * cw + q * half, half)
            act[0, pl.ds(mine_r, own_rows), co] = (
                grad * up * sg * (1.0 + gate * (1.0 - sg))
            ).astype(BF16)
            act[1, pl.ds(mine_r, own_rows), co] = (grad * gate * sg).astype(BF16)
            act[2, pl.ds(mine_r, own_rows), co] = (gate * sg * up).astype(BF16)
        send(act_rows(mine_r, u), act_rows(mine_r, u), ya_s.at[u], ya_r.at[u], y_dev)

    def ag_slice(t, u, d, k, chunk):
        if k == steps - 1:
            c = pl.ds(u * cw + d * half, half)
        else:
            c = pl.ds(u * cw, cw)
        return act.at[t, pl.ds(z_rows(chunk), zrows), c]

    def ag_step(t, u, k):
        for d in range(2):
            sign = 1 - 2 * d
            if k > 0:
                ref = ag_slice(t, u, d, k - 1, z - k * sign)
                arrived(ref, ag_s.at[t, u, d, k - 1], ag_r.at[t, u, d, k - 1], z_dev[d])
            if k < steps:
                ref = ag_slice(t, u, d, k, z - k * sign)
                send(ref, ref, ag_s.at[t, u, d, k], ag_r.at[t, u, d, k], z_dev[d])

    out_copies = []

    def write_out(src, dst, index):
        copy = pltpu.make_async_copy(src, dst, out_sem.at[index])
        copy.start()
        out_copies.append(copy)

    def wide_dense(t):
        def body(j, carry):
            value = dot(tok_t[...], act[t, :, pl.ds(al(j * 2 * BLK, BLK), 2 * BLK)])
            low = lane_half(BLK) == 0
            for a in range(drb):
                for b in range(2):
                    both = value[a * BLK : (a + 1) * BLK, b * BLK : (b + 1) * BLK]
                    turned = swap(both)
                    dense[a * fcb + 4 * j + 2 * b] = jnp.where(low, both, turned)
                    dense[a * fcb + 4 * j + 2 * b + 1] = jnp.where(low, turned, both)
            return carry

        lax.fori_loop(0, fcb // 4, body, 0)

    def emit_wide(i):
        def body(s, carry):
            one = dense[slots_ref[i, s]]
            two = dense[slots_ref[i, s + cap // 2]]
            lanes = lane_half(HB)
            for h, value in enumerate((one, two)):
                keep = jnp.where(dp == 0, value[:HB], value[HB:])
                dp_own[i, h, s] = jnp.where(lanes == dp, keep, 0.0)
            give_one = jnp.where(dp == 0, one[HB:], one[:HB])
            give_two = jnp.where(dp == 0, two[HB:], two[:HB])
            dp_send[i, s] = jnp.where(lanes == 0, give_one, give_two).astype(BF16)
            return carry

        lax.fori_loop(0, cap // 2, body, 0)
        send(dp_send.at[i], recv_out.at[i], dp_s.at[i], dp_r.at[i], dp_dev)
        write_out(dp_own.at[i], own_out.at[i], i)

    def transpose_hidden(u):
        def body(j, carry):
            cs = pl.ds(al(u * cw + j * BLK, BLK), BLK)
            hid_t[cs, :] = act[2, :, cs].astype(F32).T.astype(BF16)
            return carry

        lax.fori_loop(0, cw // BLK, body, 0)

    def down_dense(u):
        per = cw // 256

        def body(j, carry):
            value = dot(hid_t[pl.ds(al(u * cw + j * 256, 256), 256), :], tcg[1])
            for a in range(4):
                for b in range(drb):
                    dense[(4 * (u * per + j) + a) * drb + b, pl.ds(0, HB)] = value[
                        a * HB : (a + 1) * HB, b * BLK : (b + 1) * BLK
                    ]
            return carry

        lax.fori_loop(0, per, body, 0)

    def emit_down():
        def body(s, carry):
            down_own[s] = dense[slots_ref[2, s], pl.ds(0, HB)]
            return carry

        lax.fori_loop(0, cap, body, 0)
        write_out(down_own, down_out, 2)

    def col_products(j, parts, first):
        step = min(256, width)

        def body(q, carry):
            cs = pl.ds(al(q * step, step), step)
            value = None if first else col_part[j, :, cs]
            for mul, a, b in parts:
                term = mul(a(), b(cs))
                value = term if value is None else value + term
            col_part[j, :, cs] = value
            return carry

        lax.fori_loop(0, width // step, body, 0)

    def layer_product(u):
        us = pl.ds(u * cw, cw)
        col_products(0, [(dot, lambda: act[2, :, us], lambda cs: wd[us, cs])], u == 0)

    def grad_product(t):
        w = (wg, wu)[t]
        col_products(1, [(dot_t, lambda: act[t], lambda cs: w[cs, :])], t == 0)

    def col_rows(c):
        return pl.ds(al(c * pair, pair), pair)

    def col_first(j):
        for xx in range(nx):
            ca_send[j, xx] = col_part[j, col_rows(xx * 2 + 1 - core), :].astype(BF16)
        send(ca_send.at[j], ca_recv.at[j], ca_s.at[j], ca_r.at[j], sib)

    def pair_sum(j, xx):
        return col_part[j, col_rows(xx * 2 + core), :] + ca_recv[j, xx].astype(F32)

    def col_second(j):
        arrived(ca_recv.at[j], ca_s.at[j], ca_r.at[j], sib)
        for k in range(1, nx):
            cb_send[j, k - 1] = pair_sum(j, lax.rem(x + k, nx)).astype(BF16)
            send(cb_send.at[j, k - 1], cb_recv.at[j, k - 1], cb_s.at[j, k - 1], cb_r.at[j, k - 1], x_dev(k))

    def col_third(j):
        value = pair_sum(j, x)
        for k in range(1, nx):
            arrived(cb_recv.at[j, k - 1], cb_s.at[j, k - 1], cb_r.at[j, k - 1], sib)
            value = value + cb_recv[j, k - 1].astype(F32)
        cc_sum[j] = value
        cc_send[j] = cc_sum[j, pl.ds(al((1 - dp) * n_tok, n_tok), n_tok), :].astype(BF16)
        send(cc_send.at[j], cc_recv.at[j], cc_s.at[j], cc_r.at[j], dp_dev)

    def col_last(j, out):
        arrived(cc_recv.at[j], cc_s.at[j], cc_r.at[j], dp_dev)
        value = cc_sum[j, pl.ds(al(dp * n_tok, n_tok), n_tok), :] + cc_recv[j].astype(F32)
        col_stage[j] = value.astype(BF16)
        write_out(col_stage.at[j], out, 3 + j)

    S = steps
    slots = {}

    def at(s, f, *a):
        slots.setdefault(s, []).append(functools.partial(f, *a))

    def y_arrived(u):
        arrived(act_rows(theirs_r, u), ya_s.at[u], ya_r.at[u], y_dev)

    def second_unit():
        product(2, 1)
        for t in range(3):
            for d in range(2):
                rs_start(t, 1, d, 0)

    def tok_transpose():
        tok_t[...] = tcg[0].astype(F32).T.astype(BF16)

    at(S, rs_finish, 0)
    at(S + 1, activate, 0)
    at(S + 2, y_arrived, 0)
    for k in range(1, S):
        at(k, rs_step, 0, k)
    at(S - 1, second_unit)
    for k in range(1, S):
        at(S - 1 + k, rs_step, 1, k)
    at(2 * S - 1, rs_finish, 1)
    at(2 * S, activate, 1)
    for k in range(S + 1):
        at(S + 2 + k, ag_step, 0, 0, k)
        at(S + 2 + k, ag_step, 1, 0, k)
        at(S + 3 + k, ag_step, 2, 0, k)
    at(2 * S + 1, y_arrived, 1)
    for k in range(S + 1):
        at(2 * S + 1 + k, ag_step, 0, 1, k)
        at(2 * S + 2 + k, ag_step, 1, 1, k)
        at(2 * S + 3 + k, ag_step, 2, 1, k)
    at(2 * S - 1, tok_transpose)
    at(2 * S + 4, transpose_hidden, 0)
    at(2 * S + 4, layer_product, 0)
    at(3 * S + 1, wide_dense, 0)
    at(3 * S + 1, emit_wide, 0)
    at(3 * S + 1, grad_product, 0)
    at(3 * S + 2, grad_product, 1)
    at(3 * S + 2, col_first, 1)
    at(3 * S + 2, wide_dense, 1)
    at(3 * S + 2, emit_wide, 1)
    at(3 * S + 2, col_second, 1)
    at(3 * S + 3, layer_product, 1)
    at(3 * S + 3, col_first, 0)
    at(3 * S + 3, col_third, 1)
    at(3 * S + 3, transpose_hidden, 1)
    at(3 * S + 3, col_second, 0)
    at(3 * S + 3, down_dense, 0)
    at(3 * S + 3, down_dense, 1)
    at(3 * S + 3, emit_down)
    at(3 * S + 3, col_third, 0)
    at(3 * S + 3, col_last, 1, tgrad_out)
    at(3 * S + 3, col_last, 0, layer_out)
    for s in sorted(slots):
        for f in slots[s]:
            f()
    for i in range(2):
        arrived(recv_out.at[i], dp_s.at[i], dp_r.at[i], dp_dev)
    for c in out_copies:
        c.wait()
    for c in sends:
        c.wait_send()


def finish(layer, tgrad, own, recv, down, layer_o, tgrad_o, gate_o, up_o, down_o):
    dp = lax.axis_index("dp")
    layer_o[...] = layer[...]
    tgrad_o[...] = tgrad[...]
    down_o[...] = down[...]
    lanes = lane_half(HB)
    for i, out in enumerate((gate_o, up_o)):
        for s in range(recv.shape[1]):
            value = recv[i, s].astype(F32)
            turned = swap(value)
            for h in range(2):
                other = jnp.where(dp == 1 - h, value, turned)
                out[h, s] = jnp.where(lanes == dp, own[i, h, s], other)


def per_device(tokens, cotangent, gate_blocks, up_blocks, down_blocks, gate_slots, up_slots, down_slots):
    n_row, n_col = lax.axis_size("row"), lax.axis_size("col")
    n_tok, width = tokens.shape
    cap = gate_blocks.shape[2]
    hid = FF // n_col // 2
    nz, nx = n_row // 2, n_col // 2
    steps = nz // 2
    group = 2 * n_tok * n_col
    zrows = group // nz
    own_rows = zrows // 2
    cw = hid // UNITS
    drb, fcb = width // BLK, hid // HB
    pair = 2 * n_tok
    slots = jnp.concatenate([gate_slots[0], up_slots[0], down_slots[0]], axis=0)
    place = jnp.arange(drb * fcb, dtype=jnp.int32)
    order = jnp.arange(cap, dtype=jnp.int32)
    inv = jnp.min(
        jnp.where(slots[:, None, :] == place[None, :, None], order[None, None, :], cap), axis=2
    )
    slots = jnp.where(slots < 0, drb * fcb, slots)
    dims = (n_row, n_col, n_tok, width, hid, cap)
    smem = pl.BlockSpec(memory_space=pltpu.SMEM)
    anym = pl.BlockSpec(memory_space=pl.ANY)
    vm = pltpu.VMEM
    dma = pltpu.SemaphoreType.DMA
    scratch = [
        vm((3, cap + 1, BLK, BLK), BF16),
        vm((2, group, width), BF16),
        vm((width, hid), BF16),
        vm((width, hid), BF16),
        vm((hid, width), BF16),
        vm((3, group, hid), F32),
        vm((3, UNITS, 2, steps, zrows, cw), BF16),
        vm((3, UNITS, 2, steps, zrows, cw), BF16),
        vm((UNITS, 3, own_rows, cw), BF16),
        vm((UNITS, 3, own_rows, cw), BF16),
        vm((UNITS, 3, own_rows, cw), F32),
        vm((3, group, hid), BF16),
        vm((width, group), BF16),
        vm((hid, group), BF16),
        vm((drb * fcb + 1, BLK, BLK), F32),
        vm((2, cap // 2, HB, BLK), BF16),
        vm((2, 2, cap // 2, HB, BLK), F32),
        vm((cap, HB, BLK), F32),
        vm((2, group, width), F32),
        vm((2, nx, pair, width), BF16),
        vm((2, nx, pair, width), BF16),
        vm((2, nx - 1, pair, width), BF16),
        vm((2, nx - 1, pair, width), BF16),
        vm((2, pair, width), F32),
        vm((2, n_tok, width), BF16),
        vm((2, n_tok, width), BF16),
        vm((2, n_tok, width), BF16),
        dma((5,)),
        dma((5,)),
        dma((2, 4 * nx - 1)),
        dma((2, 4 * nx - 1)),
        dma((3, UNITS, 2, steps)),
        dma((3, UNITS, 2, steps)),
        dma((UNITS,)),
        dma((UNITS,)),
        dma((UNITS,)),
        dma((UNITS,)),
        dma((3, UNITS, 2, steps)),
        dma((3, UNITS, 2, steps)),
        dma((2,)),
        dma((2,)),
        dma((2,)),
        dma((2,)),
        dma((2, nx - 1)),
        dma((2, nx - 1)),
        dma((2,)),
        dma((2,)),
    ]
    flops = 9 * 2 * group * width * hid
    inner = (
        jax.ShapeDtypeStruct((n_tok, width), BF16),
        jax.ShapeDtypeStruct((n_tok, width), BF16),
        jax.ShapeDtypeStruct((2, 2, cap // 2, HB, BLK), F32),
        jax.ShapeDtypeStruct((2, cap // 2, HB, BLK), BF16),
        jax.ShapeDtypeStruct((cap, HB, BLK), F32),
    )
    results = pl.pallas_call(
        functools.partial(kernel, dims),
        out_shape=inner,
        in_specs=[smem, smem, anym, anym, anym, anym, anym],
        out_specs=(anym,) * 5,
        scratch_shapes=scratch,
        compiler_params=pltpu.CompilerParams(
            collective_id=0, has_side_effects=True, vmem_limit_bytes=56 * 1024 * 1024
        ),
        cost_estimate=pl.CostEstimate(flops=flops, bytes_accessed=8 * 1024 * 1024, transcendentals=0),
        name="ffn",
    )(slots, inv, tokens, cotangent, gate_blocks[0, 0], up_blocks[0, 0], down_blocks[0, 0])
    ns = cap // 2 // GRID
    flat = pl.BlockSpec((n_tok, width), lambda g: (0, 0))
    wide = pl.BlockSpec((2, ns, HB, BLK), lambda g: (0, g, 0, 0))
    tall = pl.BlockSpec((2 * ns, HB, BLK), lambda g: (g, 0, 0))
    layer, tgrad, gate_grad, up_grad, down_grad = pl.pallas_call(
        finish,
        grid=(GRID,),
        out_shape=(
            inner[0],
            inner[1],
            jax.ShapeDtypeStruct((2, cap // 2, HB, BLK), F32),
            jax.ShapeDtypeStruct((2, cap // 2, HB, BLK), F32),
            inner[4],
        ),
        in_specs=[
            flat,
            flat,
            pl.BlockSpec((2, 2, ns, HB, BLK), lambda g: (0, 0, g, 0, 0)),
            wide,
            tall,
        ],
        out_specs=(flat, flat, wide, wide, tall),
        name="finish",
    )(*results)
    shape = (1, 1, cap, HB, BLK)
    return (layer, tgrad, gate_grad.reshape(shape), up_grad.reshape(shape), down_grad.reshape(shape))


def solution(mesh):
    in_specs = (
        P(("col", "dp"), "row"),
        P(("col", "dp"), "row"),
        P("row", "col", None, None, None),
        P("row", "col", None, None, None),
        P("col", "row", None, None, None),
        P("row", "col", None),
        P("row", "col", None),
        P("col", "row", None),
    )
    out_specs = (
        P(("col", "dp"), "row"),
        P(("col", "dp"), "row"),
        P("row", "col", None, "dp", None),
        P("row", "col", None, "dp", None),
        P("col", "row", None, "dp", None),
    )
    return jax.shard_map(
        per_device, mesh=mesh, in_specs=in_specs, out_specs=out_specs, check_vma=False
    )
```

```python
import functools

import jax
import jax.numpy as jnp
from jax import lax
from jax.experimental import pallas as pl
from jax.experimental.pallas import tpu as pltpu
from jax.sharding import PartitionSpec as P

FF = 16384
BLK = 128
HB = BLK // 2
UNITS = 2
GRID = 4
MESH = pl.DeviceIdType.MESH
F32 = jnp.float32
BF16 = jnp.bfloat16


def dot(a, b):
    return lax.dot_general(a, b, (((1,), (0,)), ((), ())), preferred_element_type=F32)


def dot_t(a, b):
    return lax.dot_general(a, b, (((1,), (1,)), ((), ())), preferred_element_type=F32)


def al(value, step):
    return pl.multiple_of(value, step)


def swap(value):
    return pltpu.roll(value, HB, 1)


def lane_half(rows):
    return (lax.broadcasted_iota(jnp.int32, (rows, BLK), 1) >= HB).astype(jnp.int32)


def kernel(
    dims,
    slots_ref,
    inv_ref,
    tok_in,
    cot_in,
    gate_in,
    up_in,
    down_in,
    layer_out,
    tgrad_out,
    own_out,
    recv_out,
    down_out,
    blocks,
    tcg,
    wg,
    wu,
    wd,
    part,
    rs_send,
    rs_recv,
    y_send,
    y_recv,
    y_own,
    yb_send,
    yb_recv,
    act,
    tok_t,
    hid_t,
    dense_g,
    dense_u,
    dense_d,
    dp_send,
    dp_own,
    down_own,
    col_part,
    ca_send,
    ca_recv,
    cb_send,
    cb_recv,
    cc_sum,
    cc_send,
    cc_recv,
    col_stage,
    loc_sem,
    out_sem,
    p1_s,
    p1_r,
    rs_s,
    rs_r,
    ys_s,
    ys_r,
    yb_s,
    yb_r,
    ya_s,
    ya_r,
    az_s,
    az_r,
    ay_s,
    ay_r,
    ag_s,
    ag_r,
    dp_s,
    dp_r,
    ca_s,
    ca_r,
    cb_s,
    cb_r,
    cc_s,
    cc_r,
):
    n_row, n_col, n_tok, width, hid, cap = dims
    nz, nx = n_row // 2, n_col // 2
    steps = nz // 2
    group = 2 * n_tok * n_col
    zrows = group // nz
    own_rows = zrows // 2
    cw = hid // UNITS
    half = cw // 2
    drb, fcb = width // BLK, hid // HB
    pair = 2 * n_tok

    row, col, dp = lax.axis_index("row"), lax.axis_index("col"), lax.axis_index("dp")
    z, yh = lax.div(row, 2), lax.rem(row, 2)
    x, core = lax.div(col, 2), lax.rem(col, 2)
    z_right = (lax.rem(z + 1, nz) * 2 + yh, col, dp)
    z_left = (lax.rem(z + nz - 1, nz) * 2 + yh, col, dp)
    z_dev = (z_right, z_left)
    y_dev = (z * 2 + 1 - yh, col, dp)
    sib = (row, x * 2 + 1 - core, dp)
    dp_dev = (row, col, 1 - dp)

    def x_dev(k, d):
        return (row, lax.rem(x + k, nx) * 2 + core, d)

    sends = []

    def send(src, dst, s_sem, r_sem, dev):
        copy = pltpu.make_async_remote_copy(
            src_ref=src, dst_ref=dst, send_sem=s_sem, recv_sem=r_sem, device_id=dev, device_id_type=MESH
        )
        copy.start()
        sends.append(copy)

    def arrived(dst, s_sem, r_sem, dev):
        pltpu.make_async_remote_copy(
            src_ref=dst, dst_ref=dst, send_sem=s_sem, recv_sem=r_sem, device_id=dev, device_id_type=MESH
        ).wait_recv()

    mine = pl.ds(al((col * 2 + dp) * n_tok, n_tok), n_tok)
    own_loads = [
        pltpu.make_async_copy(ref, tcg.at[j, mine, :], loc_sem.at[j])
        for j, ref in enumerate((tok_in, cot_in))
    ]
    block_loads = [
        pltpu.make_async_copy(ref, blocks.at[i, pl.ds(0, cap)], loc_sem.at[2 + i])
        for i, ref in enumerate((gate_in, up_in, down_in))
    ]
    for c in own_loads + block_loads:
        c.start()

    barrier = pltpu.get_barrier_semaphore()
    peers = [z_right, z_left, y_dev, sib, dp_dev] + [
        x_dev(k, d) for k in range(1, nx) for d in (dp, 1 - dp)
    ]
    for dev in peers:
        pl.semaphore_signal(barrier, inc=1, device_id=dev, device_id_type=MESH)
    pl.semaphore_wait(barrier, len(peers))

    def rows_of(j, index, n):
        return tcg.at[j, pl.ds(al(index * n_tok, n_tok), n * n_tok), :]

    def source(k, c):
        return (lax.rem(x + nx - k, nx) * 2 + c) * 2

    def give(j, ref, s, dev):
        send(ref, ref, p1_s.at[j, s], p1_r.at[j, s], dev)

    def take(j, ref, s):
        arrived(ref, p1_s.at[j, s], p1_r.at[j, s], sib)

    def gather_start(j):
        own_loads[j].wait()
        own = rows_of(j, source(0, core) + dp, 1)
        for k in range(1, nx):
            give(j, own, k, x_dev(k, dp))
            give(j, own, nx + k, x_dev(k, 1 - dp))
        give(j, own, nx, dp_dev)

    def gather_pass(j):
        for k in range(nx):
            if k > 0:
                take(j, rows_of(j, source(k, core) + dp, 1), k)
            take(j, rows_of(j, source(k, core) + 1 - dp, 1), nx + k)
            give(j, rows_of(j, source(k, core), 2), 2 * nx + k - 1 if k else 0, sib)

    def gather_end(j):
        for k in range(nx):
            take(j, rows_of(j, source(k, 1 - core), 2), 2 * nx + k - 1 if k else 0)

    gather_start(0)
    gather_start(1)

    for c in block_loads:
        c.wait()
    for i in range(3):
        blocks[i, cap] = jnp.zeros((BLK, BLK), BF16)
    for ref in (dense_g, dense_u, dense_d):
        ref[drb * fcb] = jnp.zeros(ref.shape[1:], F32)

    def place_wide(p, carry):
        r, c = p // (fcb // 2), p % (fcb // 2)
        keep = lane_half(BLK) == dp
        for i, w in enumerate((wg, wu)):
            even = blocks[i, inv_ref[i, 2 * p]].astype(F32)
            odd = blocks[i, inv_ref[i, 2 * p + 1]].astype(F32)
            stay = jnp.where(dp == 0, even, odd)
            move = swap(jnp.where(dp == 0, odd, even))
            w[pl.ds(al(r * BLK, BLK), BLK), pl.ds(al(c * BLK, BLK), BLK)] = jnp.where(
                keep, stay, move
            ).astype(BF16)
        return carry

    def place_down(p, carry):
        value = blocks[2, inv_ref[2, p]]
        r, c = p // drb, p % drb
        wd[pl.ds(al(r * HB, HB), HB), pl.ds(al(c * BLK, BLK), BLK)] = jnp.where(
            dp == 0, value[:HB], value[HB:]
        )
        return carry

    lax.fori_loop(0, drb * fcb // 2, place_wide, 0)
    lax.fori_loop(0, drb * fcb, place_down, 0)
    gather_pass(0)
    gather_end(0)

    def z_rows(t):
        return al(lax.rem(t + 2 * nz, nz) * zrows, zrows)

    def unit_rows(u, target):
        if u == 0:
            return z_rows(target)
        return al(z_rows(target) + yh * own_rows, own_rows)

    count = (zrows, own_rows)

    def rs_ref(buf, t, u, d, k):
        cs = pl.ds(d * half, half) if k == 0 else pl.ds(0, cw)
        return buf.at[t, u, d, k, pl.ds(0, count[u]), cs]

    def rs_start(t, u, d, k):
        target = z + (steps - k) * (1 - 2 * d)
        rs = pl.ds(unit_rows(u, target), count[u])
        to = pl.ds(0, count[u])
        for h in range(2):
            if k == 0 and h != d:
                continue
            hc = pl.ds(h * half, half)
            value = part[t, rs, pl.ds(u * cw + h * half, half)]
            if k > 1 or (k == 1 and h == d):
                value = value + rs_recv[t, u, d, k - 1, to, hc].astype(F32)
            rs_send[t, u, d, k, to, hc] = value.astype(BF16)
        send(
            rs_ref(rs_send, t, u, d, k),
            rs_ref(rs_recv, t, u, d, k),
            rs_s.at[t, u, d, k],
            rs_r.at[t, u, d, k],
            z_dev[d],
        )

    def rs_wait(t, u, d, k):
        arrived(rs_ref(rs_recv, t, u, d, k), rs_s.at[t, u, d, k], rs_r.at[t, u, d, k], z_dev[d])

    def rs_step(t, u, k):
        for d in range(2):
            rs_wait(t, u, d, k - 1)
            rs_start(t, u, d, k)

    def yb_start(t):
        for c in range(nz):
            r0 = al(c * zrows + (1 - yh) * own_rows, own_rows)
            yb_send[t, c] = part[t, pl.ds(r0, own_rows), pl.ds(cw, cw)].astype(BF16)
        send(yb_send.at[t], yb_recv.at[t], yb_s.at[t], yb_r.at[t], y_dev)

    def yb_add(t):
        arrived(yb_recv.at[t], yb_s.at[t], yb_r.at[t], y_dev)
        for c in range(nz):
            rs = pl.ds(al(c * zrows + yh * own_rows, own_rows), own_rows)
            part[t, rs, pl.ds(cw, cw)] = part[t, rs, pl.ds(cw, cw)] + yb_recv[t, c].astype(F32)
        for d in range(2):
            rs_start(t, 1, d, 0)

    tile = min(256, cw)

    def product(t, u):
        def body(j, carry):
            cs = pl.ds(al(u * cw + j * tile, tile), tile)
            if t == 2:
                part[t, :, cs] = dot_t(tcg[1], wd[cs, :])
            else:
                part[t, :, cs] = dot(tcg[0], (wg, wu)[t][:, cs])
            return carry

        lax.fori_loop(0, cw // tile, body, 0)

    for t in range(2):
        product(t, 0)
        for d in range(2):
            rs_start(t, 0, d, 0)
        product(t, 1)
        yb_start(t)
        if t == 0:
            gather_pass(1)
    gather_end(1)
    product(2, 0)
    for d in range(2):
        rs_start(2, 0, d, 0)
    product(2, 1)
    yb_start(2)

    mine_r = al(z * zrows + yh * own_rows, own_rows)
    theirs_r = al(z * zrows + (1 - yh) * own_rows, own_rows)
    mine_o, theirs_o = al(yh * own_rows, own_rows), al((1 - yh) * own_rows, own_rows)

    def last_sum(t, u, r0, o0):
        value = part[t, pl.ds(r0, own_rows), pl.ds(u * cw, cw)]
        for d in range(2):
            value = value + rs_recv[t, u, d, steps - 1, pl.ds(o0, own_rows), :].astype(F32)
        return value

    def rs_finish(t, u):
        for d in range(2):
            rs_wait(t, u, d, steps - 1)
        if u == 0:
            y_send[t] = last_sum(t, u, theirs_r, theirs_o).astype(BF16)
            y_own[u, t] = last_sum(t, u, mine_r, mine_o)
            if t == 2:
                send(y_send, y_recv, ys_s.at[0], ys_r.at[0], y_dev)
        else:
            y_own[u, t] = last_sum(t, u, mine_r, 0)

    def rows_ref(r0, u):
        return act.at[:, pl.ds(r0, own_rows), pl.ds(u * cw, cw)]

    def activate(u):
        if u == 0:
            arrived(y_recv, ys_s.at[0], ys_r.at[0], y_dev)
        for q in range(2):
            cs = pl.ds(q * half, half)
            gate, up, grad = (y_own[u, t, :, cs] for t in range(3))
            if u == 0:
                gate = gate + y_recv[0, :, cs].astype(F32)
                up = up + y_recv[1, :, cs].astype(F32)
                grad = grad + y_recv[2, :, cs].astype(F32)
            sg = 1.0 / (1.0 + jnp.exp(-gate))
            co = pl.ds(u * cw + q * half, half)
            act[0, pl.ds(mine_r, own_rows), co] = (
                grad * up * sg * (1.0 + gate * (1.0 - sg))
            ).astype(BF16)
            act[1, pl.ds(mine_r, own_rows), co] = (grad * gate * sg).astype(BF16)
            act[2, pl.ds(mine_r, own_rows), co] = (gate * sg * up).astype(BF16)
        ref = rows_ref(mine_r, u)
        if u == 0:
            send(ref, ref, ay_s.at[0, steps], ay_r.at[0, steps], y_dev)
        else:
            send(ref, ref, ya_s.at[0], ya_r.at[0], y_dev)

    def az_chunk(d, k, hops, hi):
        rs = pl.ds(al(z_rows(z - hops * (1 - 2 * d)) + hi * own_rows, own_rows), own_rows)
        cs = pl.ds(d * half, half) if k == steps - 1 else pl.ds(0, cw)
        return act.at[:, rs, cs]

    def az_step(k):
        for d in range(2):
            if k > 0:
                ref = az_chunk(d, k - 1, k, yh)
                arrived(ref, az_s.at[d, k - 1], az_r.at[d, k - 1], z_dev[d])
            if k < steps:
                out = az_chunk(d, k, k, yh)
                send(out, out, az_s.at[d, k], az_r.at[d, k], z_dev[d])
            if k > 0:
                send(ref, ref, ay_s.at[d, k - 1], ay_r.at[d, k - 1], y_dev)

    def ay_wait():
        arrived(rows_ref(theirs_r, 0), ay_s.at[0, steps], ay_r.at[0, steps], y_dev)
        for k in range(1, steps + 1):
            for d in range(2):
                ref = az_chunk(d, k - 1, k, 1 - yh)
                arrived(ref, ay_s.at[d, k - 1], ay_r.at[d, k - 1], y_dev)

    def ag_slice(t, d, k, chunk):
        if k == steps - 1:
            c = pl.ds(cw + d * half, half)
        else:
            c = pl.ds(cw, cw)
        return act.at[t, pl.ds(z_rows(chunk), zrows), c]

    def ag_step(t, k):
        for d in range(2):
            sign = 1 - 2 * d
            if k > 0:
                ref = ag_slice(t, d, k - 1, z - k * sign)
                arrived(ref, ag_s.at[t, d, k - 1], ag_r.at[t, d, k - 1], z_dev[d])
            if k < steps:
                ref = ag_slice(t, d, k, z - k * sign)
                send(ref, ref, ag_s.at[t, d, k], ag_r.at[t, d, k], z_dev[d])

    out_copies = []

    def write_out(src, dst, index):
        copy = pltpu.make_async_copy(src, dst, out_sem.at[index])
        copy.start()
        out_copies.append(copy)

    def wide_dense(t, u):
        dense = (dense_g, dense_u)[t]
        per = cw // (2 * BLK)

        def body(j, carry):
            value = dot(tok_t[...], act[t, :, pl.ds(al(u * cw + j * 2 * BLK, BLK), 2 * BLK)])
            low = lane_half(BLK) == 0
            for a in range(drb):
                for b in range(2):
                    both = value[a * BLK : (a + 1) * BLK, b * BLK : (b + 1) * BLK]
                    turned = swap(both)
                    c = 4 * (u * per + j) + 2 * b
                    dense[a * fcb + c] = jnp.where(low, both, turned)
                    dense[a * fcb + c + 1] = jnp.where(low, turned, both)
            return carry

        lax.fori_loop(0, per, body, 0)

    def emit_wide(i):
        dense = (dense_g, dense_u)[i]

        def body(s, carry):
            one = dense[slots_ref[i, s]]
            two = dense[slots_ref[i, s + cap // 2]]
            lanes = lane_half(HB)
            for h, value in enumerate((one, two)):
                keep = jnp.where(dp == 0, value[:HB], value[HB:])
                dp_own[i, h, s] = jnp.where(lanes == dp, keep, 0.0)
            give_one = jnp.where(dp == 0, one[HB:], one[:HB])
            give_two = jnp.where(dp == 0, two[HB:], two[:HB])
            dp_send[i, s] = jnp.where(lanes == 0, give_one, give_two).astype(BF16)
            return carry

        lax.fori_loop(0, cap // 2, body, 0)
        send(dp_send.at[i], recv_out.at[i], dp_s.at[i], dp_r.at[i], dp_dev)
        write_out(dp_own.at[i], own_out.at[i], i)

    def transpose_hidden(u):
        def body(j, carry):
            cs = pl.ds(al(u * cw + j * BLK, BLK), BLK)
            hid_t[cs, :] = act[2, :, cs].astype(F32).T.astype(BF16)
            return carry

        lax.fori_loop(0, cw // BLK, body, 0)

    def down_dense(u):
        per = cw // 256

        def body(j, carry):
            value = dot(hid_t[pl.ds(al(u * cw + j * 256, 256), 256), :], tcg[1])
            for a in range(4):
                for b in range(drb):
                    dense_d[(4 * (u * per + j) + a) * drb + b] = value[
                        a * HB : (a + 1) * HB, b * BLK : (b + 1) * BLK
                    ]
            return carry

        lax.fori_loop(0, per, body, 0)

    def emit_down():
        def body(s, carry):
            down_own[s] = dense_d[slots_ref[2, s]]
            return carry

        lax.fori_loop(0, cap, body, 0)
        write_out(down_own, down_out, 2)

    def col_products(j, parts, first):
        step = min(256, width)

        def body(q, carry):
            cs = pl.ds(al(q * step, step), step)
            value = None if first else col_part[j, :, cs]
            for mul, a, b in parts:
                term = mul(a(), b(cs))
                value = term if value is None else value + term
            col_part[j, :, cs] = value
            return carry

        lax.fori_loop(0, width // step, body, 0)

    def layer_product(u):
        us = pl.ds(u * cw, cw)
        col_products(0, [(dot, lambda: act[2, :, us], lambda cs: wd[us, cs])], u == 0)

    def grad_product(u):
        us = pl.ds(u * cw, cw)
        parts = [
            (dot_t, lambda: act[0, :, us], lambda cs: wg[cs, us]),
            (dot_t, lambda: act[1, :, us], lambda cs: wu[cs, us]),
        ]
        col_products(1, parts, u == 0)

    def col_rows(c):
        return pl.ds(al(c * pair, pair), pair)

    def col_first(j):
        for xx in range(nx):
            ca_send[j, xx] = col_part[j, col_rows(xx * 2 + 1 - core), :].astype(BF16)
        send(ca_send.at[j], ca_recv.at[j], ca_s.at[j], ca_r.at[j], sib)

    def pair_sum(j, xx):
        return col_part[j, col_rows(xx * 2 + core), :] + ca_recv[j, xx].astype(F32)

    def col_second(j):
        arrived(ca_recv.at[j], ca_s.at[j], ca_r.at[j], sib)
        for k in range(1, nx):
            cb_send[j, k - 1] = pair_sum(j, lax.rem(x + k, nx)).astype(BF16)
            send(cb_send.at[j, k - 1], cb_recv.at[j, k - 1], cb_s.at[j, k - 1], cb_r.at[j, k - 1], x_dev(k, dp))

    def col_third(j):
        value = pair_sum(j, x)
        for k in range(1, nx):
            arrived(cb_recv.at[j, k - 1], cb_s.at[j, k - 1], cb_r.at[j, k - 1], sib)
            value = value + cb_recv[j, k - 1].astype(F32)
        cc_sum[j] = value
        cc_send[j] = cc_sum[j, pl.ds(al((1 - dp) * n_tok, n_tok), n_tok), :].astype(BF16)
        send(cc_send.at[j], cc_recv.at[j], cc_s.at[j], cc_r.at[j], dp_dev)

    def col_last(j, out):
        arrived(cc_recv.at[j], cc_s.at[j], cc_r.at[j], dp_dev)
        value = cc_sum[j, pl.ds(al(dp * n_tok, n_tok), n_tok), :] + cc_recv[j].astype(F32)
        col_stage[j] = value.astype(BF16)
        write_out(col_stage.at[j], out, 3 + j)

    S = steps
    slots = {}

    def at(s, f, *a):
        slots.setdefault(s, []).append(functools.partial(f, *a))

    def y_arrived():
        arrived(rows_ref(theirs_r, 1), ya_s.at[0], ya_r.at[0], y_dev)

    def tok_transpose():
        tok_t[...] = tcg[0].astype(F32).T.astype(BF16)

    for k in range(1, S):
        for t in range(3):
            at(k, rs_step, t, 0, k)
    at(S - 1, yb_add, 0)
    at(S - 1, yb_add, 1)
    for t in range(3):
        at(S, rs_finish, t, 0)
    at(S, rs_step, 0, 1, 1)
    at(S, rs_step, 1, 1, 1)
    at(S, yb_add, 2)
    at(S + 1, activate, 0)
    for k in range(S + 1):
        at(S + 1 + k, az_step, k)
    for k in range(2, S):
        at(S - 1 + k, rs_step, 0, 1, k)
        at(S - 1 + k, rs_step, 1, 1, k)
    for k in range(1, S):
        at(S + k, rs_step, 2, 1, k)
    at(2 * S - 1, tok_transpose)
    for t in range(3):
        at(2 * S, rs_finish, t, 1)
    at(2 * S, activate, 1)
    at(2 * S + 1, y_arrived)
    for k in range(S + 1):
        at(2 * S + 1 + k, ag_step, 0, k)
        at(2 * S + 1 + k, ag_step, 1, k)
        at(2 * S + 2 + k, ag_step, 2, k)
    A = 3 * S
    at(A, ay_wait)
    at(A, wide_dense, 0, 0)
    at(A, wide_dense, 1, 0)
    at(A, grad_product, 0)
    A = 3 * S + 1
    at(A, wide_dense, 0, 1)
    at(A, emit_wide, 0)
    at(A, grad_product, 1)
    at(A, col_first, 1)
    at(A, wide_dense, 1, 1)
    at(A, emit_wide, 1)
    at(A, col_second, 1)
    at(A, layer_product, 0)
    at(A, transpose_hidden, 0)
    at(A, down_dense, 0)
    at(A, col_third, 1)
    A = 3 * S + 2
    at(A, layer_product, 1)
    at(A, col_first, 0)
    at(A, transpose_hidden, 1)
    at(A, col_second, 0)
    at(A, down_dense, 1)
    at(A, emit_down)
    at(A, col_third, 0)
    at(A, col_last, 1, tgrad_out)
    at(A, col_last, 0, layer_out)
    for s in sorted(slots):
        for f in slots[s]:
            f()
    for i in range(2):
        arrived(recv_out.at[i], dp_s.at[i], dp_r.at[i], dp_dev)
    for c in out_copies:
        c.wait()
    for c in sends:
        c.wait_send()


def finish(layer, tgrad, own, recv, down, layer_o, tgrad_o, gate_o, up_o, down_o):
    dp = lax.axis_index("dp")
    layer_o[...] = layer[...]
    tgrad_o[...] = tgrad[...]
    down_o[...] = down[...]
    lanes = lane_half(HB)
    for i, out in enumerate((gate_o, up_o)):
        for s in range(recv.shape[1]):
            value = recv[i, s].astype(F32)
            turned = swap(value)
            for h in range(2):
                other = jnp.where(dp == 1 - h, value, turned)
                out[h, s] = jnp.where(lanes == dp, own[i, h, s], other)


def per_device(tokens, cotangent, gate_blocks, up_blocks, down_blocks, gate_slots, up_slots, down_slots):
    n_row, n_col = lax.axis_size("row"), lax.axis_size("col")
    n_tok, width = tokens.shape
    cap = gate_blocks.shape[2]
    hid = FF // n_col // 2
    nz, nx = n_row // 2, n_col // 2
    steps = nz // 2
    group = 2 * n_tok * n_col
    zrows = group // nz
    own_rows = zrows // 2
    cw = hid // UNITS
    drb, fcb = width // BLK, hid // HB
    pair = 2 * n_tok
    slots = jnp.concatenate([gate_slots[0], up_slots[0], down_slots[0]], axis=0)
    place = jnp.arange(drb * fcb, dtype=jnp.int32)
    order = jnp.arange(cap, dtype=jnp.int32)
    inv = jnp.min(
        jnp.where(slots[:, None, :] == place[None, :, None], order[None, None, :], cap), axis=2
    )
    slots = jnp.where(slots < 0, drb * fcb, slots)
    dims = (n_row, n_col, n_tok, width, hid, cap)
    smem = pl.BlockSpec(memory_space=pltpu.SMEM)
    anym = pl.BlockSpec(memory_space=pl.ANY)
    vm = pltpu.VMEM
    dma = pltpu.SemaphoreType.DMA
    scratch = [
        vm((3, cap + 1, BLK, BLK), BF16),
        vm((2, group, width), BF16),
        vm((width, hid), BF16),
        vm((width, hid), BF16),
        vm((hid, width), BF16),
        vm((3, group, hid), F32),
        vm((3, UNITS, 2, steps, zrows, cw), BF16),
        vm((3, UNITS, 2, steps, zrows, cw), BF16),
        vm((3, own_rows, cw), BF16),
        vm((3, own_rows, cw), BF16),
        vm((UNITS, 3, own_rows, cw), F32),
        vm((3, nz, own_rows, cw), BF16),
        vm((3, nz, own_rows, cw), BF16),
        vm((3, group, hid), BF16),
        vm((width, group), BF16),
        vm((hid, group), BF16),
        vm((drb * fcb + 1, BLK, BLK), F32),
        vm((drb * fcb + 1, BLK, BLK), F32),
        vm((drb * fcb + 1, HB, BLK), F32),
        vm((2, cap // 2, HB, BLK), BF16),
        vm((2, 2, cap // 2, HB, BLK), F32),
        vm((cap, HB, BLK), F32),
        vm((2, group, width), F32),
        vm((2, nx, pair, width), BF16),
        vm((2, nx, pair, width), BF16),
        vm((2, nx - 1, pair, width), BF16),
        vm((2, nx - 1, pair, width), BF16),
        vm((2, pair, width), F32),
        vm((2, n_tok, width), BF16),
        vm((2, n_tok, width), BF16),
        vm((2, n_tok, width), BF16),
        dma((5,)),
        dma((5,)),
        dma((2, 3 * nx - 1)),
        dma((2, 3 * nx - 1)),
        dma((3, UNITS, 2, steps)),
        dma((3, UNITS, 2, steps)),
        dma((1,)),
        dma((1,)),
        dma((3,)),
        dma((3,)),
        dma((1,)),
        dma((1,)),
        dma((2, steps)),
        dma((2, steps)),
        dma((2, steps + 1)),
        dma((2, steps + 1)),
        dma((3, 2, steps)),
        dma((3, 2, steps)),
        dma((2,)),
        dma((2,)),
        dma((2,)),
        dma((2,)),
        dma((2, nx - 1)),
        dma((2, nx - 1)),
        dma((2,)),
        dma((2,)),
    ]
    flops = 9 * 2 * group * width * hid
    inner = (
        jax.ShapeDtypeStruct((n_tok, width), BF16),
        jax.ShapeDtypeStruct((n_tok, width), BF16),
        jax.ShapeDtypeStruct((2, 2, cap // 2, HB, BLK), F32),
        jax.ShapeDtypeStruct((2, cap // 2, HB, BLK), BF16),
        jax.ShapeDtypeStruct((cap, HB, BLK), F32),
    )
    results = pl.pallas_call(
        functools.partial(kernel, dims),
        out_shape=inner,
        in_specs=[smem, smem, anym, anym, anym, anym, anym],
        out_specs=(anym,) * 5,
        scratch_shapes=scratch,
        compiler_params=pltpu.CompilerParams(
            collective_id=0, has_side_effects=True, vmem_limit_bytes=56 * 1024 * 1024
        ),
        cost_estimate=pl.CostEstimate(flops=flops, bytes_accessed=8 * 1024 * 1024, transcendentals=0),
        name="ffn",
    )(slots, inv, tokens, cotangent, gate_blocks[0, 0], up_blocks[0, 0], down_blocks[0, 0])
    ns = cap // 2 // GRID
    flat = pl.BlockSpec((n_tok, width), lambda g: (0, 0))
    wide = pl.BlockSpec((2, ns, HB, BLK), lambda g: (0, g, 0, 0))
    tall = pl.BlockSpec((2 * ns, HB, BLK), lambda g: (g, 0, 0))
    layer, tgrad, gate_grad, up_grad, down_grad = pl.pallas_call(
        finish,
        grid=(GRID,),
        out_shape=(
            inner[0],
            inner[1],
            jax.ShapeDtypeStruct((2, cap // 2, HB, BLK), F32),
            jax.ShapeDtypeStruct((2, cap // 2, HB, BLK), F32),
            inner[4],
        ),
        in_specs=[
            flat,
            flat,
            pl.BlockSpec((2, 2, ns, HB, BLK), lambda g: (0, 0, g, 0, 0)),
            wide,
            tall,
        ],
        out_specs=(flat, flat, wide, wide, tall),
        name="finish",
    )(*results)
    shape = (1, 1, cap, HB, BLK)
    return (layer, tgrad, gate_grad.reshape(shape), up_grad.reshape(shape), down_grad.reshape(shape))


def solution(mesh):
    in_specs = (
        P(("col", "dp"), "row"),
        P(("col", "dp"), "row"),
        P("row", "col", None, None, None),
        P("row", "col", None, None, None),
        P("col", "row", None, None, None),
        P("row", "col", None),
        P("row", "col", None),
        P("col", "row", None),
    )
    out_specs = (
        P(("col", "dp"), "row"),
        P(("col", "dp"), "row"),
        P("row", "col", None, "dp", None),
        P("row", "col", None, "dp", None),
        P("col", "row", None, "dp", None),
    )
    return jax.shard_map(
        per_device, mesh=mesh, in_specs=in_specs, out_specs=out_specs, check_vma=False
    )
```

```python
import functools

import jax
import jax.numpy as jnp
from jax import lax
from jax.experimental import pallas as pl
from jax.experimental.pallas import tpu as pltpu
from jax.sharding import PartitionSpec as P

FF = 16384
BLK = 128
HB = BLK // 2
UNITS = 2
GRID = 2
MESH = pl.DeviceIdType.MESH
F32 = jnp.float32
BF16 = jnp.bfloat16


def dot(a, b):
    return lax.dot_general(a, b, (((1,), (0,)), ((), ())), preferred_element_type=F32)


def dot_t(a, b):
    return lax.dot_general(a, b, (((1,), (1,)), ((), ())), preferred_element_type=F32)


def al(value, step):
    return pl.multiple_of(value, step)


def swap(value):
    return pltpu.roll(value, HB, 1)


def lane_half(rows):
    return (lax.broadcasted_iota(jnp.int32, (rows, BLK), 1) >= HB).astype(jnp.int32)


def kernel(
    dims,
    slots_ref,
    inv_ref,
    tok_in,
    cot_in,
    gate_in,
    up_in,
    down_in,
    layer_out,
    tgrad_out,
    own_out,
    recv_out,
    down_out,
    blocks,
    tcg,
    wg,
    wu,
    wd,
    part,
    rs_send,
    rs_recv,
    y_send,
    y_recv,
    y_own,
    yb_send,
    yb_recv,
    act,
    tok_t,
    hid_t,
    dense_g,
    dense_u,
    dense_d,
    dp_send,
    dp_own,
    down_own,
    col_part,
    ca_send,
    ca_recv,
    cb_send,
    cb_recv,
    cc_sum,
    cc_send,
    cc_recv,
    col_stage,
    loc_sem,
    out_sem,
    p1_s,
    p1_r,
    rs_s,
    rs_r,
    ys_s,
    ys_r,
    yb_s,
    yb_r,
    ya_s,
    ya_r,
    az_s,
    az_r,
    ay_s,
    ay_r,
    ag_s,
    ag_r,
    dp_s,
    dp_r,
    ca_s,
    ca_r,
    cb_s,
    cb_r,
    cc_s,
    cc_r,
):
    n_row, n_col, n_tok, width, hid, cap = dims
    nz, nx = n_row // 2, n_col // 2
    steps = nz // 2
    group = 2 * n_tok * n_col
    zrows = group // nz
    own_rows = zrows // 2
    cw = hid // UNITS
    half = cw // 2
    drb, fcb = width // BLK, hid // HB
    pair = 2 * n_tok

    row, col, dp = lax.axis_index("row"), lax.axis_index("col"), lax.axis_index("dp")
    z, yh = lax.div(row, 2), lax.rem(row, 2)
    x, core = lax.div(col, 2), lax.rem(col, 2)
    z_right = (lax.rem(z + 1, nz) * 2 + yh, col, dp)
    z_left = (lax.rem(z + nz - 1, nz) * 2 + yh, col, dp)
    z_dev = (z_right, z_left)
    y_dev = (z * 2 + 1 - yh, col, dp)
    sib = (row, x * 2 + 1 - core, dp)
    dp_dev = (row, col, 1 - dp)

    def x_dev(k, d):
        return (row, lax.rem(x + k, nx) * 2 + core, d)

    sends = []

    def send(src, dst, s_sem, r_sem, dev):
        copy = pltpu.make_async_remote_copy(
            src_ref=src, dst_ref=dst, send_sem=s_sem, recv_sem=r_sem, device_id=dev, device_id_type=MESH
        )
        copy.start()
        sends.append(copy)

    def arrived(dst, s_sem, r_sem, dev):
        pltpu.make_async_remote_copy(
            src_ref=dst, dst_ref=dst, send_sem=s_sem, recv_sem=r_sem, device_id=dev, device_id_type=MESH
        ).wait_recv()

    mine = pl.ds(al((col * 2 + dp) * n_tok, n_tok), n_tok)
    own_loads = [
        pltpu.make_async_copy(ref, tcg.at[j, mine, :], loc_sem.at[j])
        for j, ref in enumerate((tok_in, cot_in))
    ]
    block_loads = [
        pltpu.make_async_copy(ref, blocks.at[i, pl.ds(0, cap)], loc_sem.at[2 + i])
        for i, ref in enumerate((gate_in, up_in, down_in))
    ]
    for c in own_loads + block_loads:
        c.start()

    barrier = pltpu.get_barrier_semaphore()
    peers = [z_right, z_left, y_dev, sib, dp_dev] + [
        x_dev(k, d) for k in range(1, nx) for d in (dp, 1 - dp)
    ]
    for dev in peers:
        pl.semaphore_signal(barrier, inc=1, device_id=dev, device_id_type=MESH)
    pl.semaphore_wait(barrier, len(peers))

    def rows_of(j, index, n):
        return tcg.at[j, pl.ds(al(index * n_tok, n_tok), n * n_tok), :]

    def source(k, c):
        return (lax.rem(x + nx - k, nx) * 2 + c) * 2

    def give(j, ref, s, dev):
        send(ref, ref, p1_s.at[j, s], p1_r.at[j, s], dev)

    def take(j, ref, s):
        arrived(ref, p1_s.at[j, s], p1_r.at[j, s], sib)

    def gather_start(j):
        own_loads[j].wait()
        own = rows_of(j, source(0, core) + dp, 1)
        for k in range(1, nx):
            give(j, own, k, x_dev(k, dp))
            give(j, own, nx + k, x_dev(k, 1 - dp))
        give(j, own, nx, dp_dev)

    def gather_pass(j):
        for k in range(nx):
            if k > 0:
                take(j, rows_of(j, source(k, core) + dp, 1), k)
            take(j, rows_of(j, source(k, core) + 1 - dp, 1), nx + k)
            give(j, rows_of(j, source(k, core), 2), 2 * nx + k - 1 if k else 0, sib)

    def gather_end(j):
        for k in range(nx):
            take(j, rows_of(j, source(k, 1 - core), 2), 2 * nx + k - 1 if k else 0)

    gather_start(0)
    gather_start(1)

    for c in block_loads:
        c.wait()
    for i in range(3):
        blocks[i, cap] = jnp.zeros((BLK, BLK), BF16)
    for ref in (dense_g, dense_u, dense_d):
        ref[drb * fcb] = jnp.zeros(ref.shape[1:], F32)

    def place_wide(p, carry):
        r, c = p // (fcb // 2), p % (fcb // 2)
        keep = lane_half(BLK) == dp
        for i, w in enumerate((wg, wu)):
            even = blocks[i, inv_ref[i, 2 * p]].astype(F32)
            odd = blocks[i, inv_ref[i, 2 * p + 1]].astype(F32)
            stay = jnp.where(dp == 0, even, odd)
            move = swap(jnp.where(dp == 0, odd, even))
            w[pl.ds(al(r * BLK, BLK), BLK), pl.ds(al(c * BLK, BLK), BLK)] = jnp.where(
                keep, stay, move
            ).astype(BF16)
        return carry

    def place_down(p, carry):
        value = blocks[2, inv_ref[2, p]]
        r, c = p // drb, p % drb
        wd[pl.ds(al(r * HB, HB), HB), pl.ds(al(c * BLK, BLK), BLK)] = jnp.where(
            dp == 0, value[:HB], value[HB:]
        )
        return carry

    lax.fori_loop(0, drb * fcb // 2, place_wide, 0)
    lax.fori_loop(0, drb * fcb, place_down, 0)
    gather_pass(0)
    gather_end(0)

    def z_rows(t):
        return al(lax.rem(t + 2 * nz, nz) * zrows, zrows)

    def split(t, u):
        return u == 1 and t < 2

    def unit_rows(t, u, target):
        if not split(t, u):
            return z_rows(target)
        return al(z_rows(target) + yh * own_rows, own_rows)

    def count(t, u):
        return own_rows if split(t, u) else zrows

    def rs_ref(buf, t, u, d, k):
        cs = pl.ds(d * half, half) if k == 0 else pl.ds(0, cw)
        return buf.at[t, u, d, k, pl.ds(0, count(t, u)), cs]

    def rs_start(t, u, d, k):
        target = z + (steps - k) * (1 - 2 * d)
        rs = pl.ds(unit_rows(t, u, target), count(t, u))
        to = pl.ds(0, count(t, u))
        for h in range(2):
            if k == 0 and h != d:
                continue
            hc = pl.ds(h * half, half)
            value = part[t, rs, pl.ds(u * cw + h * half, half)]
            if k > 1 or (k == 1 and h == d):
                value = value + rs_recv[t, u, d, k - 1, to, hc].astype(F32)
            rs_send[t, u, d, k, to, hc] = value.astype(BF16)
        send(
            rs_ref(rs_send, t, u, d, k),
            rs_ref(rs_recv, t, u, d, k),
            rs_s.at[t, u, d, k],
            rs_r.at[t, u, d, k],
            z_dev[d],
        )

    def rs_wait(t, u, d, k):
        arrived(rs_ref(rs_recv, t, u, d, k), rs_s.at[t, u, d, k], rs_r.at[t, u, d, k], z_dev[d])

    def rs_step(t, u, k):
        for d in range(2):
            rs_wait(t, u, d, k - 1)
            rs_start(t, u, d, k)

    def yb_start(t):
        for c in range(nz):
            r0 = al(c * zrows + (1 - yh) * own_rows, own_rows)
            yb_send[t, c] = part[t, pl.ds(r0, own_rows), pl.ds(cw, cw)].astype(BF16)
        send(yb_send.at[t], yb_recv.at[t], yb_s.at[t], yb_r.at[t], y_dev)

    def yb_add(t):
        arrived(yb_recv.at[t], yb_s.at[t], yb_r.at[t], y_dev)
        for c in range(nz):
            rs = pl.ds(al(c * zrows + yh * own_rows, own_rows), own_rows)
            part[t, rs, pl.ds(cw, cw)] = part[t, rs, pl.ds(cw, cw)] + yb_recv[t, c].astype(F32)
        for d in range(2):
            rs_start(t, 1, d, 0)

    tile = min(256, cw)

    def product(t, u):
        def body(j, carry):
            cs = pl.ds(al(u * cw + j * tile, tile), tile)
            if t == 2:
                part[t, :, cs] = dot_t(tcg[1], wd[cs, :])
            else:
                part[t, :, cs] = dot(tcg[0], (wg, wu)[t][:, cs])
            return carry

        lax.fori_loop(0, cw // tile, body, 0)

    for t in range(2):
        product(t, 0)
        for d in range(2):
            rs_start(t, 0, d, 0)
        product(t, 1)
        yb_start(t)
        if t == 0:
            gather_pass(1)
    gather_end(1)
    product(2, 0)
    for d in range(2):
        rs_start(2, 0, d, 0)
    product(2, 1)

    mine_r = al(z * zrows + yh * own_rows, own_rows)
    theirs_r = al(z * zrows + (1 - yh) * own_rows, own_rows)
    mine_o, theirs_o = al(yh * own_rows, own_rows), al((1 - yh) * own_rows, own_rows)

    def last_sum(t, u, r0, o0):
        value = part[t, pl.ds(r0, own_rows), pl.ds(u * cw, cw)]
        for d in range(2):
            value = value + rs_recv[t, u, d, steps - 1, pl.ds(o0, own_rows), :].astype(F32)
        return value

    def rs_finish(t, u):
        for d in range(2):
            rs_wait(t, u, d, steps - 1)
        if split(t, u):
            y_own[u, t] = last_sum(t, u, mine_r, 0)
            return
        m = t + u
        y_send[m] = last_sum(t, u, theirs_r, theirs_o).astype(BF16)
        y_own[u, t] = last_sum(t, u, mine_r, mine_o)
        if t == 2:
            part_of = pl.ds(0, 3) if u == 0 else pl.ds(3, 1)
            send(y_send.at[part_of], y_recv.at[part_of], ys_s.at[u], ys_r.at[u], y_dev)

    def rows_ref(r0, u):
        return act.at[:, pl.ds(r0, own_rows), pl.ds(u * cw, cw)]

    def activate(u):
        part_of = pl.ds(0, 3) if u == 0 else pl.ds(3, 1)
        arrived(y_recv.at[part_of], ys_s.at[u], ys_r.at[u], y_dev)
        for q in range(2):
            cs = pl.ds(q * half, half)
            gate, up, grad = (y_own[u, t, :, cs] for t in range(3))
            if u == 0:
                gate = gate + y_recv[0, :, cs].astype(F32)
                up = up + y_recv[1, :, cs].astype(F32)
            grad = grad + y_recv[2 + u, :, cs].astype(F32)
            sg = 1.0 / (1.0 + jnp.exp(-gate))
            co = pl.ds(u * cw + q * half, half)
            act[0, pl.ds(mine_r, own_rows), co] = (
                grad * up * sg * (1.0 + gate * (1.0 - sg))
            ).astype(BF16)
            act[1, pl.ds(mine_r, own_rows), co] = (grad * gate * sg).astype(BF16)
            act[2, pl.ds(mine_r, own_rows), co] = (gate * sg * up).astype(BF16)
        ref = rows_ref(mine_r, u)
        if u == 0:
            send(ref, ref, ay_s.at[0, steps], ay_r.at[0, steps], y_dev)
        else:
            for t in range(3):
                send(ref.at[t], ref.at[t], ya_s.at[t], ya_r.at[t], y_dev)

    def az_chunk(d, k, hops, hi):
        rs = pl.ds(al(z_rows(z - hops * (1 - 2 * d)) + hi * own_rows, own_rows), own_rows)
        cs = pl.ds(d * half, half) if k == steps - 1 else pl.ds(0, cw)
        return act.at[:, rs, cs]

    def az_step(k):
        for d in range(2):
            if k > 0:
                ref = az_chunk(d, k - 1, k, yh)
                arrived(ref, az_s.at[d, k - 1], az_r.at[d, k - 1], z_dev[d])
            if k < steps:
                out = az_chunk(d, k, k, yh)
                send(out, out, az_s.at[d, k], az_r.at[d, k], z_dev[d])
            if k > 0:
                send(ref, ref, ay_s.at[d, k - 1], ay_r.at[d, k - 1], y_dev)

    def ay_wait():
        arrived(rows_ref(theirs_r, 0), ay_s.at[0, steps], ay_r.at[0, steps], y_dev)
        for k in range(1, steps + 1):
            for d in range(2):
                ref = az_chunk(d, k - 1, k, 1 - yh)
                arrived(ref, ay_s.at[d, k - 1], ay_r.at[d, k - 1], y_dev)

    def ag_slice(t, d, k, chunk):
        if k == steps - 1:
            c = pl.ds(cw + d * half, half)
        else:
            c = pl.ds(cw, cw)
        return act.at[t, pl.ds(z_rows(chunk), zrows), c]

    def ag_step(t, k):
        for d in range(2):
            sign = 1 - 2 * d
            if k > 0:
                ref = ag_slice(t, d, k - 1, z - k * sign)
                arrived(ref, ag_s.at[t, d, k - 1], ag_r.at[t, d, k - 1], z_dev[d])
            if k < steps:
                ref = ag_slice(t, d, k, z - k * sign)
                send(ref, ref, ag_s.at[t, d, k], ag_r.at[t, d, k], z_dev[d])

    out_copies = []

    def write_out(src, dst, index):
        copy = pltpu.make_async_copy(src, dst, out_sem.at[index])
        copy.start()
        out_copies.append(copy)

    def wide_dense(t, u):
        dense = (dense_g, dense_u)[t]
        per = cw // (2 * BLK)

        def body(j, carry):
            value = dot(tok_t[...], act[t, :, pl.ds(al(u * cw + j * 2 * BLK, BLK), 2 * BLK)])
            low = lane_half(BLK) == 0
            for a in range(drb):
                for b in range(2):
                    both = value[a * BLK : (a + 1) * BLK, b * BLK : (b + 1) * BLK]
                    turned = swap(both)
                    c = 4 * (u * per + j) + 2 * b
                    dense[a * fcb + c] = jnp.where(low, both, turned)
                    dense[a * fcb + c + 1] = jnp.where(low, turned, both)
            return carry

        lax.fori_loop(0, per, body, 0)

    def emit_wide(i):
        dense = (dense_g, dense_u)[i]

        def body(s, carry):
            one = dense[slots_ref[i, s]]
            two = dense[slots_ref[i, s + cap // 2]]
            lanes = lane_half(HB)
            for h, value in enumerate((one, two)):
                keep = jnp.where(dp == 0, value[:HB], value[HB:])
                dp_own[i, h, s] = jnp.where(lanes == dp, keep, 0.0)
            give_one = jnp.where(dp == 0, one[HB:], one[:HB])
            give_two = jnp.where(dp == 0, two[HB:], two[:HB])
            dp_send[i, s] = jnp.where(lanes == 0, give_one, give_two).astype(BF16)
            return carry

        lax.fori_loop(0, cap // 2, body, 0)
        send(dp_send.at[i], recv_out.at[i], dp_s.at[i], dp_r.at[i], dp_dev)
        write_out(dp_own.at[i], own_out.at[i], i)

    def transpose_hidden(u):
        def body(j, carry):
            cs = pl.ds(al(u * cw + j * BLK, BLK), BLK)
            hid_t[cs, :] = act[2, :, cs].astype(F32).T.astype(BF16)
            return carry

        lax.fori_loop(0, cw // BLK, body, 0)

    def down_dense(u):
        per = cw // 256

        def body(j, carry):
            value = dot(hid_t[pl.ds(al(u * cw + j * 256, 256), 256), :], tcg[1])
            for a in range(4):
                for b in range(drb):
                    dense_d[(4 * (u * per + j) + a) * drb + b] = value[
                        a * HB : (a + 1) * HB, b * BLK : (b + 1) * BLK
                    ]
            return carry

        lax.fori_loop(0, per, body, 0)

    def emit_down():
        def body(s, carry):
            down_own[s] = dense_d[slots_ref[2, s]]
            return carry

        lax.fori_loop(0, cap, body, 0)
        write_out(down_own, down_out, 2)

    def col_products(j, parts, first):
        step = min(256, width)

        def body(q, carry):
            cs = pl.ds(al(q * step, step), step)
            value = None if first else col_part[j, :, cs]
            for mul, a, b in parts:
                term = mul(a(), b(cs))
                value = term if value is None else value + term
            col_part[j, :, cs] = value
            return carry

        lax.fori_loop(0, width // step, body, 0)

    def layer_product(u):
        us = pl.ds(u * cw, cw)
        col_products(0, [(dot, lambda: act[2, :, us], lambda cs: wd[us, cs])], u == 0)

    def grad_product(u):
        us = pl.ds(u * cw, cw)
        parts = [
            (dot_t, lambda: act[0, :, us], lambda cs: wg[cs, us]),
            (dot_t, lambda: act[1, :, us], lambda cs: wu[cs, us]),
        ]
        col_products(1, parts, u == 0)

    def col_rows(c):
        return pl.ds(al(c * pair, pair), pair)

    def col_first(j):
        for xx in range(nx):
            ca_send[j, xx] = col_part[j, col_rows(xx * 2 + 1 - core), :].astype(BF16)
        send(ca_send.at[j], ca_recv.at[j], ca_s.at[j], ca_r.at[j], sib)

    def pair_sum(j, xx):
        return col_part[j, col_rows(xx * 2 + core), :] + ca_recv[j, xx].astype(F32)

    def col_second(j):
        arrived(ca_recv.at[j], ca_s.at[j], ca_r.at[j], sib)
        for k in range(1, nx):
            cb_send[j, k - 1] = pair_sum(j, lax.rem(x + k, nx)).astype(BF16)
            send(cb_send.at[j, k - 1], cb_recv.at[j, k - 1], cb_s.at[j, k - 1], cb_r.at[j, k - 1], x_dev(k, dp))

    def col_third(j):
        value = pair_sum(j, x)
        for k in range(1, nx):
            arrived(cb_recv.at[j, k - 1], cb_s.at[j, k - 1], cb_r.at[j, k - 1], sib)
            value = value + cb_recv[j, k - 1].astype(F32)
        cc_sum[j] = value
        cc_send[j] = cc_sum[j, pl.ds(al((1 - dp) * n_tok, n_tok), n_tok), :].astype(BF16)
        send(cc_send.at[j], cc_recv.at[j], cc_s.at[j], cc_r.at[j], dp_dev)

    def col_last(j, out):
        arrived(cc_recv.at[j], cc_s.at[j], cc_r.at[j], dp_dev)
        value = cc_sum[j, pl.ds(al(dp * n_tok, n_tok), n_tok), :] + cc_recv[j].astype(F32)
        col_stage[j] = value.astype(BF16)
        write_out(col_stage.at[j], out, 3 + j)

    S = steps
    slots = {}

    def at(s, f, *a):
        slots.setdefault(s, []).append(functools.partial(f, *a))

    def y_arrived(t):
        arrived(rows_ref(theirs_r, 1).at[t], ya_s.at[t], ya_r.at[t], y_dev)

    def tok_transpose():
        tok_t[...] = tcg[0].astype(F32).T.astype(BF16)

    def start_last():
        for d in range(2):
            rs_start(2, 1, d, 0)

    for k in range(1, S):
        for t in range(3):
            at(k, rs_step, t, 0, k)
    at(S - 2, start_last)
    at(S - 2, tok_transpose)
    at(S - 1, rs_step, 2, 1, 1)
    at(S - 1, yb_add, 0)
    at(S - 1, yb_add, 1)
    for t in range(3):
        at(S, rs_finish, t, 0)
    for k in range(1, S):
        at(S - 1 + k, rs_step, 0, 1, k)
        at(S - 1 + k, rs_step, 1, 1, k)
    for k in range(2, S):
        at(S - 2 + k, rs_step, 2, 1, k)
    at(S + 1, activate, 0)
    at(2 * S - 2, rs_finish, 2, 1)
    at(2 * S - 1, rs_finish, 0, 1)
    at(2 * S - 1, rs_finish, 1, 1)
    at(2 * S - 1, activate, 1)
    for t in range(3):
        for k in range(S + 1):
            if k == 0:
                at(2 * S + t, y_arrived, t)
            at(2 * S + t + k, ag_step, t, k)
    for k in range(S + 1):
        at(S + 1 + k, az_step, k)
    A = 3 * S - 1
    at(A, ay_wait)
    at(A, wide_dense, 0, 0)
    at(A, wide_dense, 1, 0)
    at(A, grad_product, 0)
    A = 3 * S
    at(A, wide_dense, 0, 1)
    at(A, emit_wide, 0)
    at(A, layer_product, 0)
    at(A, transpose_hidden, 0)
    A = 3 * S + 1
    at(A, wide_dense, 1, 1)
    at(A, emit_wide, 1)
    at(A, grad_product, 1)
    at(A, col_first, 1)
    at(A, down_dense, 0)
    at(A, col_second, 1)
    A = 3 * S + 2
    at(A, layer_product, 1)
    at(A, col_first, 0)
    at(A, transpose_hidden, 1)
    at(A, col_second, 0)
    at(A, col_third, 1)
    at(A, down_dense, 1)
    at(A, emit_down)
    at(A, col_third, 0)
    at(A, col_last, 1, tgrad_out)
    at(A, col_last, 0, layer_out)
    for s in sorted(slots):
        for f in slots[s]:
            f()
    for i in range(2):
        arrived(recv_out.at[i], dp_s.at[i], dp_r.at[i], dp_dev)
    for c in out_copies:
        c.wait()
    for c in sends:
        c.wait_send()


def finish(layer, tgrad, own, recv, down, layer_o, tgrad_o, gate_o, up_o, down_o):
    dp = lax.axis_index("dp")
    layer_o[...] = layer[...]
    tgrad_o[...] = tgrad[...]
    down_o[...] = down[...]
    lanes = lane_half(HB)
    for i, out in enumerate((gate_o, up_o)):
        for s in range(recv.shape[1]):
            value = recv[i, s].astype(F32)
            turned = swap(value)
            for h in range(2):
                other = jnp.where(dp == 1 - h, value, turned)
                out[h, s] = jnp.where(lanes == dp, own[i, h, s], other)


def per_device(tokens, cotangent, gate_blocks, up_blocks, down_blocks, gate_slots, up_slots, down_slots):
    n_row, n_col = lax.axis_size("row"), lax.axis_size("col")
    n_tok, width = tokens.shape
    cap = gate_blocks.shape[2]
    hid = FF // n_col // 2
    nz, nx = n_row // 2, n_col // 2
    steps = nz // 2
    group = 2 * n_tok * n_col
    zrows = group // nz
    own_rows = zrows // 2
    cw = hid // UNITS
    drb, fcb = width // BLK, hid // HB
    pair = 2 * n_tok
    slots = jnp.concatenate([gate_slots[0], up_slots[0], down_slots[0]], axis=0)
    place = jnp.arange(drb * fcb, dtype=jnp.int32)
    order = jnp.arange(cap, dtype=jnp.int32)
    inv = jnp.min(
        jnp.where(slots[:, None, :] == place[None, :, None], order[None, None, :], cap), axis=2
    )
    slots = jnp.where(slots < 0, drb * fcb, slots)
    dims = (n_row, n_col, n_tok, width, hid, cap)
    smem = pl.BlockSpec(memory_space=pltpu.SMEM)
    anym = pl.BlockSpec(memory_space=pl.ANY)
    vm = pltpu.VMEM
    dma = pltpu.SemaphoreType.DMA
    scratch = [
        vm((3, cap + 1, BLK, BLK), BF16),
        vm((2, group, width), BF16),
        vm((width, hid), BF16),
        vm((width, hid), BF16),
        vm((hid, width), BF16),
        vm((3, group, hid), F32),
        vm((3, UNITS, 2, steps, zrows, cw), BF16),
        vm((3, UNITS, 2, steps, zrows, cw), BF16),
        vm((4, own_rows, cw), BF16),
        vm((4, own_rows, cw), BF16),
        vm((UNITS, 3, own_rows, cw), F32),
        vm((2, nz, own_rows, cw), BF16),
        vm((2, nz, own_rows, cw), BF16),
        vm((3, group, hid), BF16),
        vm((width, group), BF16),
        vm((hid, group), BF16),
        vm((drb * fcb + 1, BLK, BLK), F32),
        vm((drb * fcb + 1, BLK, BLK), F32),
        vm((drb * fcb + 1, HB, BLK), F32),
        vm((2, cap // 2, HB, BLK), BF16),
        vm((2, 2, cap // 2, HB, BLK), F32),
        vm((cap, HB, BLK), F32),
        vm((2, group, width), F32),
        vm((2, nx, pair, width), BF16),
        vm((2, nx, pair, width), BF16),
        vm((2, nx - 1, pair, width), BF16),
        vm((2, nx - 1, pair, width), BF16),
        vm((2, pair, width), F32),
        vm((2, n_tok, width), BF16),
        vm((2, n_tok, width), BF16),
        vm((2, n_tok, width), BF16),
        dma((5,)),
        dma((5,)),
        dma((2, 3 * nx - 1)),
        dma((2, 3 * nx - 1)),
        dma((3, UNITS, 2, steps)),
        dma((3, UNITS, 2, steps)),
        dma((2,)),
        dma((2,)),
        dma((2,)),
        dma((2,)),
        dma((3,)),
        dma((3,)),
        dma((2, steps)),
        dma((2, steps)),
        dma((2, steps + 1)),
        dma((2, steps + 1)),
        dma((3, 2, steps)),
        dma((3, 2, steps)),
        dma((2,)),
        dma((2,)),
        dma((2,)),
        dma((2,)),
        dma((2, nx - 1)),
        dma((2, nx - 1)),
        dma((2,)),
        dma((2,)),
    ]
    flops = 9 * 2 * group * width * hid
    inner = (
        jax.ShapeDtypeStruct((n_tok, width), BF16),
        jax.ShapeDtypeStruct((n_tok, width), BF16),
        jax.ShapeDtypeStruct((2, 2, cap // 2, HB, BLK), F32),
        jax.ShapeDtypeStruct((2, cap // 2, HB, BLK), BF16),
        jax.ShapeDtypeStruct((cap, HB, BLK), F32),
    )
    results = pl.pallas_call(
        functools.partial(kernel, dims),
        out_shape=inner,
        in_specs=[smem, smem, anym, anym, anym, anym, anym],
        out_specs=(anym,) * 5,
        scratch_shapes=scratch,
        compiler_params=pltpu.CompilerParams(
            collective_id=0, has_side_effects=True, vmem_limit_bytes=56 * 1024 * 1024
        ),
        cost_estimate=pl.CostEstimate(flops=flops, bytes_accessed=8 * 1024 * 1024, transcendentals=0),
        name="ffn",
    )(slots, inv, tokens, cotangent, gate_blocks[0, 0], up_blocks[0, 0], down_blocks[0, 0])
    ns = cap // 2 // GRID
    flat = pl.BlockSpec((n_tok, width), lambda g: (0, 0))
    wide = pl.BlockSpec((2, ns, HB, BLK), lambda g: (0, g, 0, 0))
    tall = pl.BlockSpec((2 * ns, HB, BLK), lambda g: (g, 0, 0))
    layer, tgrad, gate_grad, up_grad, down_grad = pl.pallas_call(
        finish,
        grid=(GRID,),
        out_shape=(
            inner[0],
            inner[1],
            jax.ShapeDtypeStruct((2, cap // 2, HB, BLK), F32),
            jax.ShapeDtypeStruct((2, cap // 2, HB, BLK), F32),
            inner[4],
        ),
        in_specs=[
            flat,
            flat,
            pl.BlockSpec((2, 2, ns, HB, BLK), lambda g: (0, 0, g, 0, 0)),
            wide,
            tall,
        ],
        out_specs=(flat, flat, wide, wide, tall),
        name="finish",
    )(*results)
    shape = (1, 1, cap, HB, BLK)
    return (layer, tgrad, gate_grad.reshape(shape), up_grad.reshape(shape), down_grad.reshape(shape))


def solution(mesh):
    in_specs = (
        P(("col", "dp"), "row"),
        P(("col", "dp"), "row"),
        P("row", "col", None, None, None),
        P("row", "col", None, None, None),
        P("col", "row", None, None, None),
        P("row", "col", None),
        P("row", "col", None),
        P("col", "row", None),
    )
    out_specs = (
        P(("col", "dp"), "row"),
        P(("col", "dp"), "row"),
        P("row", "col", None, "dp", None),
        P("row", "col", None, "dp", None),
        P("col", "row", None, "dp", None),
    )
    return jax.shard_map(
        per_device, mesh=mesh, in_specs=in_specs, out_specs=out_specs, check_vma=False
    )
```

```python
import functools

import jax
import jax.numpy as jnp
from jax import lax
from jax.experimental import pallas as pl
from jax.experimental.pallas import tpu as pltpu
from jax.sharding import PartitionSpec as P

FF = 16384
BLK = 128
HB = BLK // 2
UNITS = 2
GRID = 2
MESH = pl.DeviceIdType.MESH
F32 = jnp.float32
BF16 = jnp.bfloat16


def dot(a, b):
    return lax.dot_general(a, b, (((1,), (0,)), ((), ())), preferred_element_type=F32)


def dot_t(a, b):
    return lax.dot_general(a, b, (((1,), (1,)), ((), ())), preferred_element_type=F32)


def al(value, step):
    return pl.multiple_of(value, step)


def swap(value):
    return pltpu.roll(value, HB, 1)


def lane_half(rows):
    return (lax.broadcasted_iota(jnp.int32, (rows, BLK), 1) >= HB).astype(jnp.int32)


def kernel(
    dims,
    slots_ref,
    inv_ref,
    tok_in,
    cot_in,
    gate_in,
    up_in,
    down_in,
    layer_out,
    tgrad_out,
    own_out,
    recv_out,
    down_out,
    blocks,
    tcg,
    wg,
    wu,
    wd,
    part,
    rs_send,
    rs_recv,
    y_send,
    y_recv,
    y_own,
    yb_send,
    yb_recv,
    act,
    tok_t,
    hid_t,
    dense_g,
    dense_u,
    dense_d,
    dp_send,
    dp_own,
    down_own,
    col_part,
    ca_send,
    ca_recv,
    cb_send,
    cb_recv,
    cc_sum,
    cc_send,
    cc_recv,
    col_stage,
    loc_sem,
    out_sem,
    p1_s,
    p1_r,
    rs_s,
    rs_r,
    ys_s,
    ys_r,
    yb_s,
    yb_r,
    ya_s,
    ya_r,
    az_s,
    az_r,
    ay_s,
    ay_r,
    ag_s,
    ag_r,
    dp_s,
    dp_r,
    ca_s,
    ca_r,
    cb_s,
    cb_r,
    cc_s,
    cc_r,
):
    n_row, n_col, n_tok, width, hid, cap = dims
    nz, nx = n_row // 2, n_col // 2
    steps = nz // 2
    group = 2 * n_tok * n_col
    zrows = group // nz
    own_rows = zrows // 2
    cw = hid // UNITS
    half = cw // 2
    drb, fcb = width // BLK, hid // HB
    pair = 2 * n_tok

    row, col, dp = lax.axis_index("row"), lax.axis_index("col"), lax.axis_index("dp")
    z, yh = lax.div(row, 2), lax.rem(row, 2)
    x, core = lax.div(col, 2), lax.rem(col, 2)
    z_right = (lax.rem(z + 1, nz) * 2 + yh, col, dp)
    z_left = (lax.rem(z + nz - 1, nz) * 2 + yh, col, dp)
    z_dev = (z_right, z_left)
    y_dev = (z * 2 + 1 - yh, col, dp)
    sib = (row, x * 2 + 1 - core, dp)
    dp_dev = (row, col, 1 - dp)

    def x_dev(k, d):
        return (row, lax.rem(x + k, nx) * 2 + core, d)

    sends = []

    def send(src, dst, s_sem, r_sem, dev):
        copy = pltpu.make_async_remote_copy(
            src_ref=src, dst_ref=dst, send_sem=s_sem, recv_sem=r_sem, device_id=dev, device_id_type=MESH
        )
        copy.start()
        sends.append(copy)

    def arrived(dst, s_sem, r_sem, dev):
        pltpu.make_async_remote_copy(
            src_ref=dst, dst_ref=dst, send_sem=s_sem, recv_sem=r_sem, device_id=dev, device_id_type=MESH
        ).wait_recv()

    mine = pl.ds(al((col * 2 + dp) * n_tok, n_tok), n_tok)
    own_loads = [
        pltpu.make_async_copy(ref, tcg.at[j, mine, :], loc_sem.at[j])
        for j, ref in enumerate((tok_in, cot_in))
    ]
    block_loads = [
        pltpu.make_async_copy(ref, blocks.at[i, pl.ds(0, cap)], loc_sem.at[2 + i])
        for i, ref in enumerate((gate_in, up_in, down_in))
    ]
    for c in own_loads + block_loads:
        c.start()

    barrier = pltpu.get_barrier_semaphore()
    peers = [z_right, z_left, y_dev, sib, dp_dev] + [
        x_dev(k, d) for k in range(1, nx) for d in (dp, 1 - dp)
    ]
    for dev in peers:
        pl.semaphore_signal(barrier, inc=1, device_id=dev, device_id_type=MESH)
    pl.semaphore_wait(barrier, len(peers))

    def rows_of(j, index, n):
        return tcg.at[j, pl.ds(al(index * n_tok, n_tok), n * n_tok), :]

    def source(k, c):
        return (lax.rem(x + nx - k, nx) * 2 + c) * 2

    def give(j, ref, s, dev):
        send(ref, ref, p1_s.at[j, s], p1_r.at[j, s], dev)

    def take(j, ref, s):
        arrived(ref, p1_s.at[j, s], p1_r.at[j, s], sib)

    def gather_start(j):
        own_loads[j].wait()
        own = rows_of(j, source(0, core) + dp, 1)
        for k in range(1, nx):
            give(j, own, k, x_dev(k, dp))
            give(j, own, nx + k, x_dev(k, 1 - dp))
        give(j, own, nx, dp_dev)

    def gather_pass(j):
        for k in range(nx):
            if k > 0:
                take(j, rows_of(j, source(k, core) + dp, 1), k)
            take(j, rows_of(j, source(k, core) + 1 - dp, 1), nx + k)
            give(j, rows_of(j, source(k, core), 2), 2 * nx + k - 1 if k else 0, sib)

    def gather_end(j):
        for k in range(nx):
            take(j, rows_of(j, source(k, 1 - core), 2), 2 * nx + k - 1 if k else 0)

    gather_start(0)
    gather_start(1)

    for c in block_loads:
        c.wait()
    for i in range(3):
        blocks[i, cap] = jnp.zeros((BLK, BLK), BF16)
    for ref in (dense_g, dense_u, dense_d):
        ref[drb * fcb] = jnp.zeros(ref.shape[1:], F32)

    def place_wide(p, carry):
        r, c = p // (fcb // 2), p % (fcb // 2)
        keep = lane_half(BLK) == dp
        for i, w in enumerate((wg, wu)):
            even = blocks[i, inv_ref[i, 2 * p]].astype(F32)
            odd = blocks[i, inv_ref[i, 2 * p + 1]].astype(F32)
            stay = jnp.where(dp == 0, even, odd)
            move = swap(jnp.where(dp == 0, odd, even))
            w[pl.ds(al(r * BLK, BLK), BLK), pl.ds(al(c * BLK, BLK), BLK)] = jnp.where(
                keep, stay, move
            ).astype(BF16)
        return carry

    def place_down(p, carry):
        value = blocks[2, inv_ref[2, p]]
        r, c = p // drb, p % drb
        wd[pl.ds(al(r * HB, HB), HB), pl.ds(al(c * BLK, BLK), BLK)] = jnp.where(
            dp == 0, value[:HB], value[HB:]
        )
        return carry

    lax.fori_loop(0, drb * fcb // 2, place_wide, 0)
    lax.fori_loop(0, drb * fcb, place_down, 0)
    gather_pass(0)
    gather_end(0)

    def z_rows(t):
        return al(lax.rem(t + 2 * nz, nz) * zrows, zrows)

    def split(t, u):
        return u == 1 and t < 2

    def unit_rows(t, u, target):
        if not split(t, u):
            return z_rows(target)
        return al(z_rows(target) + yh * own_rows, own_rows)

    def count(t, u):
        return own_rows if split(t, u) else zrows

    def rs_ref(buf, t, u, d, k):
        cs = pl.ds(d * half, half) if k == 0 else pl.ds(0, cw)
        return buf.at[t, u, d, k, pl.ds(0, count(t, u)), cs]

    def rs_start(t, u, d, k):
        target = z + (steps - k) * (1 - 2 * d)
        rs = pl.ds(unit_rows(t, u, target), count(t, u))
        to = pl.ds(0, count(t, u))
        for h in range(2):
            if k == 0 and h != d:
                continue
            hc = pl.ds(h * half, half)
            value = part[t, rs, pl.ds(u * cw + h * half, half)]
            if k > 1 or (k == 1 and h == d):
                value = value + rs_recv[t, u, d, k - 1, to, hc].astype(F32)
            rs_send[t, u, d, k, to, hc] = value.astype(BF16)
        send(
            rs_ref(rs_send, t, u, d, k),
            rs_ref(rs_recv, t, u, d, k),
            rs_s.at[t, u, d, k],
            rs_r.at[t, u, d, k],
            z_dev[d],
        )

    def rs_wait(t, u, d, k):
        arrived(rs_ref(rs_recv, t, u, d, k), rs_s.at[t, u, d, k], rs_r.at[t, u, d, k], z_dev[d])

    def rs_step(t, u, k):
        for d in range(2):
            rs_wait(t, u, d, k - 1)
            rs_start(t, u, d, k)

    def yb_start(t):
        for c in range(nz):
            r0 = al(c * zrows + (1 - yh) * own_rows, own_rows)
            yb_send[t, c] = part[t, pl.ds(r0, own_rows), pl.ds(cw, cw)].astype(BF16)
        send(yb_send.at[t], yb_recv.at[t], yb_s.at[t], yb_r.at[t], y_dev)

    def yb_add(t):
        arrived(yb_recv.at[t], yb_s.at[t], yb_r.at[t], y_dev)
        for c in range(nz):
            rs = pl.ds(al(c * zrows + yh * own_rows, own_rows), own_rows)
            part[t, rs, pl.ds(cw, cw)] = part[t, rs, pl.ds(cw, cw)] + yb_recv[t, c].astype(F32)
        for d in range(2):
            rs_start(t, 1, d, 0)

    tile = min(256, cw)

    def product(t, u):
        def body(j, carry):
            cs = pl.ds(al(u * cw + j * tile, tile), tile)
            if t == 2:
                part[t, :, cs] = dot_t(tcg[1], wd[cs, :])
            else:
                part[t, :, cs] = dot(tcg[0], (wg, wu)[t][:, cs])
            return carry

        lax.fori_loop(0, cw // tile, body, 0)

    for t in range(2):
        product(t, 0)
        for d in range(2):
            rs_start(t, 0, d, 0)
        product(t, 1)
        yb_start(t)
        if t == 0:
            gather_pass(1)
    gather_end(1)
    product(2, 0)
    for d in range(2):
        rs_start(2, 0, d, 0)
    product(2, 1)

    mine_r = al(z * zrows + yh * own_rows, own_rows)
    theirs_r = al(z * zrows + (1 - yh) * own_rows, own_rows)
    mine_o, theirs_o = al(yh * own_rows, own_rows), al((1 - yh) * own_rows, own_rows)

    def last_sum(t, u, r0, o0):
        value = part[t, pl.ds(r0, own_rows), pl.ds(u * cw, cw)]
        for d in range(2):
            value = value + rs_recv[t, u, d, steps - 1, pl.ds(o0, own_rows), :].astype(F32)
        return value

    def rs_finish(t, u):
        for d in range(2):
            rs_wait(t, u, d, steps - 1)
        if split(t, u):
            y_own[u, t] = last_sum(t, u, mine_r, 0)
            return
        m = t + u
        y_send[m] = last_sum(t, u, theirs_r, theirs_o).astype(BF16)
        y_own[u, t] = last_sum(t, u, mine_r, mine_o)
        if t == 2:
            part_of = pl.ds(0, 3) if u == 0 else pl.ds(3, 1)
            send(y_send.at[part_of], y_recv.at[part_of], ys_s.at[u], ys_r.at[u], y_dev)

    def rows_ref(r0, u):
        return act.at[:, pl.ds(r0, own_rows), pl.ds(u * cw, cw)]

    def activate(u):
        part_of = pl.ds(0, 3) if u == 0 else pl.ds(3, 1)
        arrived(y_recv.at[part_of], ys_s.at[u], ys_r.at[u], y_dev)
        for q in range(2):
            cs = pl.ds(q * half, half)
            gate, up, grad = (y_own[u, t, :, cs] for t in range(3))
            if u == 0:
                gate = gate + y_recv[0, :, cs].astype(F32)
                up = up + y_recv[1, :, cs].astype(F32)
            grad = grad + y_recv[2 + u, :, cs].astype(F32)
            sg = 1.0 / (1.0 + jnp.exp(-gate))
            co = pl.ds(u * cw + q * half, half)
            act[0, pl.ds(mine_r, own_rows), co] = (
                grad * up * sg * (1.0 + gate * (1.0 - sg))
            ).astype(BF16)
            act[1, pl.ds(mine_r, own_rows), co] = (grad * gate * sg).astype(BF16)
            act[2, pl.ds(mine_r, own_rows), co] = (gate * sg * up).astype(BF16)
        ref = rows_ref(mine_r, u)
        if u == 0:
            send(ref, ref, ay_s.at[0, steps], ay_r.at[0, steps], y_dev)
        else:
            for t in range(3):
                send(ref.at[t], ref.at[t], ya_s.at[t], ya_r.at[t], y_dev)

    def az_chunk(d, k, hops, hi):
        rs = pl.ds(al(z_rows(z - hops * (1 - 2 * d)) + hi * own_rows, own_rows), own_rows)
        cs = pl.ds(d * half, half) if k == steps - 1 else pl.ds(0, cw)
        return act.at[:, rs, cs]

    def az_step(k):
        for d in range(2):
            if k > 0:
                ref = az_chunk(d, k - 1, k, yh)
                arrived(ref, az_s.at[d, k - 1], az_r.at[d, k - 1], z_dev[d])
            if k < steps:
                out = az_chunk(d, k, k, yh)
                send(out, out, az_s.at[d, k], az_r.at[d, k], z_dev[d])
            if k > 0:
                send(ref, ref, ay_s.at[d, k - 1], ay_r.at[d, k - 1], y_dev)

    def ay_wait():
        arrived(rows_ref(theirs_r, 0), ay_s.at[0, steps], ay_r.at[0, steps], y_dev)
        for k in range(1, steps + 1):
            for d in range(2):
                ref = az_chunk(d, k - 1, k, 1 - yh)
                arrived(ref, ay_s.at[d, k - 1], ay_r.at[d, k - 1], y_dev)

    def ag_slice(t, d, k, chunk):
        if k == steps - 1:
            c = pl.ds(cw + d * half, half)
        else:
            c = pl.ds(cw, cw)
        return act.at[t, pl.ds(z_rows(chunk), zrows), c]

    def ag_step(t, k):
        for d in range(2):
            sign = 1 - 2 * d
            if k > 0:
                ref = ag_slice(t, d, k - 1, z - k * sign)
                arrived(ref, ag_s.at[t, d, k - 1], ag_r.at[t, d, k - 1], z_dev[d])
            if k < steps:
                ref = ag_slice(t, d, k, z - k * sign)
                send(ref, ref, ag_s.at[t, d, k], ag_r.at[t, d, k], z_dev[d])

    out_copies = []

    def write_out(src, dst, index):
        copy = pltpu.make_async_copy(src, dst, out_sem.at[index])
        copy.start()
        out_copies.append(copy)

    def wide_dense(t, u):
        dense = (dense_g, dense_u)[t]
        per = cw // (2 * BLK)

        def body(j, carry):
            value = dot(tok_t[...], act[t, :, pl.ds(al(u * cw + j * 2 * BLK, BLK), 2 * BLK)])
            low = lane_half(BLK) == 0
            for a in range(drb):
                for b in range(2):
                    both = value[a * BLK : (a + 1) * BLK, b * BLK : (b + 1) * BLK]
                    turned = swap(both)
                    c = 4 * (u * per + j) + 2 * b
                    dense[a * fcb + c] = jnp.where(low, both, turned)
                    dense[a * fcb + c + 1] = jnp.where(low, turned, both)
            return carry

        lax.fori_loop(0, per, body, 0)

    def emit_wide(i):
        dense = (dense_g, dense_u)[i]

        def body(s, carry):
            one = dense[slots_ref[i, s]]
            two = dense[slots_ref[i, s + cap // 2]]
            lanes = lane_half(HB)
            for h, value in enumerate((one, two)):
                keep = jnp.where(dp == 0, value[:HB], value[HB:])
                dp_own[i, h, s] = jnp.where(lanes == dp, keep, 0.0)
            give_one = jnp.where(dp == 0, one[HB:], one[:HB])
            give_two = jnp.where(dp == 0, two[HB:], two[:HB])
            dp_send[i, s] = jnp.where(lanes == 0, give_one, give_two).astype(BF16)
            return carry

        lax.fori_loop(0, cap // 2, body, 0)
        send(dp_send.at[i], recv_out.at[i], dp_s.at[i], dp_r.at[i], dp_dev)
        write_out(dp_own.at[i], own_out.at[i], i)

    def transpose_hidden(u):
        def body(j, carry):
            cs = pl.ds(al(u * cw + j * BLK, BLK), BLK)
            hid_t[cs, :] = act[2, :, cs].astype(F32).T.astype(BF16)
            return carry

        lax.fori_loop(0, cw // BLK, body, 0)

    def down_dense(u):
        per = cw // 256

        def body(j, carry):
            value = dot(hid_t[pl.ds(al(u * cw + j * 256, 256), 256), :], tcg[1])
            for a in range(4):
                for b in range(drb):
                    dense_d[(4 * (u * per + j) + a) * drb + b] = value[
                        a * HB : (a + 1) * HB, b * BLK : (b + 1) * BLK
                    ]
            return carry

        lax.fori_loop(0, per, body, 0)

    def emit_down():
        def body(s, carry):
            down_own[s] = dense_d[slots_ref[2, s]]
            return carry

        lax.fori_loop(0, cap, body, 0)
        write_out(down_own, down_out, 2)

    def col_products(j, parts, first):
        step = min(256, width)

        def body(q, carry):
            cs = pl.ds(al(q * step, step), step)
            value = None if first else col_part[j, :, cs]
            for mul, a, b in parts:
                term = mul(a(), b(cs))
                value = term if value is None else value + term
            col_part[j, :, cs] = value
            return carry

        lax.fori_loop(0, width // step, body, 0)

    def layer_product(u):
        us = pl.ds(u * cw, cw)
        col_products(0, [(dot, lambda: act[2, :, us], lambda cs: wd[us, cs])], u == 0)

    def grad_product(u):
        us = pl.ds(u * cw, cw)
        parts = [
            (dot_t, lambda: act[0, :, us], lambda cs: wg[cs, us]),
            (dot_t, lambda: act[1, :, us], lambda cs: wu[cs, us]),
        ]
        col_products(1, parts, u == 0)

    def col_rows(c):
        return pl.ds(al(c * pair, pair), pair)

    def col_first(j):
        for xx in range(nx):
            ca_send[j, xx] = col_part[j, col_rows(xx * 2 + 1 - core), :].astype(BF16)
        send(ca_send.at[j], ca_recv.at[j], ca_s.at[j], ca_r.at[j], sib)

    def pair_sum(j, xx):
        return col_part[j, col_rows(xx * 2 + core), :] + ca_recv[j, xx].astype(F32)

    def col_second(j):
        arrived(ca_recv.at[j], ca_s.at[j], ca_r.at[j], sib)
        for k in range(1, nx):
            cb_send[j, k - 1] = pair_sum(j, lax.rem(x + k, nx)).astype(BF16)
            send(cb_send.at[j, k - 1], cb_recv.at[j, k - 1], cb_s.at[j, k - 1], cb_r.at[j, k - 1], x_dev(k, dp))

    def col_third(j):
        value = pair_sum(j, x)
        for k in range(1, nx):
            arrived(cb_recv.at[j, k - 1], cb_s.at[j, k - 1], cb_r.at[j, k - 1], sib)
            value = value + cb_recv[j, k - 1].astype(F32)
        cc_sum[j] = value
        cc_send[j] = cc_sum[j, pl.ds(al((1 - dp) * n_tok, n_tok), n_tok), :].astype(BF16)
        send(cc_send.at[j], cc_recv.at[j], cc_s.at[j], cc_r.at[j], dp_dev)

    def col_last(j, out):
        arrived(cc_recv.at[j], cc_s.at[j], cc_r.at[j], dp_dev)
        value = cc_sum[j, pl.ds(al(dp * n_tok, n_tok), n_tok), :] + cc_recv[j].astype(F32)
        col_stage[j] = value.astype(BF16)
        write_out(col_stage.at[j], out, 3 + j)

    S = steps
    slots = {}

    def at(s, f, *a):
        slots.setdefault(s, []).append(functools.partial(f, *a))

    def y_arrived(t):
        arrived(rows_ref(theirs_r, 1).at[t], ya_s.at[t], ya_r.at[t], y_dev)

    def tok_transpose():
        tok_t[...] = tcg[0].astype(F32).T.astype(BF16)

    def start_last():
        for d in range(2):
            rs_start(2, 1, d, 0)

    for k in range(1, S):
        for t in range(3):
            at(k, rs_step, t, 0, k)
    at(S - 2, start_last)
    at(S - 2, tok_transpose)
    at(S - 1, rs_step, 2, 1, 1)
    at(S - 1, yb_add, 0)
    at(S - 1, yb_add, 1)
    for t in range(3):
        at(S, rs_finish, t, 0)
    for k in range(1, S):
        at(S - 1 + k, rs_step, 0, 1, k)
        at(S - 1 + k, rs_step, 1, 1, k)
    for k in range(2, S):
        at(S - 2 + k, rs_step, 2, 1, k)
    at(S + 1, activate, 0)
    at(2 * S - 2, rs_finish, 2, 1)
    at(2 * S - 1, rs_finish, 0, 1)
    at(2 * S - 1, rs_finish, 1, 1)
    at(2 * S - 1, activate, 1)
    for t in range(3):
        lag = 2 * S + (t == 2)
        at(lag, y_arrived, t)
        for k in range(S + 1):
            at(lag + k, ag_step, t, k)
    for k in range(S + 1):
        at(S + 1 + k, az_step, k)
    A = 3 * S - 1
    at(A, ay_wait)
    at(A, wide_dense, 0, 0)
    at(A, wide_dense, 1, 0)
    at(A, grad_product, 0)
    A = 3 * S
    at(A, wide_dense, 0, 1)
    at(A, emit_wide, 0)
    at(A, wide_dense, 1, 1)
    at(A, emit_wide, 1)
    at(A, grad_product, 1)
    at(A, col_first, 1)
    at(A, layer_product, 0)
    at(A, col_second, 1)
    A = 3 * S + 1
    at(A, layer_product, 1)
    at(A, col_first, 0)
    at(A, transpose_hidden, 0)
    at(A, transpose_hidden, 1)
    at(A, col_second, 0)
    at(A, col_third, 1)
    at(A, down_dense, 0)
    at(A, down_dense, 1)
    at(A, emit_down)
    at(A, col_third, 0)
    at(A, col_last, 1, tgrad_out)
    at(A, col_last, 0, layer_out)
    for s in sorted(slots):
        for f in slots[s]:
            f()
    for i in range(2):
        arrived(recv_out.at[i], dp_s.at[i], dp_r.at[i], dp_dev)
    for c in out_copies:
        c.wait()
    for c in sends:
        c.wait_send()


def finish(layer, tgrad, own, recv, down, layer_o, tgrad_o, gate_o, up_o, down_o):
    dp = lax.axis_index("dp")
    layer_o[...] = layer[...]
    tgrad_o[...] = tgrad[...]
    down_o[...] = down[...]
    lanes = lane_half(HB)
    for i, out in enumerate((gate_o, up_o)):
        for s in range(recv.shape[1]):
            value = recv[i, s].astype(F32)
            turned = swap(value)
            for h in range(2):
                other = jnp.where(dp == 1 - h, value, turned)
                out[h, s] = jnp.where(lanes == dp, own[i, h, s], other)


def per_device(tokens, cotangent, gate_blocks, up_blocks, down_blocks, gate_slots, up_slots, down_slots):
    n_row, n_col = lax.axis_size("row"), lax.axis_size("col")
    n_tok, width = tokens.shape
    cap = gate_blocks.shape[2]
    hid = FF // n_col // 2
    nz, nx = n_row // 2, n_col // 2
    steps = nz // 2
    group = 2 * n_tok * n_col
    zrows = group // nz
    own_rows = zrows // 2
    cw = hid // UNITS
    drb, fcb = width // BLK, hid // HB
    pair = 2 * n_tok
    slots = jnp.concatenate([gate_slots[0], up_slots[0], down_slots[0]], axis=0)
    place = jnp.arange(drb * fcb, dtype=jnp.int32)
    order = jnp.arange(cap, dtype=jnp.int32)
    inv = jnp.min(
        jnp.where(slots[:, None, :] == place[None, :, None], order[None, None, :], cap), axis=2
    )
    slots = jnp.where(slots < 0, drb * fcb, slots)
    dims = (n_row, n_col, n_tok, width, hid, cap)
    smem = pl.BlockSpec(memory_space=pltpu.SMEM)
    anym = pl.BlockSpec(memory_space=pl.ANY)
    vm = pltpu.VMEM
    dma = pltpu.SemaphoreType.DMA
    scratch = [
        vm((3, cap + 1, BLK, BLK), BF16),
        vm((2, group, width), BF16),
        vm((width, hid), BF16),
        vm((width, hid), BF16),
        vm((hid, width), BF16),
        vm((3, group, hid), F32),
        vm((3, UNITS, 2, steps, zrows, cw), BF16),
        vm((3, UNITS, 2, steps, zrows, cw), BF16),
        vm((4, own_rows, cw), BF16),
        vm((4, own_rows, cw), BF16),
        vm((UNITS, 3, own_rows, cw), F32),
        vm((2, nz, own_rows, cw), BF16),
        vm((2, nz, own_rows, cw), BF16),
        vm((3, group, hid), BF16),
        vm((width, group), BF16),
        vm((hid, group), BF16),
        vm((drb * fcb + 1, BLK, BLK), F32),
        vm((drb * fcb + 1, BLK, BLK), F32),
        vm((drb * fcb + 1, HB, BLK), F32),
        vm((2, cap // 2, HB, BLK), BF16),
        vm((2, 2, cap // 2, HB, BLK), F32),
        vm((cap, HB, BLK), F32),
        vm((2, group, width), F32),
        vm((2, nx, pair, width), BF16),
        vm((2, nx, pair, width), BF16),
        vm((2, nx - 1, pair, width), BF16),
        vm((2, nx - 1, pair, width), BF16),
        vm((2, pair, width), F32),
        vm((2, n_tok, width), BF16),
        vm((2, n_tok, width), BF16),
        vm((2, n_tok, width), BF16),
        dma((5,)),
        dma((5,)),
        dma((2, 3 * nx - 1)),
        dma((2, 3 * nx - 1)),
        dma((3, UNITS, 2, steps)),
        dma((3, UNITS, 2, steps)),
        dma((2,)),
        dma((2,)),
        dma((2,)),
        dma((2,)),
        dma((3,)),
        dma((3,)),
        dma((2, steps)),
        dma((2, steps)),
        dma((2, steps + 1)),
        dma((2, steps + 1)),
        dma((3, 2, steps)),
        dma((3, 2, steps)),
        dma((2,)),
        dma((2,)),
        dma((2,)),
        dma((2,)),
        dma((2, nx - 1)),
        dma((2, nx - 1)),
        dma((2,)),
        dma((2,)),
    ]
    flops = 9 * 2 * group * width * hid
    inner = (
        jax.ShapeDtypeStruct((n_tok, width), BF16),
        jax.ShapeDtypeStruct((n_tok, width), BF16),
        jax.ShapeDtypeStruct((2, 2, cap // 2, HB, BLK), F32),
        jax.ShapeDtypeStruct((2, cap // 2, HB, BLK), BF16),
        jax.ShapeDtypeStruct((cap, HB, BLK), F32),
    )
    results = pl.pallas_call(
        functools.partial(kernel, dims),
        out_shape=inner,
        in_specs=[smem, smem, anym, anym, anym, anym, anym],
        out_specs=(anym,) * 5,
        scratch_shapes=scratch,
        compiler_params=pltpu.CompilerParams(
            collective_id=0, has_side_effects=True, vmem_limit_bytes=56 * 1024 * 1024
        ),
        cost_estimate=pl.CostEstimate(flops=flops, bytes_accessed=8 * 1024 * 1024, transcendentals=0),
        name="ffn",
    )(slots, inv, tokens, cotangent, gate_blocks[0, 0], up_blocks[0, 0], down_blocks[0, 0])
    ns = cap // 2 // GRID
    flat = pl.BlockSpec((n_tok, width), lambda g: (0, 0))
    wide = pl.BlockSpec((2, ns, HB, BLK), lambda g: (0, g, 0, 0))
    tall = pl.BlockSpec((2 * ns, HB, BLK), lambda g: (g, 0, 0))
    layer, tgrad, gate_grad, up_grad, down_grad = pl.pallas_call(
        finish,
        grid=(GRID,),
        out_shape=(
            inner[0],
            inner[1],
            jax.ShapeDtypeStruct((2, cap // 2, HB, BLK), F32),
            jax.ShapeDtypeStruct((2, cap // 2, HB, BLK), F32),
            inner[4],
        ),
        in_specs=[
            flat,
            flat,
            pl.BlockSpec((2, 2, ns, HB, BLK), lambda g: (0, 0, g, 0, 0)),
            wide,
            tall,
        ],
        out_specs=(flat, flat, wide, wide, tall),
        name="finish",
    )(*results)
    shape = (1, 1, cap, HB, BLK)
    return (layer, tgrad, gate_grad.reshape(shape), up_grad.reshape(shape), down_grad.reshape(shape))


def solution(mesh):
    in_specs = (
        P(("col", "dp"), "row"),
        P(("col", "dp"), "row"),
        P("row", "col", None, None, None),
        P("row", "col", None, None, None),
        P("col", "row", None, None, None),
        P("row", "col", None),
        P("row", "col", None),
        P("col", "row", None),
    )
    out_specs = (
        P(("col", "dp"), "row"),
        P(("col", "dp"), "row"),
        P("row", "col", None, "dp", None),
        P("row", "col", None, "dp", None),
        P("col", "row", None, "dp", None),
    )
    return jax.shard_map(
        per_device, mesh=mesh, in_specs=in_specs, out_specs=out_specs, check_vma=False
    )
```

```python
import functools

import jax
import jax.numpy as jnp
from jax import lax
from jax.experimental import pallas as pl
from jax.experimental.pallas import tpu as pltpu
from jax.sharding import PartitionSpec as P

FF = 16384
BLK = 128
HB = BLK // 2
UNITS = 2
GRID = 2
MESH = pl.DeviceIdType.MESH
F32 = jnp.float32
BF16 = jnp.bfloat16


def dot(a, b):
    return lax.dot_general(a, b, (((1,), (0,)), ((), ())), preferred_element_type=F32)


def dot_t(a, b):
    return lax.dot_general(a, b, (((1,), (1,)), ((), ())), preferred_element_type=F32)


def al(value, step):
    return pl.multiple_of(value, step)


def swap(value):
    return pltpu.roll(value, HB, 1)


def lane_half(rows):
    return (lax.broadcasted_iota(jnp.int32, (rows, BLK), 1) >= HB).astype(jnp.int32)


def kernel(
    dims,
    gate_slots,
    up_slots,
    down_slots,
    inv_ref,
    tok_in,
    cot_in,
    gate_in,
    up_in,
    down_in,
    layer_out,
    tgrad_out,
    own_out,
    recv_out,
    down_out,
    blocks,
    tcg,
    wg,
    wu,
    wd,
    part,
    rs_send,
    rs_recv,
    y_send,
    y_recv,
    y_own,
    yb_send,
    yb_recv,
    act,
    tok_t,
    hid_t,
    dense_g,
    dense_u,
    dense_d,
    dp_send,
    dp_own,
    down_own,
    col_part,
    ca_send,
    ca_recv,
    cb_send,
    cb_recv,
    cc_sum,
    cc_send,
    cc_recv,
    col_stage,
    loc_sem,
    out_sem,
    p1_s,
    p1_r,
    rs_s,
    rs_r,
    ys_s,
    ys_r,
    yb_s,
    yb_r,
    ya_s,
    ya_r,
    az_s,
    az_r,
    ay_s,
    ay_r,
    ag_s,
    ag_r,
    dp_s,
    dp_r,
    ca_s,
    ca_r,
    cb_s,
    cb_r,
    cc_s,
    cc_r,
):
    n_row, n_col, n_tok, width, hid, cap = dims
    nz, nx = n_row // 2, n_col // 2
    steps = nz // 2
    group = 2 * n_tok * n_col
    zrows = group // nz
    own_rows = zrows // 2
    cw = hid // UNITS
    half = cw // 2
    drb, fcb = width // BLK, hid // HB
    pair = 2 * n_tok

    row, col, dp = lax.axis_index("row"), lax.axis_index("col"), lax.axis_index("dp")
    z, yh = lax.div(row, 2), lax.rem(row, 2)
    x, core = lax.div(col, 2), lax.rem(col, 2)
    z_right = (lax.rem(z + 1, nz) * 2 + yh, col, dp)
    z_left = (lax.rem(z + nz - 1, nz) * 2 + yh, col, dp)
    z_dev = (z_right, z_left)
    y_dev = (z * 2 + 1 - yh, col, dp)
    sib = (row, x * 2 + 1 - core, dp)
    dp_dev = (row, col, 1 - dp)

    def x_dev(k, d):
        return (row, lax.rem(x + k, nx) * 2 + core, d)

    sends = []

    def send(src, dst, s_sem, r_sem, dev):
        copy = pltpu.make_async_remote_copy(
            src_ref=src, dst_ref=dst, send_sem=s_sem, recv_sem=r_sem, device_id=dev, device_id_type=MESH
        )
        copy.start()
        sends.append(copy)

    def arrived(dst, s_sem, r_sem, dev):
        pltpu.make_async_remote_copy(
            src_ref=dst, dst_ref=dst, send_sem=s_sem, recv_sem=r_sem, device_id=dev, device_id_type=MESH
        ).wait_recv()

    mine = pl.ds(al((col * 2 + dp) * n_tok, n_tok), n_tok)
    own_loads = [
        pltpu.make_async_copy(ref, tcg.at[j, mine, :], loc_sem.at[j])
        for j, ref in enumerate((tok_in, cot_in))
    ]
    block_loads = [
        pltpu.make_async_copy(ref, blocks.at[i, pl.ds(0, cap)], loc_sem.at[2 + i])
        for i, ref in enumerate((gate_in, up_in, down_in))
    ]
    for c in own_loads + block_loads:
        c.start()

    barrier = pltpu.get_barrier_semaphore()
    peers = [z_right, z_left, y_dev, sib, dp_dev] + [
        x_dev(k, d) for k in range(1, nx) for d in (dp, 1 - dp)
    ]
    for dev in peers:
        pl.semaphore_signal(barrier, inc=1, device_id=dev, device_id_type=MESH)
    pl.semaphore_wait(barrier, len(peers))

    def rows_of(j, index, n):
        return tcg.at[j, pl.ds(al(index * n_tok, n_tok), n * n_tok), :]

    def source(k, c):
        return (lax.rem(x + nx - k, nx) * 2 + c) * 2

    def give(j, ref, s, dev):
        send(ref, ref, p1_s.at[j, s], p1_r.at[j, s], dev)

    def take(j, ref, s):
        arrived(ref, p1_s.at[j, s], p1_r.at[j, s], sib)

    def gather_start(j):
        own_loads[j].wait()
        own = rows_of(j, source(0, core) + dp, 1)
        for k in range(1, nx):
            give(j, own, k, x_dev(k, dp))
            give(j, own, nx + k, x_dev(k, 1 - dp))
        give(j, own, nx, dp_dev)

    def gather_pass(j):
        for k in range(nx):
            if k > 0:
                take(j, rows_of(j, source(k, core) + dp, 1), k)
            take(j, rows_of(j, source(k, core) + 1 - dp, 1), nx + k)
            give(j, rows_of(j, source(k, core), 2), 2 * nx + k - 1 if k else 0, sib)

    def gather_end(j):
        for k in range(nx):
            take(j, rows_of(j, source(k, 1 - core), 2), 2 * nx + k - 1 if k else 0)

    gather_start(0)
    gather_start(1)

    for c in block_loads:
        c.wait()
    for i in range(3):
        blocks[i, cap] = jnp.zeros((BLK, BLK), BF16)
    for ref in (dense_g, dense_u, dense_d):
        ref[0] = jnp.zeros(ref.shape[1:], F32)

    def place_wide(p, carry):
        r, c = p // (fcb // 2), p % (fcb // 2)
        keep = lane_half(BLK) == dp
        for i, w in enumerate((wg, wu)):
            even = blocks[i, inv_ref[i, 2 * p]].astype(F32)
            odd = blocks[i, inv_ref[i, 2 * p + 1]].astype(F32)
            stay = jnp.where(dp == 0, even, odd)
            move = swap(jnp.where(dp == 0, odd, even))
            w[pl.ds(al(r * BLK, BLK), BLK), pl.ds(al(c * BLK, BLK), BLK)] = jnp.where(
                keep, stay, move
            ).astype(BF16)
        return carry

    def place_down(p, carry):
        value = blocks[2, inv_ref[2, p]]
        r, c = p // drb, p % drb
        wd[pl.ds(al(r * HB, HB), HB), pl.ds(al(c * BLK, BLK), BLK)] = jnp.where(
            dp == 0, value[:HB], value[HB:]
        )
        return carry

    lax.fori_loop(0, drb * fcb // 2, place_wide, 0)
    lax.fori_loop(0, drb * fcb, place_down, 0)
    gather_pass(0)
    gather_end(0)

    def z_rows(t):
        return al(lax.rem(t + 2 * nz, nz) * zrows, zrows)

    def split(t, u):
        return u == 1 and t < 2

    def unit_rows(t, u, target):
        if not split(t, u):
            return z_rows(target)
        return al(z_rows(target) + yh * own_rows, own_rows)

    def count(t, u):
        return own_rows if split(t, u) else zrows

    def rs_ref(buf, t, u, d, k):
        cs = pl.ds(d * half, half) if k == 0 else pl.ds(0, cw)
        return buf.at[t, u, d, k, pl.ds(0, count(t, u)), cs]

    def rs_start(t, u, d, k):
        target = z + (steps - k) * (1 - 2 * d)
        rs = pl.ds(unit_rows(t, u, target), count(t, u))
        to = pl.ds(0, count(t, u))
        for h in range(2):
            if k == 0 and h != d:
                continue
            hc = pl.ds(h * half, half)
            value = part[t, rs, pl.ds(u * cw + h * half, half)]
            if k > 1 or (k == 1 and h == d):
                value = value + rs_recv[t, u, d, k - 1, to, hc].astype(F32)
            rs_send[t, u, d, k, to, hc] = value.astype(BF16)
        send(
            rs_ref(rs_send, t, u, d, k),
            rs_ref(rs_recv, t, u, d, k),
            rs_s.at[t, u, d, k],
            rs_r.at[t, u, d, k],
            z_dev[d],
        )

    def rs_wait(t, u, d, k):
        arrived(rs_ref(rs_recv, t, u, d, k), rs_s.at[t, u, d, k], rs_r.at[t, u, d, k], z_dev[d])

    def rs_step(t, u, k):
        for d in range(2):
            rs_wait(t, u, d, k - 1)
            rs_start(t, u, d, k)

    def yb_start(t):
        for c in range(nz):
            r0 = al(c * zrows + (1 - yh) * own_rows, own_rows)
            yb_send[t, c] = part[t, pl.ds(r0, own_rows), pl.ds(cw, cw)].astype(BF16)
        send(yb_send.at[t], yb_recv.at[t], yb_s.at[t], yb_r.at[t], y_dev)

    def yb_add(t):
        arrived(yb_recv.at[t], yb_s.at[t], yb_r.at[t], y_dev)
        for c in range(nz):
            rs = pl.ds(al(c * zrows + yh * own_rows, own_rows), own_rows)
            part[t, rs, pl.ds(cw, cw)] = part[t, rs, pl.ds(cw, cw)] + yb_recv[t, c].astype(F32)
        for d in range(2):
            rs_start(t, 1, d, 0)

    tile = min(256, cw)

    def product(t, u):
        def body(j, carry):
            cs = pl.ds(al(u * cw + j * tile, tile), tile)
            if t == 2:
                part[t, :, cs] = dot_t(tcg[1], wd[cs, :])
            else:
                part[t, :, cs] = dot(tcg[0], (wg, wu)[t][:, cs])
            return carry

        lax.fori_loop(0, cw // tile, body, 0)

    for t in range(2):
        product(t, 0)
        for d in range(2):
            rs_start(t, 0, d, 0)
        product(t, 1)
        yb_start(t)
        if t == 0:
            gather_pass(1)
    gather_end(1)
    product(2, 0)
    for d in range(2):
        rs_start(2, 0, d, 0)
    product(2, 1)

    mine_r = al(z * zrows + yh * own_rows, own_rows)
    theirs_r = al(z * zrows + (1 - yh) * own_rows, own_rows)
    mine_o, theirs_o = al(yh * own_rows, own_rows), al((1 - yh) * own_rows, own_rows)

    def last_sum(t, u, r0, o0):
        value = part[t, pl.ds(r0, own_rows), pl.ds(u * cw, cw)]
        for d in range(2):
            value = value + rs_recv[t, u, d, steps - 1, pl.ds(o0, own_rows), :].astype(F32)
        return value

    def rs_finish(t, u):
        for d in range(2):
            rs_wait(t, u, d, steps - 1)
        if split(t, u):
            y_own[u, t] = last_sum(t, u, mine_r, 0)
            return
        m = t + u
        y_send[m] = last_sum(t, u, theirs_r, theirs_o).astype(BF16)
        y_own[u, t] = last_sum(t, u, mine_r, mine_o)
        if t == 2:
            part_of = pl.ds(0, 3) if u == 0 else pl.ds(3, 1)
            send(y_send.at[part_of], y_recv.at[part_of], ys_s.at[u], ys_r.at[u], y_dev)

    def rows_ref(r0, u):
        return act.at[:, pl.ds(r0, own_rows), pl.ds(u * cw, cw)]

    def activate(u):
        part_of = pl.ds(0, 3) if u == 0 else pl.ds(3, 1)
        arrived(y_recv.at[part_of], ys_s.at[u], ys_r.at[u], y_dev)
        for q in range(2):
            cs = pl.ds(q * half, half)
            gate, up, grad = (y_own[u, t, :, cs] for t in range(3))
            if u == 0:
                gate = gate + y_recv[0, :, cs].astype(F32)
                up = up + y_recv[1, :, cs].astype(F32)
            grad = grad + y_recv[2 + u, :, cs].astype(F32)
            sg = 1.0 / (1.0 + jnp.exp(-gate))
            co = pl.ds(u * cw + q * half, half)
            act[0, pl.ds(mine_r, own_rows), co] = (
                grad * up * sg * (1.0 + gate * (1.0 - sg))
            ).astype(BF16)
            act[1, pl.ds(mine_r, own_rows), co] = (grad * gate * sg).astype(BF16)
            act[2, pl.ds(mine_r, own_rows), co] = (gate * sg * up).astype(BF16)
        ref = rows_ref(mine_r, u)
        if u == 0:
            send(ref, ref, ay_s.at[0, steps], ay_r.at[0, steps], y_dev)
        else:
            for t in range(3):
                send(ref.at[t], ref.at[t], ya_s.at[t], ya_r.at[t], y_dev)

    def az_chunk(d, k, hops, hi):
        rs = pl.ds(al(z_rows(z - hops * (1 - 2 * d)) + hi * own_rows, own_rows), own_rows)
        cs = pl.ds(d * half, half) if k == steps - 1 else pl.ds(0, cw)
        return act.at[:, rs, cs]

    def az_step(k):
        for d in range(2):
            if k > 0:
                ref = az_chunk(d, k - 1, k, yh)
                arrived(ref, az_s.at[d, k - 1], az_r.at[d, k - 1], z_dev[d])
            if k < steps:
                out = az_chunk(d, k, k, yh)
                send(out, out, az_s.at[d, k], az_r.at[d, k], z_dev[d])
            if k > 0:
                send(ref, ref, ay_s.at[d, k - 1], ay_r.at[d, k - 1], y_dev)

    def ay_wait():
        arrived(rows_ref(theirs_r, 0), ay_s.at[0, steps], ay_r.at[0, steps], y_dev)
        for k in range(1, steps + 1):
            for d in range(2):
                ref = az_chunk(d, k - 1, k, 1 - yh)
                arrived(ref, ay_s.at[d, k - 1], ay_r.at[d, k - 1], y_dev)

    def ag_slice(t, d, k, chunk):
        if k == steps - 1:
            c = pl.ds(cw + d * half, half)
        else:
            c = pl.ds(cw, cw)
        return act.at[t, pl.ds(z_rows(chunk), zrows), c]

    def ag_step(t, k):
        for d in range(2):
            sign = 1 - 2 * d
            if k > 0:
                ref = ag_slice(t, d, k - 1, z - k * sign)
                arrived(ref, ag_s.at[t, d, k - 1], ag_r.at[t, d, k - 1], z_dev[d])
            if k < steps:
                ref = ag_slice(t, d, k, z - k * sign)
                send(ref, ref, ag_s.at[t, d, k], ag_r.at[t, d, k], z_dev[d])

    out_copies = []

    def write_out(src, dst, index):
        copy = pltpu.make_async_copy(src, dst, out_sem.at[index])
        copy.start()
        out_copies.append(copy)

    def wide_dense(t, u):
        dense = (dense_g, dense_u)[t]
        per = cw // (2 * BLK)

        def body(j, carry):
            value = dot(tok_t[...], act[t, :, pl.ds(al(u * cw + j * 2 * BLK, BLK), 2 * BLK)])
            low = lane_half(BLK) == 0
            for a in range(drb):
                for b in range(2):
                    both = value[a * BLK : (a + 1) * BLK, b * BLK : (b + 1) * BLK]
                    turned = swap(both)
                    c = 4 * (u * per + j) + 2 * b
                    dense[a * fcb + c + 1] = jnp.where(low, both, turned)
                    dense[a * fcb + c + 2] = jnp.where(low, turned, both)
            return carry

        lax.fori_loop(0, per, body, 0)

    def emit_wide(i):
        dense = (dense_g, dense_u)[i]
        slot_list = (gate_slots, up_slots)[i]

        def body(s, carry):
            one = dense[slot_list[0, s] + 1]
            two = dense[slot_list[0, s + cap // 2] + 1]
            lanes = lane_half(HB)
            for h, value in enumerate((one, two)):
                keep = jnp.where(dp == 0, value[:HB], value[HB:])
                dp_own[i, h, s] = jnp.where(lanes == dp, keep, 0.0)
            give_one = jnp.where(dp == 0, one[HB:], one[:HB])
            give_two = jnp.where(dp == 0, two[HB:], two[:HB])
            dp_send[i, s] = jnp.where(lanes == 0, give_one, give_two).astype(BF16)
            return carry

        lax.fori_loop(0, cap // 2, body, 0)
        send(dp_send.at[i], recv_out.at[i], dp_s.at[i], dp_r.at[i], dp_dev)
        write_out(dp_own.at[i], own_out.at[i], i)

    def transpose_hidden(u):
        def body(j, carry):
            cs = pl.ds(al(u * cw + j * BLK, BLK), BLK)
            hid_t[cs, :] = act[2, :, cs].astype(F32).T.astype(BF16)
            return carry

        lax.fori_loop(0, cw // BLK, body, 0)

    def down_dense(u):
        per = cw // 256

        def body(j, carry):
            value = dot(hid_t[pl.ds(al(u * cw + j * 256, 256), 256), :], tcg[1])
            for a in range(4):
                for b in range(drb):
                    dense_d[(4 * (u * per + j) + a) * drb + b + 1] = value[
                        a * HB : (a + 1) * HB, b * BLK : (b + 1) * BLK
                    ]
            return carry

        lax.fori_loop(0, per, body, 0)

    def emit_down():
        def body(s, carry):
            down_own[s] = dense_d[down_slots[0, s] + 1]
            return carry

        lax.fori_loop(0, cap, body, 0)
        write_out(down_own, down_out, 2)

    def col_products(j, parts, first):
        step = min(256, width)

        def body(q, carry):
            cs = pl.ds(al(q * step, step), step)
            value = None if first else col_part[j, :, cs]
            for mul, a, b in parts:
                term = mul(a(), b(cs))
                value = term if value is None else value + term
            col_part[j, :, cs] = value
            return carry

        lax.fori_loop(0, width // step, body, 0)

    def layer_product(u):
        us = pl.ds(u * cw, cw)
        col_products(0, [(dot, lambda: act[2, :, us], lambda cs: wd[us, cs])], u == 0)

    def grad_product(u):
        us = pl.ds(u * cw, cw)
        parts = [
            (dot_t, lambda: act[0, :, us], lambda cs: wg[cs, us]),
            (dot_t, lambda: act[1, :, us], lambda cs: wu[cs, us]),
        ]
        col_products(1, parts, u == 0)

    def col_rows(c):
        return pl.ds(al(c * pair, pair), pair)

    def col_first(j):
        for xx in range(nx):
            ca_send[j, xx] = col_part[j, col_rows(xx * 2 + 1 - core), :].astype(BF16)
        send(ca_send.at[j], ca_recv.at[j], ca_s.at[j], ca_r.at[j], sib)

    def pair_sum(j, xx):
        return col_part[j, col_rows(xx * 2 + core), :] + ca_recv[j, xx].astype(F32)

    def col_second(j):
        arrived(ca_recv.at[j], ca_s.at[j], ca_r.at[j], sib)
        for k in range(1, nx):
            cb_send[j, k - 1] = pair_sum(j, lax.rem(x + k, nx)).astype(BF16)
            send(cb_send.at[j, k - 1], cb_recv.at[j, k - 1], cb_s.at[j, k - 1], cb_r.at[j, k - 1], x_dev(k, dp))

    def col_third(j):
        value = pair_sum(j, x)
        for k in range(1, nx):
            arrived(cb_recv.at[j, k - 1], cb_s.at[j, k - 1], cb_r.at[j, k - 1], sib)
            value = value + cb_recv[j, k - 1].astype(F32)
        cc_sum[j] = value
        cc_send[j] = cc_sum[j, pl.ds(al((1 - dp) * n_tok, n_tok), n_tok), :].astype(BF16)
        send(cc_send.at[j], cc_recv.at[j], cc_s.at[j], cc_r.at[j], dp_dev)

    def col_last(j, out):
        arrived(cc_recv.at[j], cc_s.at[j], cc_r.at[j], dp_dev)
        value = cc_sum[j, pl.ds(al(dp * n_tok, n_tok), n_tok), :] + cc_recv[j].astype(F32)
        col_stage[j] = value.astype(BF16)
        write_out(col_stage.at[j], out, 3 + j)

    S = steps
    slots = {}

    def at(s, f, *a):
        slots.setdefault(s, []).append(functools.partial(f, *a))

    def y_arrived(t):
        arrived(rows_ref(theirs_r, 1).at[t], ya_s.at[t], ya_r.at[t], y_dev)

    def tok_transpose():
        tok_t[...] = tcg[0].astype(F32).T.astype(BF16)

    def start_last():
        for d in range(2):
            rs_start(2, 1, d, 0)

    for k in range(1, S):
        for t in range(3):
            at(k, rs_step, t, 0, k)
    at(S - 2, start_last)
    at(S - 2, tok_transpose)
    at(S - 1, rs_step, 2, 1, 1)
    at(S - 1, yb_add, 0)
    at(S - 1, yb_add, 1)
    for t in range(3):
        at(S, rs_finish, t, 0)
    for k in range(1, S):
        at(S - 1 + k, rs_step, 0, 1, k)
        at(S - 1 + k, rs_step, 1, 1, k)
    for k in range(2, S):
        at(S - 2 + k, rs_step, 2, 1, k)
    at(S + 1, activate, 0)
    at(2 * S - 2, rs_finish, 2, 1)
    at(2 * S - 1, rs_finish, 0, 1)
    at(2 * S - 1, rs_finish, 1, 1)
    at(2 * S - 1, activate, 1)
    for t in range(3):
        lag = 2 * S + (t == 2)
        at(lag, y_arrived, t)
        for k in range(S + 1):
            at(lag + k, ag_step, t, k)
    for k in range(S + 1):
        at(S + 1 + k, az_step, k)
    A = 3 * S - 1
    at(A, ay_wait)
    at(A, wide_dense, 0, 0)
    at(A, wide_dense, 1, 0)
    at(A, grad_product, 0)
    A = 3 * S
    at(A, wide_dense, 0, 1)
    at(A, emit_wide, 0)
    at(A, wide_dense, 1, 1)
    at(A, emit_wide, 1)
    at(A, grad_product, 1)
    at(A, col_first, 1)
    at(A, layer_product, 0)
    at(A, col_second, 1)
    A = 3 * S + 1
    at(A, layer_product, 1)
    at(A, col_first, 0)
    at(A, transpose_hidden, 0)
    at(A, transpose_hidden, 1)
    at(A, col_second, 0)
    at(A, down_dense, 0)
    at(A, down_dense, 1)
    at(A, emit_down)
    at(A, col_third, 1)
    at(A, col_third, 0)
    at(A, col_last, 1, tgrad_out)
    at(A, col_last, 0, layer_out)
    for s in sorted(slots):
        for f in slots[s]:
            f()
    for i in range(2):
        arrived(recv_out.at[i], dp_s.at[i], dp_r.at[i], dp_dev)
    for c in out_copies:
        c.wait()
    for c in sends:
        c.wait_send()


def finish(layer, tgrad, own, recv, down, layer_o, tgrad_o, gate_o, up_o, down_o):
    dp = lax.axis_index("dp")
    layer_o[...] = layer[...]
    tgrad_o[...] = tgrad[...]
    down_o[...] = down[...]
    lanes = lane_half(HB)
    for i, out in enumerate((gate_o, up_o)):
        for s in range(recv.shape[1]):
            value = recv[i, s].astype(F32)
            turned = swap(value)
            for h in range(2):
                other = jnp.where(dp == 1 - h, value, turned)
                out[h, s] = jnp.where(lanes == dp, own[i, h, s], other)


def per_device(tokens, cotangent, gate_blocks, up_blocks, down_blocks, gate_slots, up_slots, down_slots):
    n_row, n_col = lax.axis_size("row"), lax.axis_size("col")
    n_tok, width = tokens.shape
    cap = gate_blocks.shape[2]
    hid = FF // n_col // 2
    nz, nx = n_row // 2, n_col // 2
    steps = nz // 2
    group = 2 * n_tok * n_col
    zrows = group // nz
    own_rows = zrows // 2
    cw = hid // UNITS
    drb, fcb = width // BLK, hid // HB
    pair = 2 * n_tok
    slots = jnp.concatenate([gate_slots[0], up_slots[0], down_slots[0]], axis=0)
    place = jnp.arange(drb * fcb, dtype=jnp.int32)
    order = jnp.arange(cap, dtype=jnp.int32)
    inv = jnp.min(
        jnp.where(slots[:, None, :] == place[None, :, None], order[None, None, :], cap), axis=2
    )
    dims = (n_row, n_col, n_tok, width, hid, cap)
    smem = pl.BlockSpec(memory_space=pltpu.SMEM)
    anym = pl.BlockSpec(memory_space=pl.ANY)
    vm = pltpu.VMEM
    dma = pltpu.SemaphoreType.DMA
    scratch = [
        vm((3, cap + 1, BLK, BLK), BF16),
        vm((2, group, width), BF16),
        vm((width, hid), BF16),
        vm((width, hid), BF16),
        vm((hid, width), BF16),
        vm((3, group, hid), F32),
        vm((3, UNITS, 2, steps, zrows, cw), BF16),
        vm((3, UNITS, 2, steps, zrows, cw), BF16),
        vm((4, own_rows, cw), BF16),
        vm((4, own_rows, cw), BF16),
        vm((UNITS, 3, own_rows, cw), F32),
        vm((2, nz, own_rows, cw), BF16),
        vm((2, nz, own_rows, cw), BF16),
        vm((3, group, hid), BF16),
        vm((width, group), BF16),
        vm((hid, group), BF16),
        vm((drb * fcb + 1, BLK, BLK), F32),
        vm((drb * fcb + 1, BLK, BLK), F32),
        vm((drb * fcb + 1, HB, BLK), F32),
        vm((2, cap // 2, HB, BLK), BF16),
        vm((2, 2, cap // 2, HB, BLK), F32),
        vm((cap, HB, BLK), F32),
        vm((2, group, width), F32),
        vm((2, nx, pair, width), BF16),
        vm((2, nx, pair, width), BF16),
        vm((2, nx - 1, pair, width), BF16),
        vm((2, nx - 1, pair, width), BF16),
        vm((2, pair, width), F32),
        vm((2, n_tok, width), BF16),
        vm((2, n_tok, width), BF16),
        vm((2, n_tok, width), BF16),
        dma((5,)),
        dma((5,)),
        dma((2, 3 * nx - 1)),
        dma((2, 3 * nx - 1)),
        dma((3, UNITS, 2, steps)),
        dma((3, UNITS, 2, steps)),
        dma((2,)),
        dma((2,)),
        dma((2,)),
        dma((2,)),
        dma((3,)),
        dma((3,)),
        dma((2, steps)),
        dma((2, steps)),
        dma((2, steps + 1)),
        dma((2, steps + 1)),
        dma((3, 2, steps)),
        dma((3, 2, steps)),
        dma((2,)),
        dma((2,)),
        dma((2,)),
        dma((2,)),
        dma((2, nx - 1)),
        dma((2, nx - 1)),
        dma((2,)),
        dma((2,)),
    ]
    flops = 9 * 2 * group * width * hid
    inner = (
        jax.ShapeDtypeStruct((n_tok, width), BF16),
        jax.ShapeDtypeStruct((n_tok, width), BF16),
        jax.ShapeDtypeStruct((2, 2, cap // 2, HB, BLK), F32),
        jax.ShapeDtypeStruct((2, cap // 2, HB, BLK), BF16),
        jax.ShapeDtypeStruct((cap, HB, BLK), F32),
    )
    results = pl.pallas_call(
        functools.partial(kernel, dims),
        out_shape=inner,
        in_specs=[smem, smem, smem, smem, anym, anym, anym, anym, anym],
        out_specs=(anym,) * 5,
        scratch_shapes=scratch,
        compiler_params=pltpu.CompilerParams(
            collective_id=0, has_side_effects=True, vmem_limit_bytes=56 * 1024 * 1024
        ),
        cost_estimate=pl.CostEstimate(flops=flops, bytes_accessed=8 * 1024 * 1024, transcendentals=0),
        name="ffn",
    )(gate_slots[0], up_slots[0], down_slots[0], inv, tokens, cotangent, gate_blocks[0, 0], up_blocks[0, 0], down_blocks[0, 0])
    ns = cap // 2 // GRID
    flat = pl.BlockSpec((n_tok, width), lambda g: (0, 0))
    wide = pl.BlockSpec((2, ns, HB, BLK), lambda g: (0, g, 0, 0))
    tall = pl.BlockSpec((2 * ns, HB, BLK), lambda g: (g, 0, 0))
    layer, tgrad, gate_grad, up_grad, down_grad = pl.pallas_call(
        finish,
        grid=(GRID,),
        out_shape=(
            inner[0],
            inner[1],
            jax.ShapeDtypeStruct((2, cap // 2, HB, BLK), F32),
            jax.ShapeDtypeStruct((2, cap // 2, HB, BLK), F32),
            inner[4],
        ),
        in_specs=[
            flat,
            flat,
            pl.BlockSpec((2, 2, ns, HB, BLK), lambda g: (0, 0, g, 0, 0)),
            wide,
            tall,
        ],
        out_specs=(flat, flat, wide, wide, tall),
        name="finish",
    )(*results)
    shape = (1, 1, cap, HB, BLK)
    return (layer, tgrad, gate_grad.reshape(shape), up_grad.reshape(shape), down_grad.reshape(shape))


def solution(mesh):
    in_specs = (
        P(("col", "dp"), "row"),
        P(("col", "dp"), "row"),
        P("row", "col", None, None, None),
        P("row", "col", None, None, None),
        P("col", "row", None, None, None),
        P("row", "col", None),
        P("row", "col", None),
        P("col", "row", None),
    )
    out_specs = (
        P(("col", "dp"), "row"),
        P(("col", "dp"), "row"),
        P("row", "col", None, "dp", None),
        P("row", "col", None, "dp", None),
        P("col", "row", None, "dp", None),
    )
    return jax.shard_map(
        per_device, mesh=mesh, in_specs=in_specs, out_specs=out_specs, check_vma=False
    )
```

```python
import functools

import jax
import jax.numpy as jnp
from jax import lax
from jax.experimental import pallas as pl
from jax.experimental.pallas import tpu as pltpu
from jax.sharding import PartitionSpec as P

FF = 16384
BLK = 128
HB = BLK // 2
UNITS = 2
GRID = 2
MESH = pl.DeviceIdType.MESH
F32 = jnp.float32
BF16 = jnp.bfloat16


def dot(a, b):
    return lax.dot_general(a, b, (((1,), (0,)), ((), ())), preferred_element_type=F32)


def dot_t(a, b):
    return lax.dot_general(a, b, (((1,), (1,)), ((), ())), preferred_element_type=F32)


def al(value, step):
    return pl.multiple_of(value, step)


def swap(value):
    return pltpu.roll(value, HB, 1)


def lane_half(rows):
    return (lax.broadcasted_iota(jnp.int32, (rows, BLK), 1) >= HB).astype(jnp.int32)


def kernel(
    dims,
    gate_slots,
    up_slots,
    down_slots,
    inv_ref,
    tok_in,
    cot_in,
    gate_in,
    up_in,
    down_in,
    layer_out,
    tgrad_out,
    own_out,
    recv_out,
    down_out,
    blocks,
    tcg,
    wg,
    wu,
    wd,
    part,
    rs_send,
    rs_recv,
    y_send,
    y_recv,
    y_own,
    yb_send,
    yb_recv,
    act,
    tok_t,
    hid_t,
    dense_g,
    dense_u,
    dense_d,
    dp_send,
    dp_own,
    down_own,
    col_part,
    ca_send,
    ca_recv,
    cb_send,
    cb_recv,
    cc_sum,
    cc_send,
    cc_recv,
    col_stage,
    loc_sem,
    out_sem,
    p1_s,
    p1_r,
    rs_s,
    rs_r,
    ys_s,
    ys_r,
    yb_s,
    yb_r,
    ya_s,
    ya_r,
    az_s,
    az_r,
    ay_s,
    ay_r,
    ag_s,
    ag_r,
    dp_s,
    dp_r,
    ca_s,
    ca_r,
    cb_s,
    cb_r,
    cc_s,
    cc_r,
):
    n_row, n_col, n_tok, width, hid, cap = dims
    nz, nx = n_row // 2, n_col // 2
    steps = nz // 2
    group = 2 * n_tok * n_col
    zrows = group // nz
    own_rows = zrows // 2
    cw = hid // UNITS
    half = cw // 2
    drb, fcb = width // BLK, hid // HB
    pair = 2 * n_tok

    row, col, dp = lax.axis_index("row"), lax.axis_index("col"), lax.axis_index("dp")
    z, yh = lax.div(row, 2), lax.rem(row, 2)
    x, core = lax.div(col, 2), lax.rem(col, 2)
    z_right = (lax.rem(z + 1, nz) * 2 + yh, col, dp)
    z_left = (lax.rem(z + nz - 1, nz) * 2 + yh, col, dp)
    z_dev = (z_right, z_left)
    y_dev = (z * 2 + 1 - yh, col, dp)
    sib = (row, x * 2 + 1 - core, dp)
    dp_dev = (row, col, 1 - dp)

    def x_dev(k, d):
        return (row, lax.rem(x + k, nx) * 2 + core, d)

    sends = []

    def send(src, dst, s_sem, r_sem, dev):
        copy = pltpu.make_async_remote_copy(
            src_ref=src, dst_ref=dst, send_sem=s_sem, recv_sem=r_sem, device_id=dev, device_id_type=MESH
        )
        copy.start()
        sends.append(copy)

    def arrived(dst, s_sem, r_sem, dev):
        pltpu.make_async_remote_copy(
            src_ref=dst, dst_ref=dst, send_sem=s_sem, recv_sem=r_sem, device_id=dev, device_id_type=MESH
        ).wait_recv()

    mine = pl.ds(al((col * 2 + dp) * n_tok, n_tok), n_tok)
    own_loads = [
        pltpu.make_async_copy(ref, tcg.at[j, mine, :], loc_sem.at[j])
        for j, ref in enumerate((tok_in, cot_in))
    ]
    block_loads = [
        pltpu.make_async_copy(ref, blocks.at[i, pl.ds(0, cap)], loc_sem.at[2 + i])
        for i, ref in enumerate((gate_in, up_in, down_in))
    ]
    for c in own_loads + block_loads:
        c.start()

    barrier = pltpu.get_barrier_semaphore()
    peers = [z_right, z_left, y_dev, sib, dp_dev] + [
        x_dev(k, d) for k in range(1, nx) for d in (dp, 1 - dp)
    ]
    for dev in peers:
        pl.semaphore_signal(barrier, inc=1, device_id=dev, device_id_type=MESH)
    pl.semaphore_wait(barrier, len(peers))

    def rows_of(j, index, n):
        return tcg.at[j, pl.ds(al(index * n_tok, n_tok), n * n_tok), :]

    def source(k, c):
        return (lax.rem(x + nx - k, nx) * 2 + c) * 2

    def give(j, ref, s, dev):
        send(ref, ref, p1_s.at[j, s], p1_r.at[j, s], dev)

    def take(j, ref, s):
        arrived(ref, p1_s.at[j, s], p1_r.at[j, s], sib)

    def gather_start(j):
        own_loads[j].wait()
        own = rows_of(j, source(0, core) + dp, 1)
        for k in range(1, nx):
            give(j, own, k, x_dev(k, dp))
            give(j, own, nx + k, x_dev(k, 1 - dp))
        give(j, own, nx, dp_dev)

    def gather_pass(j):
        for k in range(nx):
            if k > 0:
                take(j, rows_of(j, source(k, core) + dp, 1), k)
            take(j, rows_of(j, source(k, core) + 1 - dp, 1), nx + k)
            give(j, rows_of(j, source(k, core), 2), 2 * nx + k - 1 if k else 0, sib)

    def gather_end(j):
        for k in range(nx):
            take(j, rows_of(j, source(k, 1 - core), 2), 2 * nx + k - 1 if k else 0)

    gather_start(0)
    gather_start(1)

    for c in block_loads:
        c.wait()
    for i in range(3):
        blocks[i, cap] = jnp.zeros((BLK, BLK), BF16)
    for ref in (dense_g, dense_u, dense_d):
        ref[0] = jnp.zeros(ref.shape[1:], F32)

    def place_wide(p, carry):
        r, c = p // (fcb // 2), p % (fcb // 2)
        keep = lane_half(BLK) == dp
        for i, w in enumerate((wg, wu)):
            even = blocks[i, inv_ref[i, 2 * p]].astype(F32)
            odd = blocks[i, inv_ref[i, 2 * p + 1]].astype(F32)
            stay = jnp.where(dp == 0, even, odd)
            move = swap(jnp.where(dp == 0, odd, even))
            w[pl.ds(al(r * BLK, BLK), BLK), pl.ds(al(c * BLK, BLK), BLK)] = jnp.where(
                keep, stay, move
            ).astype(BF16)
        return carry

    def place_down(p, carry):
        value = blocks[2, inv_ref[2, p]]
        r, c = p // drb, p % drb
        wd[pl.ds(al(r * HB, HB), HB), pl.ds(al(c * BLK, BLK), BLK)] = jnp.where(
            dp == 0, value[:HB], value[HB:]
        )
        return carry

    lax.fori_loop(0, drb * fcb // 2, place_wide, 0)
    lax.fori_loop(0, drb * fcb, place_down, 0)
    gather_pass(0)
    gather_end(0)

    def z_rows(t):
        return al(lax.rem(t + 2 * nz, nz) * zrows, zrows)

    def split(t, u):
        return u == 1 and t < 2

    def unit_rows(t, u, target):
        if not split(t, u):
            return z_rows(target)
        return al(z_rows(target) + yh * own_rows, own_rows)

    def count(t, u):
        return own_rows if split(t, u) else zrows

    def rs_ref(buf, t, u, d, k):
        cs = pl.ds(d * half, half) if k == 0 else pl.ds(0, cw)
        return buf.at[t, u, d, k, pl.ds(0, count(t, u)), cs]

    def rs_start(t, u, d, k):
        target = z + (steps - k) * (1 - 2 * d)
        rs = pl.ds(unit_rows(t, u, target), count(t, u))
        to = pl.ds(0, count(t, u))
        for h in range(2):
            if k == 0 and h != d:
                continue
            hc = pl.ds(h * half, half)
            value = part[t, rs, pl.ds(u * cw + h * half, half)]
            if k > 1 or (k == 1 and h == d):
                value = value + rs_recv[t, u, d, k - 1, to, hc].astype(F32)
            rs_send[t, u, d, k, to, hc] = value.astype(BF16)
        send(
            rs_ref(rs_send, t, u, d, k),
            rs_ref(rs_recv, t, u, d, k),
            rs_s.at[t, u, d, k],
            rs_r.at[t, u, d, k],
            z_dev[d],
        )

    def rs_wait(t, u, d, k):
        arrived(rs_ref(rs_recv, t, u, d, k), rs_s.at[t, u, d, k], rs_r.at[t, u, d, k], z_dev[d])

    def rs_step(t, u, k):
        for d in range(2):
            rs_wait(t, u, d, k - 1)
            rs_start(t, u, d, k)

    def yb_start(t):
        for c in range(nz):
            r0 = al(c * zrows + (1 - yh) * own_rows, own_rows)
            yb_send[t, c] = part[t, pl.ds(r0, own_rows), pl.ds(cw, cw)].astype(BF16)
        send(yb_send.at[t], yb_recv.at[t], yb_s.at[t], yb_r.at[t], y_dev)

    def yb_add(t):
        arrived(yb_recv.at[t], yb_s.at[t], yb_r.at[t], y_dev)
        for c in range(nz):
            rs = pl.ds(al(c * zrows + yh * own_rows, own_rows), own_rows)
            part[t, rs, pl.ds(cw, cw)] = part[t, rs, pl.ds(cw, cw)] + yb_recv[t, c].astype(F32)
        for d in range(2):
            rs_start(t, 1, d, 0)

    tile = min(256, cw)

    def product(t, u):
        def body(j, carry):
            cs = pl.ds(al(u * cw + j * tile, tile), tile)
            if t == 2:
                part[t, :, cs] = dot_t(tcg[1], wd[cs, :])
            else:
                part[t, :, cs] = dot(tcg[0], (wg, wu)[t][:, cs])
            return carry

        lax.fori_loop(0, cw // tile, body, 0)

    for t in range(2):
        product(t, 0)
        for d in range(2):
            rs_start(t, 0, d, 0)
        product(t, 1)
        yb_start(t)
    gather_pass(1)
    gather_end(1)
    product(2, 0)
    for d in range(2):
        rs_start(2, 0, d, 0)
    product(2, 1)

    mine_r = al(z * zrows + yh * own_rows, own_rows)
    theirs_r = al(z * zrows + (1 - yh) * own_rows, own_rows)
    mine_o, theirs_o = al(yh * own_rows, own_rows), al((1 - yh) * own_rows, own_rows)

    def last_sum(t, u, r0, o0):
        value = part[t, pl.ds(r0, own_rows), pl.ds(u * cw, cw)]
        for d in range(2):
            value = value + rs_recv[t, u, d, steps - 1, pl.ds(o0, own_rows), :].astype(F32)
        return value

    def rs_finish(t, u):
        for d in range(2):
            rs_wait(t, u, d, steps - 1)
        if split(t, u):
            y_own[u, t] = last_sum(t, u, mine_r, 0)
            return
        m = t + u
        y_send[m] = last_sum(t, u, theirs_r, theirs_o).astype(BF16)
        y_own[u, t] = last_sum(t, u, mine_r, mine_o)
        if t == 2:
            part_of = pl.ds(0, 3) if u == 0 else pl.ds(3, 1)
            send(y_send.at[part_of], y_recv.at[part_of], ys_s.at[u], ys_r.at[u], y_dev)

    def rows_ref(r0, u):
        return act.at[:, pl.ds(r0, own_rows), pl.ds(u * cw, cw)]

    def activate(u):
        part_of = pl.ds(0, 3) if u == 0 else pl.ds(3, 1)
        arrived(y_recv.at[part_of], ys_s.at[u], ys_r.at[u], y_dev)
        for q in range(2):
            cs = pl.ds(q * half, half)
            gate, up, grad = (y_own[u, t, :, cs] for t in range(3))
            if u == 0:
                gate = gate + y_recv[0, :, cs].astype(F32)
                up = up + y_recv[1, :, cs].astype(F32)
            grad = grad + y_recv[2 + u, :, cs].astype(F32)
            sg = 1.0 / (1.0 + jnp.exp(-gate))
            co = pl.ds(u * cw + q * half, half)
            act[0, pl.ds(mine_r, own_rows), co] = (
                grad * up * sg * (1.0 + gate * (1.0 - sg))
            ).astype(BF16)
            act[1, pl.ds(mine_r, own_rows), co] = (grad * gate * sg).astype(BF16)
            act[2, pl.ds(mine_r, own_rows), co] = (gate * sg * up).astype(BF16)
        ref = rows_ref(mine_r, u)
        if u == 0:
            send(ref, ref, ay_s.at[0, steps], ay_r.at[0, steps], y_dev)
        else:
            for t in range(3):
                send(ref.at[t], ref.at[t], ya_s.at[t], ya_r.at[t], y_dev)

    def az_chunk(d, k, hops, hi):
        rs = pl.ds(al(z_rows(z - hops * (1 - 2 * d)) + hi * own_rows, own_rows), own_rows)
        cs = pl.ds(d * half, half) if k == steps - 1 else pl.ds(0, cw)
        return act.at[:, rs, cs]

    def az_step(k):
        for d in range(2):
            if k > 0:
                ref = az_chunk(d, k - 1, k, yh)
                arrived(ref, az_s.at[d, k - 1], az_r.at[d, k - 1], z_dev[d])
            if k < steps:
                out = az_chunk(d, k, k, yh)
                send(out, out, az_s.at[d, k], az_r.at[d, k], z_dev[d])
            if k > 0:
                send(ref, ref, ay_s.at[d, k - 1], ay_r.at[d, k - 1], y_dev)

    def ay_wait():
        arrived(rows_ref(theirs_r, 0), ay_s.at[0, steps], ay_r.at[0, steps], y_dev)
        for k in range(1, steps + 1):
            for d in range(2):
                ref = az_chunk(d, k - 1, k, 1 - yh)
                arrived(ref, ay_s.at[d, k - 1], ay_r.at[d, k - 1], y_dev)

    def ag_slice(t, d, k, chunk):
        if k == steps - 1:
            c = pl.ds(cw + d * half, half)
        else:
            c = pl.ds(cw, cw)
        return act.at[t, pl.ds(z_rows(chunk), zrows), c]

    def ag_step(t, k):
        for d in range(2):
            sign = 1 - 2 * d
            if k > 0:
                ref = ag_slice(t, d, k - 1, z - k * sign)
                arrived(ref, ag_s.at[t, d, k - 1], ag_r.at[t, d, k - 1], z_dev[d])
            if k < steps:
                ref = ag_slice(t, d, k, z - k * sign)
                send(ref, ref, ag_s.at[t, d, k], ag_r.at[t, d, k], z_dev[d])

    out_copies = []

    def write_out(src, dst, index):
        copy = pltpu.make_async_copy(src, dst, out_sem.at[index])
        copy.start()
        out_copies.append(copy)

    def wide_dense(t, u):
        dense = (dense_g, dense_u)[t]
        per = cw // (2 * BLK)

        def body(j, carry):
            value = dot(tok_t[...], act[t, :, pl.ds(al(u * cw + j * 2 * BLK, BLK), 2 * BLK)])
            low = lane_half(BLK) == 0
            for a in range(drb):
                for b in range(2):
                    both = value[a * BLK : (a + 1) * BLK, b * BLK : (b + 1) * BLK]
                    turned = swap(both)
                    c = 4 * (u * per + j) + 2 * b
                    dense[a * fcb + c + 1] = jnp.where(low, both, turned)
                    dense[a * fcb + c + 2] = jnp.where(low, turned, both)
            return carry

        lax.fori_loop(0, per, body, 0)

    def emit_wide(i):
        dense = (dense_g, dense_u)[i]
        slot_list = (gate_slots, up_slots)[i]

        def body(s, carry):
            one = dense[slot_list[0, s] + 1]
            two = dense[slot_list[0, s + cap // 2] + 1]
            lanes = lane_half(HB)
            for h, value in enumerate((one, two)):
                keep = jnp.where(dp == 0, value[:HB], value[HB:])
                dp_own[i, h, s] = jnp.where(lanes == dp, keep, 0.0)
            give_one = jnp.where(dp == 0, one[HB:], one[:HB])
            give_two = jnp.where(dp == 0, two[HB:], two[:HB])
            dp_send[i, s] = jnp.where(lanes == 0, give_one, give_two).astype(BF16)
            return carry

        lax.fori_loop(0, cap // 2, body, 0)
        send(dp_send.at[i], recv_out.at[i], dp_s.at[i], dp_r.at[i], dp_dev)
        write_out(dp_own.at[i], own_out.at[i], i)

    def transpose_hidden(u):
        def body(j, carry):
            cs = pl.ds(al(u * cw + j * BLK, BLK), BLK)
            hid_t[cs, :] = act[2, :, cs].astype(F32).T.astype(BF16)
            return carry

        lax.fori_loop(0, cw // BLK, body, 0)

    def down_dense(u):
        per = cw // 256

        def body(j, carry):
            value = dot(hid_t[pl.ds(al(u * cw + j * 256, 256), 256), :], tcg[1])
            for a in range(4):
                for b in range(drb):
                    dense_d[(4 * (u * per + j) + a) * drb + b + 1] = value[
                        a * HB : (a + 1) * HB, b * BLK : (b + 1) * BLK
                    ]
            return carry

        lax.fori_loop(0, per, body, 0)

    def emit_down():
        def body(s, carry):
            down_own[s] = dense_d[down_slots[0, s] + 1]
            return carry

        lax.fori_loop(0, cap, body, 0)
        write_out(down_own, down_out, 2)

    def col_products(j, parts, first):
        step = min(256, width)

        def body(q, carry):
            cs = pl.ds(al(q * step, step), step)
            value = None if first else col_part[j, :, cs]
            for mul, a, b in parts:
                term = mul(a(), b(cs))
                value = term if value is None else value + term
            col_part[j, :, cs] = value
            return carry

        lax.fori_loop(0, width // step, body, 0)

    def layer_product(u):
        us = pl.ds(u * cw, cw)
        col_products(0, [(dot, lambda: act[2, :, us], lambda cs: wd[us, cs])], u == 0)

    def grad_product(u):
        us = pl.ds(u * cw, cw)
        parts = [
            (dot_t, lambda: act[0, :, us], lambda cs: wg[cs, us]),
            (dot_t, lambda: act[1, :, us], lambda cs: wu[cs, us]),
        ]
        col_products(1, parts, u == 0)

    def col_rows(c):
        return pl.ds(al(c * pair, pair), pair)

    def col_first(j):
        for xx in range(nx):
            ca_send[j, xx] = col_part[j, col_rows(xx * 2 + 1 - core), :].astype(BF16)
        send(ca_send.at[j], ca_recv.at[j], ca_s.at[j], ca_r.at[j], sib)

    def pair_sum(j, xx):
        return col_part[j, col_rows(xx * 2 + core), :] + ca_recv[j, xx].astype(F32)

    def col_second(j):
        arrived(ca_recv.at[j], ca_s.at[j], ca_r.at[j], sib)
        for k in range(1, nx):
            cb_send[j, k - 1] = pair_sum(j, lax.rem(x + k, nx)).astype(BF16)
            send(cb_send.at[j, k - 1], cb_recv.at[j, k - 1], cb_s.at[j, k - 1], cb_r.at[j, k - 1], x_dev(k, dp))

    def col_third(j):
        value = pair_sum(j, x)
        for k in range(1, nx):
            arrived(cb_recv.at[j, k - 1], cb_s.at[j, k - 1], cb_r.at[j, k - 1], sib)
            value = value + cb_recv[j, k - 1].astype(F32)
        cc_sum[j] = value
        cc_send[j] = cc_sum[j, pl.ds(al((1 - dp) * n_tok, n_tok), n_tok), :].astype(BF16)
        send(cc_send.at[j], cc_recv.at[j], cc_s.at[j], cc_r.at[j], dp_dev)

    def col_last(j, out):
        arrived(cc_recv.at[j], cc_s.at[j], cc_r.at[j], dp_dev)
        value = cc_sum[j, pl.ds(al(dp * n_tok, n_tok), n_tok), :] + cc_recv[j].astype(F32)
        col_stage[j] = value.astype(BF16)
        write_out(col_stage.at[j], out, 3 + j)

    S = steps
    slots = {}

    def at(s, f, *a):
        slots.setdefault(s, []).append(functools.partial(f, *a))

    def y_arrived(t):
        arrived(rows_ref(theirs_r, 1).at[t], ya_s.at[t], ya_r.at[t], y_dev)

    def tok_transpose():
        tok_t[...] = tcg[0].astype(F32).T.astype(BF16)

    def start_last():
        for d in range(2):
            rs_start(2, 1, d, 0)

    for k in range(1, S):
        for t in range(3):
            at(k, rs_step, t, 0, k)
    at(S - 2, start_last)
    at(S - 2, tok_transpose)
    at(S - 1, rs_step, 2, 1, 1)
    at(S - 1, yb_add, 0)
    at(S - 1, yb_add, 1)
    for t in range(3):
        at(S, rs_finish, t, 0)
    for k in range(1, S):
        at(S - 1 + k, rs_step, 0, 1, k)
        at(S - 1 + k, rs_step, 1, 1, k)
    for k in range(2, S):
        at(S - 2 + k, rs_step, 2, 1, k)
    at(S + 1, activate, 0)
    at(2 * S - 2, rs_finish, 2, 1)
    at(2 * S - 1, rs_finish, 0, 1)
    at(2 * S - 1, rs_finish, 1, 1)
    at(2 * S - 1, activate, 1)
    for t in range(3):
        lag = 2 * S + (t == 2)
        at(lag, y_arrived, t)
        for k in range(S + 1):
            at(lag + k, ag_step, t, k)
    for k in range(S + 1):
        at(S + 1 + k, az_step, k)
    A = 3 * S - 1
    at(A, ay_wait)
    at(A, wide_dense, 0, 0)
    at(A, wide_dense, 1, 0)
    at(A, grad_product, 0)
    A = 3 * S
    at(A, wide_dense, 0, 1)
    at(A, emit_wide, 0)
    at(A, wide_dense, 1, 1)
    at(A, emit_wide, 1)
    at(A, grad_product, 1)
    at(A, col_first, 1)
    at(A, layer_product, 0)
    at(A, col_second, 1)
    A = 3 * S + 1
    at(A, layer_product, 1)
    at(A, col_first, 0)
    at(A, transpose_hidden, 0)
    at(A, transpose_hidden, 1)
    at(A, col_second, 0)
    at(A, down_dense, 0)
    at(A, down_dense, 1)
    at(A, emit_down)
    at(A, col_third, 1)
    at(A, col_third, 0)
    at(A, col_last, 1, tgrad_out)
    at(A, col_last, 0, layer_out)
    for s in sorted(slots):
        for f in slots[s]:
            f()
    for i in range(2):
        arrived(recv_out.at[i], dp_s.at[i], dp_r.at[i], dp_dev)
    for c in out_copies:
        c.wait()
    for c in sends:
        c.wait_send()


def finish(layer, tgrad, own, recv, down, layer_o, tgrad_o, gate_o, up_o, down_o):
    dp = lax.axis_index("dp")
    layer_o[...] = layer[...]
    tgrad_o[...] = tgrad[...]
    down_o[...] = down[...]
    lanes = lane_half(HB)
    for i, out in enumerate((gate_o, up_o)):
        for s in range(recv.shape[1]):
            value = recv[i, s].astype(F32)
            turned = swap(value)
            for h in range(2):
                other = jnp.where(dp == 1 - h, value, turned)
                out[h, s] = jnp.where(lanes == dp, own[i, h, s], other)


def per_device(tokens, cotangent, gate_blocks, up_blocks, down_blocks, gate_slots, up_slots, down_slots):
    n_row, n_col = lax.axis_size("row"), lax.axis_size("col")
    n_tok, width = tokens.shape
    cap = gate_blocks.shape[2]
    hid = FF // n_col // 2
    nz, nx = n_row // 2, n_col // 2
    steps = nz // 2
    group = 2 * n_tok * n_col
    zrows = group // nz
    own_rows = zrows // 2
    cw = hid // UNITS
    drb, fcb = width // BLK, hid // HB
    pair = 2 * n_tok
    slots = jnp.concatenate([gate_slots[0], up_slots[0], down_slots[0]], axis=0)
    place = jnp.arange(drb * fcb, dtype=jnp.int32)
    order = jnp.arange(cap, dtype=jnp.int32)
    inv = jnp.min(
        jnp.where(slots[:, None, :] == place[None, :, None], order[None, None, :], cap), axis=2
    )
    dims = (n_row, n_col, n_tok, width, hid, cap)
    smem = pl.BlockSpec(memory_space=pltpu.SMEM)
    anym = pl.BlockSpec(memory_space=pl.ANY)
    vm = pltpu.VMEM
    dma = pltpu.SemaphoreType.DMA
    scratch = [
        vm((3, cap + 1, BLK, BLK), BF16),
        vm((2, group, width), BF16),
        vm((width, hid), BF16),
        vm((width, hid), BF16),
        vm((hid, width), BF16),
        vm((3, group, hid), F32),
        vm((3, UNITS, 2, steps, zrows, cw), BF16),
        vm((3, UNITS, 2, steps, zrows, cw), BF16),
        vm((4, own_rows, cw), BF16),
        vm((4, own_rows, cw), BF16),
        vm((UNITS, 3, own_rows, cw), F32),
        vm((2, nz, own_rows, cw), BF16),
        vm((2, nz, own_rows, cw), BF16),
        vm((3, group, hid), BF16),
        vm((width, group), BF16),
        vm((hid, group), BF16),
        vm((drb * fcb + 1, BLK, BLK), F32),
        vm((drb * fcb + 1, BLK, BLK), F32),
        vm((drb * fcb + 1, HB, BLK), F32),
        vm((2, cap // 2, HB, BLK), BF16),
        vm((2, 2, cap // 2, HB, BLK), F32),
        vm((cap, HB, BLK), F32),
        vm((2, group, width), F32),
        vm((2, nx, pair, width), BF16),
        vm((2, nx, pair, width), BF16),
        vm((2, nx - 1, pair, width), BF16),
        vm((2, nx - 1, pair, width), BF16),
        vm((2, pair, width), F32),
        vm((2, n_tok, width), BF16),
        vm((2, n_tok, width), BF16),
        vm((2, n_tok, width), BF16),
        dma((5,)),
        dma((5,)),
        dma((2, 3 * nx - 1)),
        dma((2, 3 * nx - 1)),
        dma((3, UNITS, 2, steps)),
        dma((3, UNITS, 2, steps)),
        dma((2,)),
        dma((2,)),
        dma((2,)),
        dma((2,)),
        dma((3,)),
        dma((3,)),
        dma((2, steps)),
        dma((2, steps)),
        dma((2, steps + 1)),
        dma((2, steps + 1)),
        dma((3, 2, steps)),
        dma((3, 2, steps)),
        dma((2,)),
        dma((2,)),
        dma((2,)),
        dma((2,)),
        dma((2, nx - 1)),
        dma((2, nx - 1)),
        dma((2,)),
        dma((2,)),
    ]
    flops = 9 * 2 * group * width * hid
    inner = (
        jax.ShapeDtypeStruct((n_tok, width), BF16),
        jax.ShapeDtypeStruct((n_tok, width), BF16),
        jax.ShapeDtypeStruct((2, 2, cap // 2, HB, BLK), F32),
        jax.ShapeDtypeStruct((2, cap // 2, HB, BLK), BF16),
        jax.ShapeDtypeStruct((cap, HB, BLK), F32),
    )
    results = pl.pallas_call(
        functools.partial(kernel, dims),
        out_shape=inner,
        in_specs=[smem, smem, smem, smem, anym, anym, anym, anym, anym],
        out_specs=(anym,) * 5,
        scratch_shapes=scratch,
        compiler_params=pltpu.CompilerParams(
            collective_id=0, has_side_effects=True, vmem_limit_bytes=56 * 1024 * 1024
        ),
        cost_estimate=pl.CostEstimate(flops=flops, bytes_accessed=8 * 1024 * 1024, transcendentals=0),
        name="ffn",
    )(gate_slots[0], up_slots[0], down_slots[0], inv, tokens, cotangent, gate_blocks[0, 0], up_blocks[0, 0], down_blocks[0, 0])
    ns = cap // 2 // GRID
    flat = pl.BlockSpec((n_tok, width), lambda g: (0, 0))
    wide = pl.BlockSpec((2, ns, HB, BLK), lambda g: (0, g, 0, 0))
    tall = pl.BlockSpec((2 * ns, HB, BLK), lambda g: (g, 0, 0))
    layer, tgrad, gate_grad, up_grad, down_grad = pl.pallas_call(
        finish,
        grid=(GRID,),
        out_shape=(
            inner[0],
            inner[1],
            jax.ShapeDtypeStruct((2, cap // 2, HB, BLK), F32),
            jax.ShapeDtypeStruct((2, cap // 2, HB, BLK), F32),
            inner[4],
        ),
        in_specs=[
            flat,
            flat,
            pl.BlockSpec((2, 2, ns, HB, BLK), lambda g: (0, 0, g, 0, 0)),
            wide,
            tall,
        ],
        out_specs=(flat, flat, wide, wide, tall),
        name="finish",
    )(*results)
    shape = (1, 1, cap, HB, BLK)
    return (layer, tgrad, gate_grad.reshape(shape), up_grad.reshape(shape), down_grad.reshape(shape))


def solution(mesh):
    in_specs = (
        P(("col", "dp"), "row"),
        P(("col", "dp"), "row"),
        P("row", "col", None, None, None),
        P("row", "col", None, None, None),
        P("col", "row", None, None, None),
        P("row", "col", None),
        P("row", "col", None),
        P("col", "row", None),
    )
    out_specs = (
        P(("col", "dp"), "row"),
        P(("col", "dp"), "row"),
        P("row", "col", None, "dp", None),
        P("row", "col", None, "dp", None),
        P("col", "row", None, "dp", None),
    )
    return jax.shard_map(
        per_device, mesh=mesh, in_specs=in_specs, out_specs=out_specs, check_vma=False
    )
```
